512 devices in a mesh: grp: 2 (over x_hi), seq: 32 (over x_lo, z), head: 8 (over y, core).
Axes of the slice: x: 4 (x_hi: 2, x_lo: 2; x = x_hi * 2 + x_lo), y: 4, z: 16, core: 2. Of those that a mesh axis runs over, the one named last changes fastest.
Arguments:
- features: bfloat16 [2, 32, 16, 32, 512], P('grp', 'seq', 'head'), may hold values from -6 to 6
- conv_weight: bfloat16 [3, 3, 3, 512, 16], replicated, may hold values from -0.0546875 to 0.0546875
- conv_bias: float32 [16], replicated, may hold values from -3 to 3
- token_order: int32 [4096], P('seq'), may hold values from 0 to 4095, each once
- embed_weight: bfloat16 [64, 3072], replicated, may hold values from -0.75 to 0.75
- norm_gain: float32 [3072], replicated, may hold values from 0.1 to 1.9
- qkv_weight: bfloat16 [3072, 3, 2048], P('seq', None, 'head'), may hold values from -0.109375 to 0.109375
- grad_out: bfloat16 [2, 4096, 2048], P('grp', 'seq', 'head'), may hold values from -6 to 6
Outputs:
- attended: bfloat16 [2, 4096, 2048], P('grp', 'seq', 'head')
- embed_grad: float32 [64, 3072], P(None, 'head')
The draws below stay inside these ranges and needn't reach their ends.
All inputs are finite; a program needn't handle non-finite values.
Results may differ from the reference program's by a relative error of at most 0.0052.
Values may be sent and summed in bfloat16 or wider, within the bound.
No kernel may reach another device: no remote copies, remote signals or barrier semaphores. Data moves between devices by JAX's collectives and lax.ppermute only.
A program may use at most 64 MiB of HBM per device.

```python
import jax
import jax.numpy as jnp
from jax import lax

C_ENC = 512
LAT = 16
D = 3072
HEADS = 32
HEAD_DIM = 64
LW = 32
CLIPS = 2
FRAMES = 32
LH = 16
PATCH = 64
TOKENS = 4096


def levels(key, extent, split, smallest, largest):
    def one(dim, shards_of):
        draws = jax.random.uniform(jax.random.fold_in(jax.random.fold_in(key, 6), dim), (shards_of,), jnp.float32, smallest / len(split), largest / len(split))
        return jnp.repeat(jnp.exp(draws), extent[dim] // shards_of).reshape((-1,) + (1,) * (len(extent) - dim - 1))

    factor_of = one(*split[0])
    for cut in split[1:]:
        factor_of = factor_of * one(*cut)
    return factor_of


def bell_draw(own_key, shape, spread, most, split=(), kind=jnp.bfloat16):
    result = jax.random.normal(own_key, shape, jnp.float32) * spread
    if len(split) > 0:
        result = levels(own_key, shape, split, -0.22, 0.18) * result
    return jnp.clip(result, min=-most, max=most).astype(kind)


def setup_inputs(seed: int = 0) -> dict:
    splits = jax.random.split(jax.random.key(seed), 9)
    features = bell_draw(splits[0], (CLIPS, FRAMES, LH, LW, C_ENC), 1.0, 6.0, ((0, 2), (1, 32), (2, 8)))
    conv_weight = bell_draw(splits[1], (3, 3, 3, C_ENC, LAT), (27 * C_ENC) ** -0.5, 0.0546875)
    conv_bias = bell_draw(splits[2], (LAT,), 0.5, 3.0, (), jnp.float32)
    token_order = jax.random.permutation(splits[3], TOKENS).astype(jnp.int32)
    embed_weight = bell_draw(splits[4], (PATCH, D), PATCH ** -0.5, 0.75)
    norm_gain = jnp.clip(1.0 + 0.18 * jax.random.normal(splits[5], (D,), jnp.float32), 0.1, 1.9)
    qkv_weight = bell_draw(splits[6], (D, 3, HEADS * HEAD_DIM), D ** -0.5, 0.109375, ((0, 32), (2, 8)))
    grad_out = bell_draw(splits[7], (CLIPS, TOKENS, HEADS * HEAD_DIM), 1.0, 6.0, ((0, 2), (1, 32), (2, 8)))
    return dict(features=features, conv_weight=conv_weight, conv_bias=conv_bias, token_order=token_order, embed_weight=embed_weight, norm_gain=norm_gain, qkv_weight=qkv_weight, grad_out=grad_out)


def encode(clip_feat, conv_weight, conv_bias):
    padded = jnp.pad(clip_feat, ((2, 0), (1, 1), (1, 1), (0, 0)))
    total = jnp.zeros((FRAMES * LH * LW, LAT), jnp.float32) + conv_bias
    for a in range(3):
        for b in range(3):
            for e in range(3):
                piece = padded[a:a + FRAMES, b:b + LH, e:e + LW].reshape(-1, C_ENC)
                total = total + jnp.dot(piece, conv_weight[a, b, e], preferred_element_type=jnp.float32)
    return total.astype(jnp.bfloat16).reshape(FRAMES, LH, LW, LAT)

def patchify(latent):
    frames = latent.shape[0]
    blocks = latent.reshape(frames, LH // 2, 2, LW // 2, 2, LAT)
    blocks = jnp.transpose(blocks, (0, 1, 3, 2, 4, 5))
    return blocks.reshape(frames * (LH // 2) * (LW // 2), 4 * LAT)

def one_head(operands):
    query, keys, values, cotan = operands
    factor = HEAD_DIM ** (-0.5)
    scores = jnp.dot(query, keys.T, preferred_element_type=jnp.float32) * factor
    top = lax.optimization_barrier(jnp.max(scores, axis=-1, keepdims=True))
    lse = top + jnp.log(lax.optimization_barrier(jnp.sum(jnp.exp(scores - top), axis=-1, keepdims=True)))
    probs = jnp.exp(scores - lse)
    probs_low = probs.astype(jnp.bfloat16)
    output = jnp.dot(probs_low, values, preferred_element_type=jnp.float32).astype(jnp.bfloat16)
    delta = lax.optimization_barrier(jnp.sum(cotan.astype(jnp.float32) * output.astype(jnp.float32), axis=-1, keepdims=True))
    dprob = jnp.dot(cotan, values.T, preferred_element_type=jnp.float32)
    dscore = (probs * (dprob - delta)).astype(jnp.bfloat16)
    grad_q = jnp.dot(dscore, keys, preferred_element_type=jnp.float32) * factor
    grad_k = jnp.dot(dscore.T, query, preferred_element_type=jnp.float32) * factor
    grad_v = jnp.dot(probs_low.T, cotan, preferred_element_type=jnp.float32)
    return (output, grad_q, grad_k, grad_v)

def per_heads(matrix):
    return jnp.transpose(matrix.reshape(TOKENS, HEADS, HEAD_DIM), (1, 0, 2))

def from_heads(stacked):
    return jnp.transpose(stacked, (1, 0, 2)).reshape(TOKENS, HEADS * HEAD_DIM)

def reference(features, conv_weight, conv_bias, token_order, embed_weight, norm_gain, qkv_weight, grad_out):
    width = HEADS * HEAD_DIM
    flat_weight = qkv_weight.reshape(D, 3 * width)
    outputs = []
    embed_grad = jnp.zeros((PATCH, D), jnp.float32)
    for clip in range(CLIPS):
        latent = encode(features[clip], conv_weight, conv_bias)
        patches = patchify(latent)
        tokens = jnp.take(patches, token_order.astype(jnp.int32), axis=0)
        mixed = jnp.dot(tokens, embed_weight, preferred_element_type=jnp.float32)
        inverse = lax.rsqrt(lax.optimization_barrier(jnp.mean(mixed * mixed, axis=-1, keepdims=True)) + 1e-06)
        normal = mixed * inverse
        hidden = (normal * norm_gain).astype(jnp.bfloat16)
        proj = jnp.dot(hidden, flat_weight, preferred_element_type=jnp.float32).astype(jnp.bfloat16)
        proj = proj.reshape(TOKENS, 3, width)
        output, grad_q, grad_k, grad_v = lax.map(one_head, (per_heads(proj[:, 0]), per_heads(proj[:, 1]), per_heads(proj[:, 2]), per_heads(grad_out[clip])))
        outputs.append(from_heads(output))
        grads = jnp.stack([from_heads(grad_q), from_heads(grad_k), from_heads(grad_v)], axis=1).reshape(TOKENS, 3 * width).astype(jnp.bfloat16)
        back = jnp.dot(grads, flat_weight.T, preferred_element_type=jnp.float32)
        scaled = back * norm_gain
        inner = lax.optimization_barrier(jnp.mean(scaled * normal, axis=-1, keepdims=True))
        dmixed = inverse * (scaled - normal * inner)
        embed_grad = embed_grad + jnp.dot(tokens.astype(jnp.float32).T, dmixed, preferred_element_type=jnp.float32, precision=lax.Precision.HIGHEST)
    return (jnp.stack(outputs, axis=0), embed_grad)
```

```python
import jax
import jax.numpy as jnp
from jax import lax
from jax.experimental import pallas as pl
from jax.experimental.pallas import tpu as pltpu
from jax.sharding import Mesh
from jax.sharding import PartitionSpec as P

D = 3072
HEAD_DIM = 64
FEAT = 64
SEQ = ("seq_0", "seq_1")
HEAD = ("head_0", "head_1")
PLANE = ("head_0", "head_1", "grp", "seq_0")
F32 = jnp.float32
BF16 = jnp.bfloat16
CHUNK = 512
HIGHEST = lax.Precision.HIGHEST


def shifted(value, axis, steps):
    count = lax.axis_size(axis)
    leading, last = (max(0, -steps), min(count, count - steps))
    return lax.ppermute(value, axis, [(source, source + steps) for source in range(leading, last)])


def extended(block, axis, dim, width):
    count = lax.axis_size(axis)
    forward = [(i, i + 1) for i in range(count - 1)]
    backward = [(target, source) for source, target in forward]
    low = lax.ppermute(
        lax.slice_in_dim(block, block.shape[dim] - width, None, axis=dim), axis, forward
    )
    high = lax.ppermute(lax.slice_in_dim(block, 0, width, axis=dim), axis, backward)
    return jnp.concatenate([low, block, high], axis=dim)


def from_everyone(array, axis):
    copies = jnp.broadcast_to(array, (lax.axis_size(axis), *array.shape))
    return lax.all_to_all(copies, axis, split_axis=0, concat_axis=0, tiled=True)


def encode_tile(tile, conv_weight, conv_bias):
    frames, rows, columns, channels = tile.shape
    earlier = [shifted(tile, SEQ, hop) for hop in (2, 1)]
    stacked = jnp.concatenate(earlier + [tile], axis=0)
    padded = extended(stacked, HEAD, 1, 1)
    padded = jnp.pad(padded, ((0, 0), (0, 0), (1, 1), (0, 0)))
    total = jnp.zeros((frames * rows * columns, conv_weight.shape[-1]), F32) + conv_bias
    for a in range(3):
        for b in range(3):
            for e in range(3):
                piece = padded[a : a + frames, b : b + rows, e : e + columns].reshape(-1, channels)
                total = total + jnp.dot(piece, conv_weight[a, b, e], preferred_element_type=F32)
    return total.astype(BF16).reshape(frames, rows, columns, conv_weight.shape[-1])


def two(x):
    high = x.astype(BF16)
    return high, (x - high.astype(F32)).astype(BF16)


def three(x):
    high, rest = x.astype(BF16), None
    rest = x - high.astype(F32)
    mid = rest.astype(BF16)
    return high, mid, (rest - mid.astype(F32)).astype(BF16)


def mm(a, b, dims=((1,), (0,)), precision=None):
    return lax.dot_general(a, b, (dims, ((), ())), preferred_element_type=F32, precision=precision)


NT = ((1,), (1,))
TN = ((0,), (0,))


def attention_kernel(
    x_ref, mt_ref, gram_ref, row_ref, half_ref, cot_ref,
    out_ref, at_ref, b_ref,
    both, keys, scores, probs, csum, query, qsum,
):
    head = pl.program_id(0)
    heads = pl.num_programs(0)
    pairs = x_ref.shape[0]
    factor = HEAD_DIM**-0.5
    zero = jnp.zeros((FEAT, FEAT), BF16)

    @pl.when(head == 0)
    def _():
        x = x_ref[...]
        pieces = [
            jnp.concatenate(
                [jnp.concatenate([g, zero], axis=1), jnp.concatenate([zero, g], axis=1)], axis=0
            )
            for g in three(gram_ref[...])
        ]
        y = (mm(x, pieces[2]) + mm(x, pieces[1])) + mm(x, pieces[0])
        lane_i = lax.broadcasted_iota(jnp.int32, (2 * FEAT, 2 * FEAT), 0) // FEAT
        lane_j = lax.broadcasted_iota(jnp.int32, (2 * FEAT, 2 * FEAT), 1) // FEAT
        ones = (lane_i == lane_j).astype(F32).astype(BF16)
        z = three(y * x.astype(F32))
        square = (mm(z[2], ones) + mm(z[1], ones)) + mm(z[0], ones)
        normed = x.astype(F32) * lax.rsqrt(jnp.maximum(square, 0.0) + 1e-06)
        high, low = two(normed)
        both[:, : 2 * FEAT] = high
        both[:, 2 * FEAT :] = low
        csum[...] = jnp.zeros_like(csum)
        qsum[...] = jnp.zeros_like(qsum)
        hot = lax.broadcasted_iota(jnp.int32, (row_ref.shape[0], pairs), 1) == row_ref[...]
        got = mm(hot.astype(F32).astype(BF16), both[...])
        second = half_ref[...] == 1
        for k in range(2):
            piece = got[:, 2 * FEAT * k : 2 * FEAT * (k + 1)]
            query[:, FEAT * k : FEAT * (k + 1)] = jnp.where(
                second, piece[:, FEAT:], piece[:, :FEAT]
            ).astype(BF16)

    pair, odd = head // 2, head % 2

    def weight(t):
        block = mt_ref[pl.ds(pl.multiple_of(t * 2 * FEAT + pair * FEAT, FEAT), FEAT), :]
        return jnp.where(odd == 1, block[:, FEAT:], block[:, :FEAT])

    w_q, w_k, w_v = weight(0), weight(1), weight(2)

    def stacked(pick):
        rows = []
        for w in (w_k, w_v):
            m = pick(w)
            rows.append(jnp.concatenate([m, zero], axis=1))
            rows.append(jnp.concatenate([zero, m], axis=1))
        return jnp.concatenate(rows, axis=0)

    main = stacked(lambda w: two(w)[0])
    rest = stacked(lambda w: two(w)[1])
    keys[...] = (
        mm(jnp.concatenate([main, main], axis=1), both[...], NT)
        + mm(rest, both[:, : 2 * FEAT], NT)
    ).astype(BF16)

    q_high, q_low = query[:, :FEAT], query[:, FEAT:]
    wq_high, wq_low = two(w_q)
    q = (mm(q_high, wq_high, NT) + (mm(q_high, wq_low, NT) + mm(q_low, wq_high, NT))).astype(BF16)
    q_scaled = (q.astype(F32) * factor).astype(BF16)
    cot = cot_ref[0]
    count = q.shape[0]

    top = jnp.full((count, 128), -jnp.inf, F32)
    for part in range(2):
        for c in range(0, pairs, CHUNK):
            s = mm(q_scaled, keys[part * FEAT : (part + 1) * FEAT, c : c + CHUNK])
            scores[:, part * pairs + c : part * pairs + c + CHUNK] = s
            for k in range(0, CHUNK, 128):
                top = jnp.maximum(top, s[:, k : k + 128])
    top = jnp.max(top, axis=1, keepdims=True)

    total = jnp.zeros((count, 128), F32)
    mixed = [jnp.zeros((count, 4 * FEAT), F32) for _ in range(2)]
    for part in range(2):
        for c in range(0, pairs, CHUNK):
            at = part * pairs + c
            p = jnp.exp(scores[:, at : at + CHUNK] - top)
            probs[:, at : at + CHUNK] = p
            for k in range(0, CHUNK, 128):
                total = total + p[:, k : k + 128]
            mixed[part] = mixed[part] + mm(p.astype(BF16), both[c : c + CHUNK, :])

    def folded(m):
        return (m[0][:, :FEAT] + m[0][:, 2 * FEAT : 3 * FEAT]) + (
            m[1][:, FEAT : 2 * FEAT] + m[1][:, 3 * FEAT :]
        )

    inverse = 1.0 / jnp.sum(total, axis=1, keepdims=True)
    value = folded(mixed) * inverse
    out = mm(value, w_v, NT, HIGHEST).astype(BF16)
    out_ref[0] = out
    delta = jnp.sum(cot.astype(F32) * out.astype(F32), axis=1, keepdims=True)

    mixed = [jnp.zeros((count, 4 * FEAT), F32) for _ in range(2)]
    for part in range(2):
        for c in range(0, pairs, CHUNK):
            at = part * pairs + c
            dp = mm(cot, keys[(2 + part) * FEAT : (3 + part) * FEAT, c : c + CHUNK])
            p = probs[:, at : at + CHUNK] * inverse
            ds = p * (dp - delta)
            mixed[part] = mixed[part] + mm(ds.astype(BF16), both[c : c + CHUNK, :])
            both_sides = ds * scores[:, at : at + CHUNK] + p * dp
            csum[:, at : at + CHUNK] += jnp.sum(both_sides.reshape(count // 8, 8, CHUNK), axis=0)
    grad = folded(mixed)
    dq = mm(grad, w_k, NT, HIGHEST) * factor
    q32 = q.astype(F32)
    qsum[...] += jnp.broadcast_to(jnp.sum(dq * q32, axis=1, keepdims=True), qsum.shape)
    own = q_high.astype(F32) + q_low.astype(F32)
    a_q = mm(dq, own, TN, HIGHEST)
    a_k = mm(q_scaled.astype(F32), grad, TN, HIGHEST)
    a_v = mm(cot.astype(F32), value, TN, HIGHEST)
    for t, a in enumerate((a_q, a_k, a_v)):
        rows = pl.ds(pl.multiple_of(t * 2 * FEAT + pair * FEAT, FEAT), FEAT)

        @pl.when(odd == 0)
        def _():
            at_ref[rows, :FEAT] = a

        @pl.when(odd == 1)
        def _():
            at_ref[rows, FEAT:] = a

    @pl.when(head == heads - 1)
    def _():
        eye_i = lax.broadcasted_iota(jnp.int32, (2 * FEAT, 2 * FEAT), 0)
        eye_j = lax.broadcasted_iota(jnp.int32, (2 * FEAT, 2 * FEAT), 1)
        eye = (eye_i == eye_j).astype(F32).astype(BF16)
        high = both[:, : 2 * FEAT]
        turned = mm(eye, high, NT)
        c_all = jnp.sum(csum[...], axis=0, keepdims=True)
        weighted = jnp.concatenate(
            [turned[:FEAT] * c_all[:, :pairs], turned[FEAT:] * c_all[:, pairs:]], axis=0
        )
        full = mm(weighted.astype(BF16), high)
        own_part = mm(own * qsum[:, :FEAT], own, TN, HIGHEST)
        b_ref[...] = ((full[:FEAT, :FEAT] + full[FEAT:, FEAT:]) + own_part) * (1.0 / D)


def attention(x, mt, gram, row, half, cot):
    heads, count, _ = cot.shape
    pairs = x.shape[0]
    whole = lambda *shape: pl.BlockSpec(shape, lambda i: (0,) * len(shape))
    per_head = pl.BlockSpec((1, count, HEAD_DIM), lambda i: (i, 0, 0))
    return pl.pallas_call(
        attention_kernel,
        grid=(heads,),
        in_specs=[
            whole(*x.shape), whole(*mt.shape), whole(*gram.shape),
            whole(*row.shape), whole(*half.shape), per_head,
        ],
        out_specs=[per_head, whole(*mt.shape), whole(*gram.shape)],
        out_shape=[
            jax.ShapeDtypeStruct(cot.shape, BF16),
            jax.ShapeDtypeStruct(mt.shape, F32),
            jax.ShapeDtypeStruct(gram.shape, F32),
        ],
        scratch_shapes=[
            pltpu.VMEM((pairs, 4 * FEAT), BF16),
            pltpu.VMEM((4 * FEAT, pairs), BF16),
            pltpu.VMEM((count, 2 * pairs), F32),
            pltpu.VMEM((count, 2 * pairs), F32),
            pltpu.VMEM((8, 2 * pairs), F32),
            pltpu.VMEM((count, 2 * FEAT), BF16),
            pltpu.VMEM((count, 128), F32),
        ],
        compiler_params=pltpu.CompilerParams(
            dimension_semantics=("arbitrary",), vmem_limit_bytes=48 * 1024 * 1024
        ),
        name="attention",
    )(x, mt, gram, row, half, cot)


def per_device(
    features, conv_weight, conv_bias, token_order, embed_weight, norm_gain, qkv_weight, grad_out
):
    seq_count = lax.axis_size(SEQ)
    depth, _, width = qkv_weight.shape
    heads = width // HEAD_DIM
    rows = 3 * (heads // 2) * HEAD_DIM
    rows_each = rows // seq_count

    w = qkv_weight.reshape(depth, 3, heads // 2, 2, HEAD_DIM)
    w = jnp.transpose(w, (1, 2, 4, 3, 0)).reshape(seq_count, rows_each * 2, depth)
    w_slice = lax.all_to_all(w, SEQ, 0, 0, tiled=True)
    embed32 = embed_weight.astype(F32)
    gained = jnp.concatenate(two(embed32 * norm_gain), axis=0).reshape(2 * FEAT, seq_count, depth)
    m_slice = lax.dot_general(
        w_slice, gained, (((0, 2), (1, 2)), ((), ())), preferred_element_type=F32
    )
    m_slice = (m_slice[:, :FEAT] + m_slice[:, FEAT:]).reshape(rows_each, 2 * FEAT)
    mt = from_everyone(m_slice, SEQ).reshape(rows, 2 * FEAT)
    gram = lax.dot_general(
        embed_weight, embed_weight, (((1,), (1,)), ((), ())), preferred_element_type=F32
    ) * (1.0 / D)

    tile = encode_tile(features[0], conv_weight, conv_bias)
    _, _, columns, channels = tile.shape
    patch = jnp.transpose(tile.reshape(2, columns // 2, 2, channels), (1, 0, 2, 3))
    patch = patch.reshape(2, columns // 4, FEAT)
    patch = jnp.transpose(patch, (1, 0, 2)).reshape(columns // 4, 2 * FEAT)
    every = from_everyone(from_everyone(patch, SEQ), HEAD)
    every = every.reshape(-1, 2 * FEAT)

    per_patch_row = columns // 4
    head_count = lax.axis_size(HEAD)
    j = token_order % (2 * per_patch_row)
    i = (token_order // (2 * per_patch_row)) % head_count
    f = token_order // (2 * per_patch_row * head_count)
    row = (i * seq_count + f) * per_patch_row + j % per_patch_row
    half = j // per_patch_row

    cot = jnp.transpose(grad_out[0].reshape(-1, heads, HEAD_DIM), (1, 0, 2))
    out, at, b = attention(every, mt, gram, row[:, None], half[:, None], cot)
    attended = jnp.transpose(out, (1, 0, 2)).reshape(1, -1, width)

    at = lax.all_to_all(at.reshape(seq_count, rows_each, 2 * FEAT), SEQ, 0, 0, tiled=True)
    a_slice = jnp.sum(at, axis=0).reshape(rows_each * 2, FEAT)
    a_both = jnp.concatenate(two(a_slice), axis=1)
    t = lax.dot_general(
        a_both, w_slice, (((0,), (1,)), ((), ())), preferred_element_type=F32
    )
    t = t[:FEAT] + t[FEAT:]
    second = jnp.dot(b, embed32, preferred_element_type=F32, precision=HIGHEST)
    t = t * norm_gain.reshape(seq_count, depth) - second.reshape(FEAT, seq_count, depth)
    t = jnp.transpose(t, (1, 0, 2)).astype(BF16)
    t = lax.all_to_all(t, PLANE, 0, 0, tiled=True)
    t = jnp.sum(t.astype(F32), axis=0)
    t = jnp.sum(from_everyone(t, "seq_1"), axis=0)
    t = from_everyone(t, ("grp", "seq_0"))
    embed_grad = jnp.transpose(t, (1, 0, 2)).reshape(FEAT, -1)
    return (attended, embed_grad)


def solution(mesh):
    torus = Mesh(
        mesh.devices.reshape(mesh.shape["grp"], 2, 16, 4, 2),
        ("grp", "seq_0", "seq_1", "head_0", "head_1"),
    )
    return jax.shard_map(
        per_device,
        mesh=torus,
        in_specs=(
            P("grp", SEQ, HEAD, None, None),
            P(),
            P(),
            P(SEQ),
            P(),
            P(),
            P(SEQ, None, HEAD),
            P("grp", SEQ, HEAD),
        ),
        out_specs=(P("grp", SEQ, HEAD), P(None, HEAD)),
        check_vma=False,
    )
```

```python
import jax
import jax.numpy as jnp
from jax import lax
from jax.experimental import pallas as pl
from jax.experimental.pallas import tpu as pltpu
from jax.sharding import Mesh
from jax.sharding import PartitionSpec as P

D = 3072
HEAD_DIM = 64
FEAT = 64
SEQ = ("seq_0", "seq_1")
HEAD = ("head_0", "head_1")
PLANE = ("head_0", "head_1", "grp", "seq_0")
F32 = jnp.float32
BF16 = jnp.bfloat16
CHUNK = 512
HIGHEST = lax.Precision.HIGHEST


def shifted(value, axis, steps):
    count = lax.axis_size(axis)
    leading, last = (max(0, -steps), min(count, count - steps))
    return lax.ppermute(value, axis, [(source, source + steps) for source in range(leading, last)])


def extended(block, axis, dim, width):
    count = lax.axis_size(axis)
    forward = [(i, i + 1) for i in range(count - 1)]
    backward = [(target, source) for source, target in forward]
    low = lax.ppermute(
        lax.slice_in_dim(block, block.shape[dim] - width, None, axis=dim), axis, forward
    )
    high = lax.ppermute(lax.slice_in_dim(block, 0, width, axis=dim), axis, backward)
    return jnp.concatenate([low, block, high], axis=dim)


def from_everyone(array, axis):
    copies = jnp.broadcast_to(array, (lax.axis_size(axis), *array.shape))
    return lax.all_to_all(copies, axis, split_axis=0, concat_axis=0, tiled=True)


def encode_tile(tile, conv_weight, conv_bias):
    frames, rows, columns, channels = tile.shape
    earlier = [shifted(tile, SEQ, hop) for hop in (2, 1)]
    stacked = jnp.concatenate(earlier + [tile], axis=0)
    padded = extended(stacked, HEAD, 1, 1)
    padded = jnp.pad(padded, ((0, 0), (0, 0), (1, 1), (0, 0)))
    total = jnp.zeros((frames * rows * columns, conv_weight.shape[-1]), F32) + conv_bias
    for a in range(3):
        for b in range(3):
            for e in range(3):
                piece = padded[a : a + frames, b : b + rows, e : e + columns].reshape(-1, channels)
                total = total + jnp.dot(piece, conv_weight[a, b, e], preferred_element_type=F32)
    return total.astype(BF16).reshape(frames, rows, columns, conv_weight.shape[-1])


def two(x):
    high = x.astype(BF16)
    return high, (x - high.astype(F32)).astype(BF16)


def three(x):
    high, rest = x.astype(BF16), None
    rest = x - high.astype(F32)
    mid = rest.astype(BF16)
    return high, mid, (rest - mid.astype(F32)).astype(BF16)


def mm(a, b, dims=((1,), (0,)), precision=None):
    return lax.dot_general(a, b, (dims, ((), ())), preferred_element_type=F32, precision=precision)


NT = ((1,), (1,))
TN = ((0,), (0,))


def attention_kernel(
    x_ref, high_ref, low_ref, gram_ref, row_ref, half_ref, cot_ref,
    out_ref, at_ref, b_ref,
    both, keys, scores, probs, csum, query, qsum,
):
    head = pl.program_id(0)
    heads = pl.num_programs(0)
    pairs = x_ref.shape[0]
    factor = HEAD_DIM**-0.5
    zero = jnp.zeros((FEAT, FEAT), BF16)

    @pl.when(head == 0)
    def _():
        x = x_ref[...]
        pieces = [
            jnp.concatenate(
                [jnp.concatenate([g, zero], axis=1), jnp.concatenate([zero, g], axis=1)], axis=0
            )
            for g in three(gram_ref[...])
        ]
        y = (mm(x, pieces[2]) + mm(x, pieces[1])) + mm(x, pieces[0])
        lane_i = lax.broadcasted_iota(jnp.int32, (2 * FEAT, 2 * FEAT), 0) // FEAT
        lane_j = lax.broadcasted_iota(jnp.int32, (2 * FEAT, 2 * FEAT), 1) // FEAT
        ones = (lane_i == lane_j).astype(F32).astype(BF16)
        z = three(y * x.astype(F32))
        square = (mm(z[2], ones) + mm(z[1], ones)) + mm(z[0], ones)
        normed = x.astype(F32) * lax.rsqrt(jnp.maximum(square, 0.0) + 1e-06)
        high, low = two(normed)
        both[:, : 2 * FEAT] = high
        both[:, 2 * FEAT :] = low
        csum[...] = jnp.zeros_like(csum)
        qsum[...] = jnp.zeros_like(qsum)
        hot = lax.broadcasted_iota(jnp.int32, (row_ref.shape[0], pairs), 1) == row_ref[...]
        got = mm(hot.astype(F32).astype(BF16), both[...])
        second = half_ref[...] == 1
        for k in range(2):
            piece = got[:, 2 * FEAT * k : 2 * FEAT * (k + 1)]
            query[:, FEAT * k : FEAT * (k + 1)] = jnp.where(
                second, piece[:, FEAT:], piece[:, :FEAT]
            ).astype(BF16)

    pair, odd = head // 2, head % 2

    def weight(t, ref):
        block = ref[pl.ds(pl.multiple_of(t * 2 * FEAT + pair * FEAT, FEAT), FEAT), :]
        block = block.astype(F32)
        return jnp.where(odd == 1, block[:, FEAT:], block[:, :FEAT])

    w_high = [weight(t, high_ref) for t in range(3)]
    w_low = [weight(t, low_ref) for t in range(3)]
    w_k, w_v = w_high[1] + w_low[1], w_high[2] + w_low[2]

    def stacked(parts):
        rows = []
        for m in parts:
            rows.append(jnp.concatenate([m, zero], axis=1))
            rows.append(jnp.concatenate([zero, m], axis=1))
        return jnp.concatenate(rows, axis=0)

    main = stacked([w.astype(BF16) for w in w_high[1:]])
    rest = stacked([w.astype(BF16) for w in w_low[1:]])
    keys[...] = (
        mm(jnp.concatenate([main, main], axis=1), both[...], NT)
        + mm(rest, both[:, : 2 * FEAT], NT)
    ).astype(BF16)

    q_high, q_low = query[:, :FEAT], query[:, FEAT:]
    wq_high, wq_low = w_high[0].astype(BF16), w_low[0].astype(BF16)
    q = (mm(q_high, wq_high, NT) + (mm(q_high, wq_low, NT) + mm(q_low, wq_high, NT))).astype(BF16)
    q_scaled = (q.astype(F32) * factor).astype(BF16)
    cot = cot_ref[0]
    count = q.shape[0]

    top = jnp.full((count, 128), -jnp.inf, F32)
    for part in range(2):
        for c in range(0, pairs, CHUNK):
            s = mm(q_scaled, keys[part * FEAT : (part + 1) * FEAT, c : c + CHUNK])
            scores[:, part * pairs + c : part * pairs + c + CHUNK] = s
            for k in range(0, CHUNK, 128):
                top = jnp.maximum(top, s[:, k : k + 128])
    top = jnp.max(top, axis=1, keepdims=True)

    total = jnp.zeros((count, 128), F32)
    mixed = [jnp.zeros((count, 4 * FEAT), F32) for _ in range(2)]
    for part in range(2):
        for c in range(0, pairs, CHUNK):
            at = part * pairs + c
            p = jnp.exp(scores[:, at : at + CHUNK] - top)
            probs[:, at : at + CHUNK] = p
            for k in range(0, CHUNK, 128):
                total = total + p[:, k : k + 128]
            mixed[part] = mixed[part] + mm(p.astype(BF16), both[c : c + CHUNK, :])

    def folded(m):
        return (m[0][:, :FEAT] + m[0][:, 2 * FEAT : 3 * FEAT]) + (
            m[1][:, FEAT : 2 * FEAT] + m[1][:, 3 * FEAT :]
        )

    inverse = 1.0 / jnp.sum(total, axis=1, keepdims=True)
    value = folded(mixed) * inverse
    out = mm(value, w_v, NT, HIGHEST).astype(BF16)
    out_ref[0] = out
    delta = jnp.sum(cot.astype(F32) * out.astype(F32), axis=1, keepdims=True)

    mixed = [jnp.zeros((count, 4 * FEAT), F32) for _ in range(2)]
    for part in range(2):
        for c in range(0, pairs, CHUNK):
            at = part * pairs + c
            dp = mm(cot, keys[(2 + part) * FEAT : (3 + part) * FEAT, c : c + CHUNK])
            p = probs[:, at : at + CHUNK] * inverse
            ds = p * (dp - delta)
            mixed[part] = mixed[part] + mm(ds.astype(BF16), both[c : c + CHUNK, :])
            both_sides = ds * scores[:, at : at + CHUNK] + p * dp
            csum[:, at : at + CHUNK] += jnp.sum(both_sides.reshape(count // 8, 8, CHUNK), axis=0)
    grad = folded(mixed)
    dq = mm(grad, w_k, NT, HIGHEST) * factor
    q32 = q.astype(F32)
    qsum[...] += jnp.broadcast_to(jnp.sum(dq * q32, axis=1, keepdims=True), qsum.shape)
    own = q_high.astype(F32) + q_low.astype(F32)
    a_q = mm(dq, own, TN, HIGHEST)
    a_k = mm(q_scaled.astype(F32), grad, TN, HIGHEST)
    a_v = mm(cot.astype(F32), value, TN, HIGHEST)
    for t, a in enumerate((a_q, a_k, a_v)):
        rows = pl.ds(pl.multiple_of(t * 2 * FEAT + pair * FEAT, FEAT), FEAT)

        @pl.when(odd == 0)
        def _():
            at_ref[rows, :FEAT] = a

        @pl.when(odd == 1)
        def _():
            at_ref[rows, FEAT:] = a

    @pl.when(head == heads - 1)
    def _():
        eye_i = lax.broadcasted_iota(jnp.int32, (2 * FEAT, 2 * FEAT), 0)
        eye_j = lax.broadcasted_iota(jnp.int32, (2 * FEAT, 2 * FEAT), 1)
        eye = (eye_i == eye_j).astype(F32).astype(BF16)
        high = both[:, : 2 * FEAT]
        turned = mm(eye, high, NT)
        c_all = jnp.sum(csum[...], axis=0, keepdims=True)
        weighted = jnp.concatenate(
            [turned[:FEAT] * c_all[:, :pairs], turned[FEAT:] * c_all[:, pairs:]], axis=0
        )
        full = mm(weighted.astype(BF16), high)
        own_part = mm(own * qsum[:, :FEAT], own, TN, HIGHEST)
        b_ref[...] = ((full[:FEAT, :FEAT] + full[FEAT:, FEAT:]) + own_part) * (1.0 / D)


def attention(x, high, low, gram, row, half, cot):
    heads, count, _ = cot.shape
    pairs = x.shape[0]
    whole = lambda *shape: pl.BlockSpec(shape, lambda i: (0,) * len(shape))
    per_head = pl.BlockSpec((1, count, HEAD_DIM), lambda i: (i, 0, 0))
    return pl.pallas_call(
        attention_kernel,
        grid=(heads,),
        in_specs=[
            whole(*x.shape), whole(*high.shape), whole(*low.shape), whole(*gram.shape),
            whole(*row.shape), whole(*half.shape), per_head,
        ],
        out_specs=[per_head, whole(*high.shape), whole(*gram.shape)],
        out_shape=[
            jax.ShapeDtypeStruct(cot.shape, BF16),
            jax.ShapeDtypeStruct(high.shape, F32),
            jax.ShapeDtypeStruct(gram.shape, F32),
        ],
        scratch_shapes=[
            pltpu.VMEM((pairs, 4 * FEAT), BF16),
            pltpu.VMEM((4 * FEAT, pairs), BF16),
            pltpu.VMEM((count, 2 * pairs), F32),
            pltpu.VMEM((count, 2 * pairs), F32),
            pltpu.VMEM((8, 2 * pairs), F32),
            pltpu.VMEM((count, 2 * FEAT), BF16),
            pltpu.VMEM((count, 128), F32),
        ],
        compiler_params=pltpu.CompilerParams(
            dimension_semantics=("arbitrary",), vmem_limit_bytes=48 * 1024 * 1024
        ),
        name="attention",
    )(x, high, low, gram, row, half, cot)


def per_device(
    features, conv_weight, conv_bias, token_order, embed_weight, norm_gain, qkv_weight, grad_out
):
    seq_count = lax.axis_size(SEQ)
    depth, _, width = qkv_weight.shape
    heads = width // HEAD_DIM
    rows = 3 * (heads // 2) * HEAD_DIM
    rows_each = rows // seq_count

    w = qkv_weight.reshape(depth, 3, heads // 2, 2, HEAD_DIM)
    w = jnp.transpose(w, (1, 2, 4, 3, 0)).reshape(seq_count, rows_each * 2, depth)
    w_slice = lax.all_to_all(w, SEQ, 0, 0, tiled=True)
    w_slice = jnp.transpose(w_slice, (1, 0, 2)).reshape(rows_each * 2, D)
    embed32 = embed_weight.astype(F32)
    gained = jnp.concatenate(two(embed32 * norm_gain), axis=0)
    m_slice = mm(w_slice, gained, NT)
    m_slice = (m_slice[:, :FEAT] + m_slice[:, FEAT:]).reshape(rows_each, 2 * FEAT)
    gram = lax.dot_general(
        embed_weight, embed_weight, (((1,), (1,)), ((), ())), preferred_element_type=F32
    ) * (1.0 / D)

    tile = encode_tile(features[0], conv_weight, conv_bias)
    _, _, columns, channels = tile.shape
    patch = jnp.transpose(tile.reshape(2, columns // 2, 2, channels), (1, 0, 2, 3))
    patch = patch.reshape(2, columns // 4, FEAT)
    patch = jnp.transpose(patch, (1, 0, 2)).reshape(columns // 4, 2 * FEAT)
    own_rows = columns // 4
    arrived = from_everyone(jnp.concatenate([patch, *two(m_slice)], axis=0), SEQ)
    every = from_everyone(arrived[:, :own_rows], HEAD).reshape(-1, 2 * FEAT)
    m_high = arrived[:, own_rows : own_rows + rows_each].reshape(rows, 2 * FEAT)
    m_low = arrived[:, own_rows + rows_each :].reshape(rows, 2 * FEAT)

    per_patch_row = columns // 4
    head_count = lax.axis_size(HEAD)
    j = token_order % (2 * per_patch_row)
    i = (token_order // (2 * per_patch_row)) % head_count
    f = token_order // (2 * per_patch_row * head_count)
    row = (i * seq_count + f) * per_patch_row + j % per_patch_row
    half = j // per_patch_row

    cot = jnp.transpose(grad_out[0].reshape(-1, heads, HEAD_DIM), (1, 0, 2))
    out, at, b = attention(every, m_high, m_low, gram, row[:, None], half[:, None], cot)
    attended = jnp.transpose(out, (1, 0, 2)).reshape(1, -1, width)

    at = lax.all_to_all(at.reshape(seq_count, rows_each, 2 * FEAT), SEQ, 0, 0, tiled=True)
    a_slice = jnp.sum(at, axis=0).reshape(rows_each * 2, FEAT)
    a_both = jnp.concatenate(two(a_slice), axis=1)
    t = mm(a_both, w_slice, TN)
    t = t[:FEAT] + t[FEAT:]
    t = t * norm_gain - mm(b, embed32, precision=HIGHEST)
    parts = lax.axis_size(("grp", "seq_0"))
    t = jnp.transpose(t.reshape(parts, FEAT // parts, head_count, -1), (2, 0, 1, 3))
    t = t.astype(BF16).reshape(parts * head_count, FEAT // parts, -1)
    t = lax.all_to_all(t, PLANE, 0, 0, tiled=True)
    t = jnp.sum(t.astype(F32), axis=0).astype(BF16)
    t = jnp.sum(from_everyone(t, "seq_1").astype(F32), axis=0)
    embed_grad = from_everyone(t, ("grp", "seq_0")).reshape(FEAT, -1)
    return (attended, embed_grad)


def solution(mesh):
    torus = Mesh(
        mesh.devices.reshape(mesh.shape["grp"], 2, 16, 4, 2),
        ("grp", "seq_0", "seq_1", "head_0", "head_1"),
    )
    return jax.shard_map(
        per_device,
        mesh=torus,
        in_specs=(
            P("grp", SEQ, HEAD, None, None),
            P(),
            P(),
            P(SEQ),
            P(),
            P(),
            P(SEQ, None, HEAD),
            P("grp", SEQ, HEAD),
        ),
        out_specs=(P("grp", SEQ, HEAD), P(None, HEAD)),
        check_vma=False,
    )
```

```python
import jax
import jax.numpy as jnp
from jax import lax
from jax.experimental import pallas as pl
from jax.experimental.pallas import tpu as pltpu
from jax.sharding import Mesh
from jax.sharding import PartitionSpec as P

D = 3072
HEAD_DIM = 64
FEAT = 64
SEQ = ("seq_0", "seq_1")
HEAD = ("head_0", "head_1")
PLANE = ("head_0", "head_1", "grp", "seq_0")
F32 = jnp.float32
BF16 = jnp.bfloat16
CHUNK = 512
HIGHEST = lax.Precision.HIGHEST


def shifted(value, axis, steps):
    count = lax.axis_size(axis)
    leading, last = (max(0, -steps), min(count, count - steps))
    return lax.ppermute(value, axis, [(source, source + steps) for source in range(leading, last)])


def extended(block, axis, dim, width):
    count = lax.axis_size(axis)
    forward = [(i, i + 1) for i in range(count - 1)]
    backward = [(target, source) for source, target in forward]
    low = lax.ppermute(
        lax.slice_in_dim(block, block.shape[dim] - width, None, axis=dim), axis, forward
    )
    high = lax.ppermute(lax.slice_in_dim(block, 0, width, axis=dim), axis, backward)
    return jnp.concatenate([low, block, high], axis=dim)


def from_everyone(array, axis):
    copies = jnp.broadcast_to(array, (lax.axis_size(axis), *array.shape))
    return lax.all_to_all(copies, axis, split_axis=0, concat_axis=0, tiled=True)


def encode_tile(tile, conv_weight, conv_bias):
    frames, rows, columns, channels = tile.shape
    earlier = [shifted(tile, SEQ, hop) for hop in (2, 1)]
    stacked = jnp.concatenate(earlier + [tile], axis=0)
    padded = extended(stacked, HEAD, 1, 1)
    padded = jnp.pad(padded, ((0, 0), (0, 0), (1, 1), (0, 0)))
    total = jnp.zeros((frames * rows * columns, conv_weight.shape[-1]), F32) + conv_bias
    for a in range(3):
        for b in range(3):
            for e in range(3):
                piece = padded[a : a + frames, b : b + rows, e : e + columns].reshape(-1, channels)
                total = total + jnp.dot(piece, conv_weight[a, b, e], preferred_element_type=F32)
    return total.astype(BF16).reshape(frames, rows, columns, conv_weight.shape[-1])


def two(x):
    high = x.astype(BF16)
    return high, (x - high.astype(F32)).astype(BF16)


def three(x):
    high, rest = x.astype(BF16), None
    rest = x - high.astype(F32)
    mid = rest.astype(BF16)
    return high, mid, (rest - mid.astype(F32)).astype(BF16)


def mm(a, b, dims=((1,), (0,)), precision=None):
    return lax.dot_general(a, b, (dims, ((), ())), preferred_element_type=F32, precision=precision)


NT = ((1,), (1,))
TN = ((0,), (0,))


def attention_kernel(
    x_ref, high_ref, low_ref, gram_ref, row_ref, half_ref, cot_ref,
    out_ref, at_ref, b_ref,
    both, keys, scores, probs, csum, query, qsum,
):
    head = pl.program_id(0)
    heads = pl.num_programs(0)
    pairs = x_ref.shape[0]
    factor = HEAD_DIM**-0.5
    zero = jnp.zeros((FEAT, FEAT), BF16)

    @pl.when(head == 0)
    def _():
        x = x_ref[...]
        pieces = [
            jnp.concatenate(
                [jnp.concatenate([g, zero], axis=1), jnp.concatenate([zero, g], axis=1)], axis=0
            )
            for g in three(gram_ref[...])
        ]
        y = (mm(x, pieces[2]) + mm(x, pieces[1])) + mm(x, pieces[0])
        lane_i = lax.broadcasted_iota(jnp.int32, (2 * FEAT, 2 * FEAT), 0) // FEAT
        lane_j = lax.broadcasted_iota(jnp.int32, (2 * FEAT, 2 * FEAT), 1) // FEAT
        ones = (lane_i == lane_j).astype(F32).astype(BF16)
        z = three(y * x.astype(F32))
        square = (mm(z[2], ones) + mm(z[1], ones)) + mm(z[0], ones)
        normed = x.astype(F32) * lax.rsqrt(jnp.maximum(square, 0.0) + 1e-06)
        high, low = two(normed)
        both[:, : 2 * FEAT] = high
        both[:, 2 * FEAT :] = low
        csum[...] = jnp.zeros_like(csum)
        qsum[...] = jnp.zeros_like(qsum)
        hot = lax.broadcasted_iota(jnp.int32, (row_ref.shape[0], pairs), 1) == row_ref[...]
        got = mm(hot.astype(F32).astype(BF16), both[...])
        second = half_ref[...] == 1
        for k in range(2):
            piece = got[:, 2 * FEAT * k : 2 * FEAT * (k + 1)]
            query[:, FEAT * k : FEAT * (k + 1)] = jnp.where(
                second, piece[:, FEAT:], piece[:, :FEAT]
            ).astype(BF16)

    odd = head % 2

    def weight(t, ref):
        block = ref[t * FEAT : (t + 1) * FEAT, :]
        block = block.astype(F32)
        return jnp.where(odd == 1, block[:, FEAT:], block[:, :FEAT])

    w_high = [weight(t, high_ref) for t in range(3)]
    w_low = [weight(t, low_ref) for t in range(3)]
    w_k, w_v = w_high[1] + w_low[1], w_high[2] + w_low[2]

    def stacked(parts):
        rows = []
        for m in parts:
            rows.append(jnp.concatenate([m, zero], axis=1))
            rows.append(jnp.concatenate([zero, m], axis=1))
        return jnp.concatenate(rows, axis=0)

    main = stacked([w.astype(BF16) for w in w_high[1:]])
    rest = stacked([w.astype(BF16) for w in w_low[1:]])
    keys[...] = (
        mm(jnp.concatenate([main, main], axis=1), both[...], NT)
        + mm(rest, both[:, : 2 * FEAT], NT)
    ).astype(BF16)

    q_high, q_low = query[:, :FEAT], query[:, FEAT:]
    wq_high, wq_low = w_high[0].astype(BF16), w_low[0].astype(BF16)
    q = (mm(q_high, wq_high, NT) + (mm(q_high, wq_low, NT) + mm(q_low, wq_high, NT))).astype(BF16)
    q_scaled = (q.astype(F32) * factor).astype(BF16)
    cot = cot_ref[0]
    count = q.shape[0]

    top = jnp.full((count, 128), -jnp.inf, F32)
    for part in range(2):
        for c in range(0, pairs, CHUNK):
            s = mm(q_scaled, keys[part * FEAT : (part + 1) * FEAT, c : c + CHUNK])
            scores[:, part * pairs + c : part * pairs + c + CHUNK] = s
            for k in range(0, CHUNK, 128):
                top = jnp.maximum(top, s[:, k : k + 128])
    top = jnp.max(top, axis=1, keepdims=True)

    total = jnp.zeros((count, 128), F32)
    mixed = [jnp.zeros((count, 4 * FEAT), F32) for _ in range(2)]
    for part in range(2):
        for c in range(0, pairs, CHUNK):
            at = part * pairs + c
            p = jnp.exp(scores[:, at : at + CHUNK] - top)
            probs[:, at : at + CHUNK] = p
            for k in range(0, CHUNK, 128):
                total = total + p[:, k : k + 128]
            mixed[part] = mixed[part] + mm(p.astype(BF16), both[c : c + CHUNK, :])

    def folded(m):
        return (m[0][:, :FEAT] + m[0][:, 2 * FEAT : 3 * FEAT]) + (
            m[1][:, FEAT : 2 * FEAT] + m[1][:, 3 * FEAT :]
        )

    inverse = 1.0 / jnp.sum(total, axis=1, keepdims=True)
    value = folded(mixed) * inverse
    out = mm(value, w_v, NT, HIGHEST).astype(BF16)
    out_ref[0] = out
    delta = jnp.sum(cot.astype(F32) * out.astype(F32), axis=1, keepdims=True)

    mixed = [jnp.zeros((count, 4 * FEAT), F32) for _ in range(2)]
    for part in range(2):
        for c in range(0, pairs, CHUNK):
            at = part * pairs + c
            dp = mm(cot, keys[(2 + part) * FEAT : (3 + part) * FEAT, c : c + CHUNK])
            p = probs[:, at : at + CHUNK] * inverse
            ds = p * (dp - delta)
            mixed[part] = mixed[part] + mm(ds.astype(BF16), both[c : c + CHUNK, :])
            both_sides = ds * scores[:, at : at + CHUNK] + p * dp
            csum[:, at : at + CHUNK] += jnp.sum(both_sides.reshape(count // 8, 8, CHUNK), axis=0)
    grad = folded(mixed)
    dq = mm(grad, w_k, NT, HIGHEST) * factor
    q32 = q.astype(F32)
    qsum[...] += jnp.broadcast_to(jnp.sum(dq * q32, axis=1, keepdims=True), qsum.shape)
    own = q_high.astype(F32) + q_low.astype(F32)
    a_q = mm(dq, own, TN, HIGHEST)
    a_k = mm(q_scaled.astype(F32), grad, TN, HIGHEST)
    a_v = mm(cot.astype(F32), value, TN, HIGHEST)
    for t, a in enumerate((a_q, a_k, a_v)):
        at_ref[pl.ds(pl.multiple_of(t * 2 * FEAT + odd * FEAT, FEAT), FEAT), :] = a

    @pl.when(head == heads - 1)
    def _():
        eye_i = lax.broadcasted_iota(jnp.int32, (2 * FEAT, 2 * FEAT), 0)
        eye_j = lax.broadcasted_iota(jnp.int32, (2 * FEAT, 2 * FEAT), 1)
        eye = (eye_i == eye_j).astype(F32).astype(BF16)
        high = both[:, : 2 * FEAT]
        turned = mm(eye, high, NT)
        c_all = jnp.sum(csum[...], axis=0, keepdims=True)
        weighted = jnp.concatenate(
            [turned[:FEAT] * c_all[:, :pairs], turned[FEAT:] * c_all[:, pairs:]], axis=0
        )
        full = mm(weighted.astype(BF16), high)
        own_part = mm(own * qsum[:, :FEAT], own, TN, HIGHEST)
        b_ref[...] = ((full[:FEAT, :FEAT] + full[FEAT:, FEAT:]) + own_part) * (1.0 / D)


def attention(x, high, low, gram, row, half, cot):
    heads, count, _ = cot.shape
    pairs = x.shape[0]
    whole = lambda *shape: pl.BlockSpec(shape, lambda i: (0,) * len(shape))
    per_head = pl.BlockSpec((1, count, HEAD_DIM), lambda i: (i, 0, 0))
    return pl.pallas_call(
        attention_kernel,
        grid=(heads,),
        in_specs=[
            whole(*x.shape), whole(*high.shape), whole(*low.shape), whole(*gram.shape),
            whole(*row.shape), whole(*half.shape), per_head,
        ],
        out_specs=[per_head, whole(2 * high.shape[0], FEAT), whole(*gram.shape)],
        out_shape=[
            jax.ShapeDtypeStruct(cot.shape, BF16),
            jax.ShapeDtypeStruct((2 * high.shape[0], FEAT), F32),
            jax.ShapeDtypeStruct(gram.shape, F32),
        ],
        scratch_shapes=[
            pltpu.VMEM((pairs, 4 * FEAT), BF16),
            pltpu.VMEM((4 * FEAT, pairs), BF16),
            pltpu.VMEM((count, 2 * pairs), F32),
            pltpu.VMEM((count, 2 * pairs), F32),
            pltpu.VMEM((8, 2 * pairs), F32),
            pltpu.VMEM((count, 2 * FEAT), BF16),
            pltpu.VMEM((count, 128), F32),
        ],
        compiler_params=pltpu.CompilerParams(
            dimension_semantics=("arbitrary",), vmem_limit_bytes=48 * 1024 * 1024
        ),
        name="attention",
    )(x, high, low, gram, row, half, cot)


def per_device(
    features, conv_weight, conv_bias, token_order, embed_weight, norm_gain, qkv_weight, grad_out
):
    far = lax.axis_index("seq_0")
    near_count = lax.axis_size("seq_1")
    depth, _, width = qkv_weight.shape
    pair = 2 * HEAD_DIM
    rows = 3 * HEAD_DIM
    rows_each = rows // near_count

    def swapped(array, axis):
        first, second = jnp.split(array, 2, axis=axis)
        mine = jnp.where(far == 0, first, second)
        given = jnp.where(far == 0, second, first)
        return mine, lax.ppermute(given, "seq_0", [(0, 1), (1, 0)])

    def in_order(mine, other):
        return jnp.where(far == 0, jnp.stack([mine, other]), jnp.stack([other, mine]))

    w = in_order(*swapped(qkv_weight, 2)).reshape(2, depth, 3 * pair)
    embed32 = embed_weight.astype(F32)
    start = lax.axis_index("seq_1") * depth
    m_part = 0.0
    for k in range(2):
        at = start + k * (D // 2)
        gained = lax.dynamic_slice_in_dim(embed_weight, at, depth, 1).astype(F32)
        gained = jnp.concatenate(
            two(gained * lax.dynamic_slice_in_dim(norm_gain, at, depth, 0)), axis=0
        )
        m_part = m_part + lax.dot_general(
            w[k], gained, (((0,), (1,)), ((), ())), preferred_element_type=F32
        )
    m_part = (m_part[:, :FEAT] + m_part[:, FEAT:]).reshape(3, 2, HEAD_DIM, FEAT)
    m_part = jnp.transpose(m_part, (0, 2, 1, 3)).reshape(near_count, rows_each, 2 * FEAT)
    m_slice = jnp.sum(lax.all_to_all(m_part, "seq_1", 0, 0, tiled=True), axis=0)
    w_full = lax.all_gather(w, "seq_1", axis=0)
    gram = lax.dot_general(
        embed_weight, embed_weight, (((1,), (1,)), ((), ())), preferred_element_type=F32
    ) * (1.0 / D)

    tile = encode_tile(features[0], conv_weight, conv_bias)
    _, _, columns, channels = tile.shape
    patch = jnp.transpose(tile.reshape(2, columns // 2, 2, channels), (1, 0, 2, 3))
    patch = patch.reshape(2, columns // 4, FEAT)
    patch = jnp.transpose(patch, (1, 0, 2)).reshape(columns // 4, 2 * FEAT)
    own_rows = columns // 4
    arrived = from_everyone(jnp.concatenate([patch, *two(m_slice)], axis=0), "seq_1")
    every = from_everyone(arrived[:, :own_rows], ("seq_0", *HEAD)).reshape(-1, 2 * FEAT)
    m_high = arrived[:, own_rows : own_rows + rows_each].reshape(rows, 2 * FEAT)
    m_low = arrived[:, own_rows + rows_each :].reshape(rows, 2 * FEAT)

    per_patch_row = columns // 4
    head_count = lax.axis_size(HEAD)
    order = in_order(token_order, lax.ppermute(token_order, "seq_0", [(0, 1), (1, 0)]))
    order = order.reshape(-1, 1)
    j = order % (2 * per_patch_row)
    i = (order // (2 * per_patch_row)) % head_count
    f = order // (2 * per_patch_row * head_count)
    plane = (f // near_count) * head_count + i
    row = (plane * near_count + f % near_count) * per_patch_row + j % per_patch_row
    half = j // per_patch_row

    cot = in_order(*swapped(grad_out[0], 1)).reshape(-1, 2, HEAD_DIM)
    out, at, b = attention(
        every, m_high, m_low, gram, row, half, jnp.transpose(cot, (1, 0, 2))
    )
    out = jnp.transpose(out, (1, 0, 2)).reshape(2, -1, pair)
    mine = jnp.where(far == 0, out[0], out[1])
    other = lax.ppermute(jnp.where(far == 0, out[1], out[0]), "seq_0", [(0, 1), (1, 0)])
    attended = jnp.where(
        far == 0,
        jnp.concatenate([mine, other], axis=1),
        jnp.concatenate([other, mine], axis=1),
    )[None]

    a_both = jnp.concatenate(two(at), axis=1)
    w_full = jnp.transpose(w_full, (1, 0, 2, 3)).reshape(D, 3 * pair)
    t = mm(a_both, w_full, ((0,), (1,)))
    t = t[:FEAT] + t[FEAT:]
    t = t * norm_gain - mm(b, embed32, precision=HIGHEST)
    parts = lax.axis_size(("grp", "seq_0"))
    t = jnp.transpose(t.reshape(parts, FEAT // parts, head_count, -1), (2, 0, 1, 3))
    t = t.astype(BF16).reshape(parts * head_count, FEAT // parts, -1)
    t = lax.all_to_all(t, PLANE, 0, 0, tiled=True)
    t = jnp.sum(t.astype(F32), axis=0).astype(BF16)
    t = jnp.sum(from_everyone(t, "seq_1").astype(F32), axis=0)
    embed_grad = from_everyone(t, ("grp", "seq_0")).reshape(FEAT, -1)
    return (attended, embed_grad)


def solution(mesh):
    torus = Mesh(
        mesh.devices.reshape(mesh.shape["grp"], 2, 16, 4, 2),
        ("grp", "seq_0", "seq_1", "head_0", "head_1"),
    )
    return jax.shard_map(
        per_device,
        mesh=torus,
        in_specs=(
            P("grp", SEQ, HEAD, None, None),
            P(),
            P(),
            P(SEQ),
            P(),
            P(),
            P(SEQ, None, HEAD),
            P("grp", SEQ, HEAD),
        ),
        out_specs=(P("grp", SEQ, HEAD), P(None, HEAD)),
        check_vma=False,
    )
```

```python
import jax
import jax.numpy as jnp
from jax import lax
from jax.experimental import pallas as pl
from jax.experimental.pallas import tpu as pltpu
from jax.sharding import Mesh
from jax.sharding import PartitionSpec as P

D = 3072
HEAD_DIM = 64
FEAT = 64
SEQ = ("seq_0", "seq_1")
HEAD = ("head_0", "head_1")
PLANE = ("head_0", "head_1", "grp", "seq_0")
F32 = jnp.float32
BF16 = jnp.bfloat16
CHUNK = 512
HIGHEST = lax.Precision.HIGHEST


def shifted(value, axis, steps):
    count = lax.axis_size(axis)
    leading, last = (max(0, -steps), min(count, count - steps))
    return lax.ppermute(value, axis, [(source, source + steps) for source in range(leading, last)])


def from_everyone(array, axis):
    copies = jnp.broadcast_to(array, (lax.axis_size(axis), *array.shape))
    return lax.all_to_all(copies, axis, split_axis=0, concat_axis=0, tiled=True)


def two(x):
    high = x.astype(BF16)
    return high, (x - high.astype(F32)).astype(BF16)


def three(x):
    high, rest = x.astype(BF16), None
    rest = x - high.astype(F32)
    mid = rest.astype(BF16)
    return high, mid, (rest - mid.astype(F32)).astype(BF16)


def mm(a, b, dims=((1,), (0,)), precision=None):
    return lax.dot_general(a, b, (dims, ((), ())), preferred_element_type=F32, precision=precision)


NT = ((1,), (1,))
TN = ((0,), (0,))


def conv_kernel(f_ref, w_ref, out_ref):
    tile = f_ref[...]
    spots, channels = tile.shape
    half = spots // 2
    cols = half // 2
    lat = w_ref.shape[0] // 27
    to = lax.broadcasted_iota(jnp.int32, (spots, spots), 0)
    source = (to // cols % 2) * half + (to % cols) * 2 + to // half
    pick = lax.broadcasted_iota(jnp.int32, (spots, spots), 1) == source
    tile = mm(pick.astype(F32).astype(BF16), tile).astype(BF16)
    zero = jnp.zeros((lat, channels), BF16)

    def block(a, taps):
        rows = []
        for b in (2, 1, 0):
            for e in taps:
                at = ((a * 3 + b) * 3 + e) * lat if e is not None else 0
                rows.append(zero if e is None else w_ref[at : at + lat, :])
        return rows + [zero, zero]

    row = lax.broadcasted_iota(jnp.int32, (cols, 128), 0)
    sums = [0.0] * 3
    for parity, here, there, shift in ((0, (1, 0), (None, 2), cols - 1), (1, (2, 1), (0, None), 1)):
        weights = jnp.concatenate(
            [w for taps in (here, there) for a in range(3) for w in block(a, taps)], axis=0
        )
        got = mm(tile[parity * half : (parity + 1) * half], weights, NT)
        edge = cols - 1 if parity == 0 else 0
        for a in range(3):
            near = got[:, a * 128 : (a + 1) * 128]
            far = got[:, (a + 3) * 128 : (a + 4) * 128]
            for r in range(2):
                moved = pltpu.roll(far[r * cols : (r + 1) * cols], shift, 0)
                both = near[r * cols : (r + 1) * cols] + jnp.where(row == edge, 0.0, moved)
                sums[a] = sums[a] + (both if r == 0 else pltpu.roll(both, 32, 1))
    for a in range(3):
        out_ref[a] = sums[a]


def encode_tile(tile, conv_weight, conv_bias):
    rows, columns, channels = tile.shape
    lat = conv_weight.shape[-1]
    weight = jnp.moveaxis(conv_weight, 4, 3).reshape(27 * lat, channels)
    parts = pl.pallas_call(
        conv_kernel,
        out_shape=jax.ShapeDtypeStruct((3, columns // 2, 8 * lat), F32),
        name="taps",
    )(tile.reshape(rows * columns, channels), weight)
    total = (parts[2] + shifted(parts[1], SEQ, 1)) + shifted(parts[0], SEQ, 2)
    above, below = shifted(total, HEAD, 1), shifted(total, HEAD, -1)
    own = total[:, 2 * lat : 6 * lat]
    own = own + jnp.concatenate([above[:, 6 * lat :], below[:, : 2 * lat]], axis=1)
    patch = (own + jnp.tile(conv_bias, 4)).astype(BF16)
    first, second = jnp.split(patch, 2, axis=0)
    return jnp.concatenate([first, second], axis=1)


def attention_kernel(
    x_ref, high_ref, low_ref, gram_ref, row_ref, half_ref, cot_ref,
    out_ref, at_ref, b_ref,
    both, keys, scores, probs, csum, query, qsum,
):
    head = pl.program_id(0)
    heads = pl.num_programs(0)
    pairs = x_ref.shape[0]
    factor = HEAD_DIM**-0.5
    zero = jnp.zeros((FEAT, FEAT), BF16)

    @pl.when(head == 0)
    def _():
        x = x_ref[...]
        pieces = [
            jnp.concatenate(
                [jnp.concatenate([g, zero], axis=1), jnp.concatenate([zero, g], axis=1)], axis=0
            )
            for g in three(gram_ref[...])
        ]
        y = (mm(x, pieces[2]) + mm(x, pieces[1])) + mm(x, pieces[0])
        lane_i = lax.broadcasted_iota(jnp.int32, (2 * FEAT, 2 * FEAT), 0) // FEAT
        lane_j = lax.broadcasted_iota(jnp.int32, (2 * FEAT, 2 * FEAT), 1) // FEAT
        ones = (lane_i == lane_j).astype(F32).astype(BF16)
        z = three(y * x.astype(F32))
        square = (mm(z[2], ones) + mm(z[1], ones)) + mm(z[0], ones)
        normed = x.astype(F32) * lax.rsqrt(jnp.maximum(square, 0.0) + 1e-06)
        high, low = two(normed)
        both[:, : 2 * FEAT] = high
        both[:, 2 * FEAT :] = low
        csum[...] = jnp.zeros_like(csum)
        qsum[...] = jnp.zeros_like(qsum)
        hot = lax.broadcasted_iota(jnp.int32, (row_ref.shape[0], pairs), 1) == row_ref[...]
        got = mm(hot.astype(F32).astype(BF16), both[...])
        second = half_ref[...] == 1
        for k in range(2):
            piece = got[:, 2 * FEAT * k : 2 * FEAT * (k + 1)]
            query[:, FEAT * k : FEAT * (k + 1)] = jnp.where(
                second, piece[:, FEAT:], piece[:, :FEAT]
            ).astype(BF16)

    odd = head % 2

    def weight(t, ref):
        block = ref[t * FEAT : (t + 1) * FEAT, :]
        block = block.astype(F32)
        return jnp.where(odd == 1, block[:, FEAT:], block[:, :FEAT])

    w_high = [weight(t, high_ref) for t in range(3)]
    w_low = [weight(t, low_ref) for t in range(3)]
    w_k, w_v = w_high[1] + w_low[1], w_high[2] + w_low[2]

    def stacked(parts):
        rows = []
        for m in parts:
            rows.append(jnp.concatenate([m, zero], axis=1))
            rows.append(jnp.concatenate([zero, m], axis=1))
        return jnp.concatenate(rows, axis=0)

    main = stacked([w.astype(BF16) for w in w_high[1:]])
    rest = stacked([w.astype(BF16) for w in w_low[1:]])
    keys[...] = (
        mm(jnp.concatenate([main, main], axis=1), both[...], NT)
        + mm(rest, both[:, : 2 * FEAT], NT)
    ).astype(BF16)

    q_high, q_low = query[:, :FEAT], query[:, FEAT:]
    wq_high, wq_low = w_high[0].astype(BF16), w_low[0].astype(BF16)
    q = (mm(q_high, wq_high, NT) + (mm(q_high, wq_low, NT) + mm(q_low, wq_high, NT))).astype(BF16)
    q_scaled = (q.astype(F32) * factor).astype(BF16)
    cot = cot_ref[0]
    count = q.shape[0]

    top = jnp.full((count, 128), -jnp.inf, F32)
    for part in range(2):
        for c in range(0, pairs, CHUNK):
            s = mm(q_scaled, keys[part * FEAT : (part + 1) * FEAT, c : c + CHUNK])
            scores[:, part * pairs + c : part * pairs + c + CHUNK] = s
            for k in range(0, CHUNK, 128):
                top = jnp.maximum(top, s[:, k : k + 128])
    top = jnp.max(top, axis=1, keepdims=True)

    total = jnp.zeros((count, 128), F32)
    mixed = [jnp.zeros((count, 4 * FEAT), F32) for _ in range(2)]
    for part in range(2):
        for c in range(0, pairs, CHUNK):
            at = part * pairs + c
            p = jnp.exp(scores[:, at : at + CHUNK] - top)
            probs[:, at : at + CHUNK] = p
            for k in range(0, CHUNK, 128):
                total = total + p[:, k : k + 128]
            mixed[part] = mixed[part] + mm(p.astype(BF16), both[c : c + CHUNK, :])

    def folded(m):
        return (m[0][:, :FEAT] + m[0][:, 2 * FEAT : 3 * FEAT]) + (
            m[1][:, FEAT : 2 * FEAT] + m[1][:, 3 * FEAT :]
        )

    inverse = 1.0 / jnp.sum(total, axis=1, keepdims=True)
    value = folded(mixed) * inverse
    out = mm(value, w_v, NT, HIGHEST).astype(BF16)
    out_ref[0] = out
    delta = jnp.sum(cot.astype(F32) * out.astype(F32), axis=1, keepdims=True)

    mixed = [jnp.zeros((count, 4 * FEAT), F32) for _ in range(2)]
    for part in range(2):
        for c in range(0, pairs, CHUNK):
            at = part * pairs + c
            dp = mm(cot, keys[(2 + part) * FEAT : (3 + part) * FEAT, c : c + CHUNK])
            p = probs[:, at : at + CHUNK] * inverse
            ds = p * (dp - delta)
            mixed[part] = mixed[part] + mm(ds.astype(BF16), both[c : c + CHUNK, :])
            both_sides = ds * scores[:, at : at + CHUNK] + p * dp
            csum[:, at : at + CHUNK] += jnp.sum(both_sides.reshape(count // 8, 8, CHUNK), axis=0)
    grad = folded(mixed)
    dq = mm(grad, w_k, NT, HIGHEST) * factor
    q32 = q.astype(F32)
    qsum[...] += jnp.broadcast_to(jnp.sum(dq * q32, axis=1, keepdims=True), qsum.shape)
    own = q_high.astype(F32) + q_low.astype(F32)
    a_q = mm(dq, own, TN, HIGHEST)
    a_k = mm(q_scaled.astype(F32), grad, TN, HIGHEST)
    a_v = mm(cot.astype(F32), value, TN, HIGHEST)
    for t, a in enumerate((a_q, a_k, a_v)):
        for side in range(2):

            @pl.when(odd == side)
            def _():
                at_ref[t * FEAT : (t + 1) * FEAT, side * FEAT : (side + 1) * FEAT] = a

    @pl.when(head == heads - 1)
    def _():
        eye_i = lax.broadcasted_iota(jnp.int32, (2 * FEAT, 2 * FEAT), 0)
        eye_j = lax.broadcasted_iota(jnp.int32, (2 * FEAT, 2 * FEAT), 1)
        eye = (eye_i == eye_j).astype(F32).astype(BF16)
        high = both[:, : 2 * FEAT]
        turned = mm(eye, high, NT)
        c_all = jnp.sum(csum[...], axis=0, keepdims=True)
        weighted = jnp.concatenate(
            [turned[:FEAT] * c_all[:, :pairs], turned[FEAT:] * c_all[:, pairs:]], axis=0
        )
        full = mm(weighted.astype(BF16), high)
        own_part = mm(own * qsum[:, :FEAT], own, TN, HIGHEST)
        b_ref[...] = ((full[:FEAT, :FEAT] + full[FEAT:, FEAT:]) + own_part) * (1.0 / D)


def attention(x, high, low, gram, row, half, cot):
    heads, count, _ = cot.shape
    pairs = x.shape[0]
    whole = lambda *shape: pl.BlockSpec(shape, lambda i: (0,) * len(shape))
    per_head = pl.BlockSpec((1, count, HEAD_DIM), lambda i: (i, 0, 0))
    return pl.pallas_call(
        attention_kernel,
        grid=(heads,),
        in_specs=[
            whole(*x.shape), whole(*high.shape), whole(*low.shape), whole(*gram.shape),
            whole(*row.shape), whole(*half.shape), per_head,
        ],
        out_specs=[per_head, whole(*high.shape), whole(*gram.shape)],
        out_shape=[
            jax.ShapeDtypeStruct(cot.shape, BF16),
            jax.ShapeDtypeStruct(high.shape, F32),
            jax.ShapeDtypeStruct(gram.shape, F32),
        ],
        scratch_shapes=[
            pltpu.VMEM((pairs, 4 * FEAT), BF16),
            pltpu.VMEM((4 * FEAT, pairs), BF16),
            pltpu.VMEM((count, 2 * pairs), F32),
            pltpu.VMEM((count, 2 * pairs), F32),
            pltpu.VMEM((8, 2 * pairs), F32),
            pltpu.VMEM((count, 2 * FEAT), BF16),
            pltpu.VMEM((count, 128), F32),
        ],
        compiler_params=pltpu.CompilerParams(
            dimension_semantics=("arbitrary",), vmem_limit_bytes=48 * 1024 * 1024
        ),
        name="attention",
    )(x, high, low, gram, row, half, cot)


def per_device(
    features, conv_weight, conv_bias, token_order, embed_weight, norm_gain, qkv_weight, grad_out
):
    far = lax.axis_index("seq_0")
    near_count = lax.axis_size("seq_1")
    depth, _, width = qkv_weight.shape
    pair = 2 * HEAD_DIM
    rows = 3 * HEAD_DIM
    rows_each = rows // near_count

    def swapped(array, axis):
        first, second = jnp.split(array, 2, axis=axis)
        mine = jnp.where(far == 0, first, second)
        given = jnp.where(far == 0, second, first)
        return mine, lax.ppermute(given, "seq_0", [(0, 1), (1, 0)])

    def in_order(mine, other):
        return jnp.where(far == 0, jnp.stack([mine, other]), jnp.stack([other, mine]))

    w = qkv_weight.reshape(depth, 3, 2, 2, HEAD_DIM)
    w = jnp.transpose(w, (2, 1, 4, 3, 0)).reshape(2 * near_count, rows_each * 2, depth)
    w_slice = lax.all_to_all(w, SEQ, 0, 0, tiled=True)
    w_slice = jnp.transpose(w_slice, (1, 0, 2)).reshape(rows_each * 2, D)
    embed32 = embed_weight.astype(F32)
    gained = jnp.concatenate(two(embed32 * norm_gain), axis=0)
    m_slice = mm(w_slice, gained, NT)
    m_slice = (m_slice[:, :FEAT] + m_slice[:, FEAT:]).reshape(rows_each, 2 * FEAT)
    gram = lax.dot_general(
        embed_weight, embed_weight, (((1,), (1,)), ((), ())), preferred_element_type=F32
    ) * (1.0 / D)

    patch = encode_tile(features[0, 0], conv_weight, conv_bias)
    token_order, grad_out, patch = lax.optimization_barrier((token_order, grad_out, patch))
    own_rows = patch.shape[0]
    arrived = from_everyone(jnp.concatenate([patch, *two(m_slice)], axis=0), "seq_1")
    every = from_everyone(arrived[:, :own_rows], ("seq_0", *HEAD)).reshape(-1, 2 * FEAT)
    m_high = arrived[:, own_rows : own_rows + rows_each].reshape(rows, 2 * FEAT)
    m_low = arrived[:, own_rows + rows_each :].reshape(rows, 2 * FEAT)

    per_patch_row = own_rows
    head_count = lax.axis_size(HEAD)
    order = in_order(token_order, lax.ppermute(token_order, "seq_0", [(0, 1), (1, 0)]))
    order = order.reshape(-1, 1)
    j = order % (2 * per_patch_row)
    i = (order // (2 * per_patch_row)) % head_count
    f = order // (2 * per_patch_row * head_count)
    plane = (f // near_count) * head_count + i
    row = (plane * near_count + f % near_count) * per_patch_row + j % per_patch_row
    half = j // per_patch_row

    cot = in_order(*swapped(grad_out[0], 1)).reshape(-1, 2, HEAD_DIM)
    out, at, b = attention(
        every, m_high, m_low, gram, row, half, jnp.transpose(cot, (1, 0, 2))
    )
    out = jnp.transpose(out, (1, 0, 2)).reshape(2, -1, pair)
    mine = jnp.where(far == 0, out[0], out[1])
    other = lax.ppermute(jnp.where(far == 0, out[1], out[0]), "seq_0", [(0, 1), (1, 0)])
    attended = jnp.where(
        far == 0,
        jnp.concatenate([mine, other], axis=1),
        jnp.concatenate([other, mine], axis=1),
    )[None]

    at = lax.all_to_all(at.reshape(near_count, rows_each, 2 * FEAT), "seq_1", 0, 0, tiled=True)
    a_slice = jnp.sum(at, axis=0).reshape(rows_each * 2, FEAT)
    a_both = jnp.concatenate(two(a_slice), axis=1)
    t = mm(a_both, w_slice, TN)
    t = t[:FEAT] + t[FEAT:]
    t = t * norm_gain - mm(b, embed32, precision=HIGHEST)
    parts = lax.axis_size(("grp", "seq_0"))
    t = jnp.transpose(t.reshape(parts, FEAT // parts, head_count, -1), (2, 0, 1, 3))
    t = t.astype(BF16).reshape(parts * head_count, FEAT // parts, -1)
    t = lax.all_to_all(t, PLANE, 0, 0, tiled=True)
    t = jnp.sum(t.astype(F32), axis=0).astype(BF16)
    t = jnp.sum(from_everyone(t, "seq_1").astype(F32), axis=0)
    embed_grad = from_everyone(t, ("grp", "seq_0")).reshape(FEAT, -1)
    return (attended, embed_grad)


def solution(mesh):
    torus = Mesh(
        mesh.devices.reshape(mesh.shape["grp"], 2, 16, 4, 2),
        ("grp", "seq_0", "seq_1", "head_0", "head_1"),
    )
    return jax.shard_map(
        per_device,
        mesh=torus,
        in_specs=(
            P("grp", SEQ, HEAD, None, None),
            P(),
            P(),
            P(SEQ),
            P(),
            P(),
            P(SEQ, None, HEAD),
            P("grp", SEQ, HEAD),
        ),
        out_specs=(P("grp", SEQ, HEAD), P(None, HEAD)),
        check_vma=False,
    )
```

```python
import jax
import jax.numpy as jnp
from jax import lax
from jax.experimental import pallas as pl
from jax.experimental.pallas import tpu as pltpu
from jax.sharding import Mesh
from jax.sharding import PartitionSpec as P

D = 3072
HEAD_DIM = 64
FEAT = 64
SEQ = ("seq_0", "seq_1")
HEAD = ("head_0", "head_1")
PLANE = ("head_0", "head_1", "grp", "seq_0")
F32 = jnp.float32
BF16 = jnp.bfloat16
CHUNK = 512
HIGHEST = lax.Precision.HIGHEST


def shifted(value, axis, steps):
    count = lax.axis_size(axis)
    leading, last = (max(0, -steps), min(count, count - steps))
    return lax.ppermute(value, axis, [(source, source + steps) for source in range(leading, last)])


def from_everyone(array, axis):
    copies = jnp.broadcast_to(array, (lax.axis_size(axis), *array.shape))
    return lax.all_to_all(copies, axis, split_axis=0, concat_axis=0, tiled=True)


def two(x):
    high = x.astype(BF16)
    return high, (x - high.astype(F32)).astype(BF16)


def three(x):
    high, rest = x.astype(BF16), None
    rest = x - high.astype(F32)
    mid = rest.astype(BF16)
    return high, mid, (rest - mid.astype(F32)).astype(BF16)


def mm(a, b, dims=((1,), (0,)), precision=None):
    return lax.dot_general(a, b, (dims, ((), ())), preferred_element_type=F32, precision=precision)


NT = ((1,), (1,))
TN = ((0,), (0,))


def conv_kernel(f_ref, w_ref, out_ref):
    tile = f_ref[...]
    spots, channels = tile.shape
    half = spots // 2
    cols = half // 2
    lat = w_ref.shape[0] // 27
    to = lax.broadcasted_iota(jnp.int32, (spots, spots), 0)
    source = (to // cols % 2) * half + (to % cols) * 2 + to // half
    pick = lax.broadcasted_iota(jnp.int32, (spots, spots), 1) == source
    tile = mm(pick.astype(F32).astype(BF16), tile).astype(BF16)
    zero = jnp.zeros((lat, channels), BF16)

    def block(a, taps):
        rows = []
        for b in (2, 1, 0):
            for e in taps:
                at = ((a * 3 + b) * 3 + e) * lat if e is not None else 0
                rows.append(zero if e is None else w_ref[at : at + lat, :])
        return rows + [zero, zero]

    row = lax.broadcasted_iota(jnp.int32, (cols, 128), 0)
    sums = [0.0] * 3
    for parity, here, there, shift in ((0, (1, 0), (None, 2), cols - 1), (1, (2, 1), (0, None), 1)):
        weights = jnp.concatenate(
            [w for taps in (here, there) for a in range(3) for w in block(a, taps)], axis=0
        )
        got = mm(tile[parity * half : (parity + 1) * half], weights, NT)
        edge = cols - 1 if parity == 0 else 0
        for a in range(3):
            near = got[:, a * 128 : (a + 1) * 128]
            far = got[:, (a + 3) * 128 : (a + 4) * 128]
            for r in range(2):
                moved = pltpu.roll(far[r * cols : (r + 1) * cols], shift, 0)
                both = near[r * cols : (r + 1) * cols] + jnp.where(row == edge, 0.0, moved)
                sums[a] = sums[a] + (both if r == 0 else pltpu.roll(both, 32, 1))
    for a in range(3):
        out_ref[a] = sums[a]


def taps(tile, conv_weight):
    rows, columns, channels = tile.shape
    lat = conv_weight.shape[-1]
    weight = jnp.moveaxis(conv_weight, 4, 3).reshape(27 * lat, channels)
    return pl.pallas_call(
        conv_kernel,
        out_shape=jax.ShapeDtypeStruct((3, columns // 2, 8 * lat), F32),
        name="taps",
    )(tile.reshape(rows * columns, channels), weight)


def latent_patches(parts, conv_bias):
    lat = conv_bias.shape[0]
    total = (parts[2] + shifted(parts[1], SEQ, 1)) + shifted(parts[0], SEQ, 2)
    above, below = shifted(total, HEAD, 1), shifted(total, HEAD, -1)
    own = total[:, 2 * lat : 6 * lat]
    own = own + jnp.concatenate([above[:, 6 * lat :], below[:, : 2 * lat]], axis=1)
    patch = (own + jnp.tile(conv_bias, 4)).astype(BF16)
    first, second = jnp.split(patch, 2, axis=0)
    return jnp.concatenate([first, second], axis=1)


def attention_kernel(
    x_ref, high_ref, low_ref, gram_ref, row_ref, half_ref, cot_ref,
    out_ref, at_ref, b_ref,
    both, keys, scores, probs, csum, query, qsum,
):
    head = pl.program_id(0)
    heads = pl.num_programs(0)
    pairs = x_ref.shape[0]
    factor = HEAD_DIM**-0.5
    zero = jnp.zeros((FEAT, FEAT), BF16)

    @pl.when(head == 0)
    def _():
        x = x_ref[...]
        pieces = [
            jnp.concatenate(
                [jnp.concatenate([g, zero], axis=1), jnp.concatenate([zero, g], axis=1)], axis=0
            )
            for g in three(gram_ref[...])
        ]
        y = (mm(x, pieces[2]) + mm(x, pieces[1])) + mm(x, pieces[0])
        lane_i = lax.broadcasted_iota(jnp.int32, (2 * FEAT, 2 * FEAT), 0) // FEAT
        lane_j = lax.broadcasted_iota(jnp.int32, (2 * FEAT, 2 * FEAT), 1) // FEAT
        ones = (lane_i == lane_j).astype(F32).astype(BF16)
        z = three(y * x.astype(F32))
        square = (mm(z[2], ones) + mm(z[1], ones)) + mm(z[0], ones)
        normed = x.astype(F32) * lax.rsqrt(jnp.maximum(square, 0.0) + 1e-06)
        high, low = two(normed)
        both[:, : 2 * FEAT] = high
        both[:, 2 * FEAT :] = low
        csum[...] = jnp.zeros_like(csum)
        qsum[...] = jnp.zeros_like(qsum)
        hot = lax.broadcasted_iota(jnp.int32, (row_ref.shape[0], pairs), 1) == row_ref[...]
        got = mm(hot.astype(F32).astype(BF16), both[...])
        second = half_ref[...] == 1
        for k in range(2):
            piece = got[:, 2 * FEAT * k : 2 * FEAT * (k + 1)]
            query[:, FEAT * k : FEAT * (k + 1)] = jnp.where(
                second, piece[:, FEAT:], piece[:, :FEAT]
            ).astype(BF16)

    odd = head % 2

    def weight(t, ref):
        block = ref[t * FEAT : (t + 1) * FEAT, :]
        block = block.astype(F32)
        return jnp.where(odd == 1, block[:, FEAT:], block[:, :FEAT])

    w_high = [weight(t, high_ref) for t in range(3)]
    w_low = [weight(t, low_ref) for t in range(3)]
    w_k, w_v = w_high[1] + w_low[1], w_high[2] + w_low[2]

    def stacked(parts):
        rows = []
        for m in parts:
            rows.append(jnp.concatenate([m, zero], axis=1))
            rows.append(jnp.concatenate([zero, m], axis=1))
        return jnp.concatenate(rows, axis=0)

    main = stacked([w.astype(BF16) for w in w_high[1:]])
    rest = stacked([w.astype(BF16) for w in w_low[1:]])
    keys[...] = (
        mm(jnp.concatenate([main, main], axis=1), both[...], NT)
        + mm(rest, both[:, : 2 * FEAT], NT)
    ).astype(BF16)

    q_high, q_low = query[:, :FEAT], query[:, FEAT:]
    wq_high, wq_low = w_high[0].astype(BF16), w_low[0].astype(BF16)
    q = (mm(q_high, wq_high, NT) + (mm(q_high, wq_low, NT) + mm(q_low, wq_high, NT))).astype(BF16)
    q_scaled = (q.astype(F32) * factor).astype(BF16)
    cot = cot_ref[0]
    count = q.shape[0]

    top = jnp.full((count, 128), -jnp.inf, F32)
    for part in range(2):
        for c in range(0, pairs, CHUNK):
            s = mm(q_scaled, keys[part * FEAT : (part + 1) * FEAT, c : c + CHUNK])
            scores[:, part * pairs + c : part * pairs + c + CHUNK] = s
            for k in range(0, CHUNK, 128):
                top = jnp.maximum(top, s[:, k : k + 128])
    top = jnp.max(top, axis=1, keepdims=True)

    total = jnp.zeros((count, 128), F32)
    mixed = [jnp.zeros((count, 4 * FEAT), F32) for _ in range(2)]
    for part in range(2):
        for c in range(0, pairs, CHUNK):
            at = part * pairs + c
            p = jnp.exp(scores[:, at : at + CHUNK] - top)
            probs[:, at : at + CHUNK] = p
            for k in range(0, CHUNK, 128):
                total = total + p[:, k : k + 128]
            mixed[part] = mixed[part] + mm(p.astype(BF16), both[c : c + CHUNK, :])

    def folded(m):
        return (m[0][:, :FEAT] + m[0][:, 2 * FEAT : 3 * FEAT]) + (
            m[1][:, FEAT : 2 * FEAT] + m[1][:, 3 * FEAT :]
        )

    inverse = 1.0 / jnp.sum(total, axis=1, keepdims=True)
    value = folded(mixed) * inverse
    out = mm(value, w_v, NT, HIGHEST).astype(BF16)
    out_ref[0] = out
    delta = jnp.sum(cot.astype(F32) * out.astype(F32), axis=1, keepdims=True)

    mixed = [jnp.zeros((count, 4 * FEAT), F32) for _ in range(2)]
    for part in range(2):
        for c in range(0, pairs, CHUNK):
            at = part * pairs + c
            dp = mm(cot, keys[(2 + part) * FEAT : (3 + part) * FEAT, c : c + CHUNK])
            p = probs[:, at : at + CHUNK] * inverse
            ds = p * (dp - delta)
            mixed[part] = mixed[part] + mm(ds.astype(BF16), both[c : c + CHUNK, :])
            both_sides = ds * scores[:, at : at + CHUNK] + p * dp
            csum[:, at : at + CHUNK] += jnp.sum(both_sides.reshape(count // 8, 8, CHUNK), axis=0)
    grad = folded(mixed)
    dq = mm(grad, w_k, NT, HIGHEST) * factor
    q32 = q.astype(F32)
    qsum[...] += jnp.broadcast_to(jnp.sum(dq * q32, axis=1, keepdims=True), qsum.shape)
    own = q_high.astype(F32) + q_low.astype(F32)
    a_q = mm(dq, own, TN, HIGHEST)
    a_k = mm(q_scaled.astype(F32), grad, TN, HIGHEST)
    a_v = mm(cot.astype(F32), value, TN, HIGHEST)
    for t, a in enumerate((a_q, a_k, a_v)):
        for side in range(2):

            @pl.when(odd == side)
            def _():
                at_ref[t * FEAT : (t + 1) * FEAT, side * FEAT : (side + 1) * FEAT] = a

    @pl.when(head == heads - 1)
    def _():
        eye_i = lax.broadcasted_iota(jnp.int32, (2 * FEAT, 2 * FEAT), 0)
        eye_j = lax.broadcasted_iota(jnp.int32, (2 * FEAT, 2 * FEAT), 1)
        eye = (eye_i == eye_j).astype(F32).astype(BF16)
        high = both[:, : 2 * FEAT]
        turned = mm(eye, high, NT)
        c_all = jnp.sum(csum[...], axis=0, keepdims=True)
        weighted = jnp.concatenate(
            [turned[:FEAT] * c_all[:, :pairs], turned[FEAT:] * c_all[:, pairs:]], axis=0
        )
        full = mm(weighted.astype(BF16), high)
        own_part = mm(own * qsum[:, :FEAT], own, TN, HIGHEST)
        b_ref[...] = ((full[:FEAT, :FEAT] + full[FEAT:, FEAT:]) + own_part) * (1.0 / D)


def attention(x, high, low, gram, row, half, cot):
    heads, count, _ = cot.shape
    pairs = x.shape[0]
    whole = lambda *shape: pl.BlockSpec(shape, lambda i: (0,) * len(shape))
    per_head = pl.BlockSpec((1, count, HEAD_DIM), lambda i: (i, 0, 0))
    return pl.pallas_call(
        attention_kernel,
        grid=(heads,),
        in_specs=[
            whole(*x.shape), whole(*high.shape), whole(*low.shape), whole(*gram.shape),
            whole(*row.shape), whole(*half.shape), per_head,
        ],
        out_specs=[per_head, whole(*high.shape), whole(*gram.shape)],
        out_shape=[
            jax.ShapeDtypeStruct(cot.shape, BF16),
            jax.ShapeDtypeStruct(high.shape, F32),
            jax.ShapeDtypeStruct(gram.shape, F32),
        ],
        scratch_shapes=[
            pltpu.VMEM((pairs, 4 * FEAT), BF16),
            pltpu.VMEM((4 * FEAT, pairs), BF16),
            pltpu.VMEM((count, 2 * pairs), F32),
            pltpu.VMEM((count, 2 * pairs), F32),
            pltpu.VMEM((8, 2 * pairs), F32),
            pltpu.VMEM((count, 2 * FEAT), BF16),
            pltpu.VMEM((count, 128), F32),
        ],
        compiler_params=pltpu.CompilerParams(
            dimension_semantics=("arbitrary",), vmem_limit_bytes=48 * 1024 * 1024
        ),
        name="attention",
    )(x, high, low, gram, row, half, cot)


def per_device(
    features, conv_weight, conv_bias, token_order, embed_weight, norm_gain, qkv_weight, grad_out
):
    far = lax.axis_index("seq_0")
    near_count = lax.axis_size("seq_1")
    depth, _, width = qkv_weight.shape
    pair = 2 * HEAD_DIM
    rows = 3 * HEAD_DIM
    rows_each = rows // near_count

    def swapped(array, axis):
        first, second = jnp.split(array, 2, axis=axis)
        mine = jnp.where(far == 0, first, second)
        given = jnp.where(far == 0, second, first)
        return mine, lax.ppermute(given, "seq_0", [(0, 1), (1, 0)])

    def in_order(mine, other):
        return jnp.where(far == 0, jnp.stack([mine, other]), jnp.stack([other, mine]))

    w = qkv_weight.reshape(depth, 3, 2, 2, HEAD_DIM)
    w = jnp.transpose(w, (2, 1, 4, 3, 0)).reshape(2 * near_count, rows_each * 2, depth)
    w_slice = lax.all_to_all(w, SEQ, 0, 0, tiled=True)
    parts = taps(features[0, 0], conv_weight)
    parts, w_slice = lax.optimization_barrier((parts, w_slice))
    patch = latent_patches(parts, conv_bias)
    w_slice = jnp.transpose(w_slice, (1, 0, 2)).reshape(rows_each * 2, D)
    embed32 = embed_weight.astype(F32)
    gained = jnp.concatenate(two(embed32 * norm_gain), axis=0)
    m_slice = mm(w_slice, gained, NT)
    m_slice = (m_slice[:, :FEAT] + m_slice[:, FEAT:]).reshape(rows_each, 2 * FEAT)
    gram = lax.dot_general(
        embed_weight, embed_weight, (((1,), (1,)), ((), ())), preferred_element_type=F32
    ) * (1.0 / D)

    token_order, grad_out, patch = lax.optimization_barrier((token_order, grad_out, patch))
    own_rows = patch.shape[0]
    arrived = from_everyone(jnp.concatenate([patch, *two(m_slice)], axis=0), "seq_1")
    every = from_everyone(arrived[:, :own_rows], ("seq_0", *HEAD)).reshape(-1, 2 * FEAT)
    m_high = arrived[:, own_rows : own_rows + rows_each].reshape(rows, 2 * FEAT)
    m_low = arrived[:, own_rows + rows_each :].reshape(rows, 2 * FEAT)

    per_patch_row = own_rows
    head_count = lax.axis_size(HEAD)
    order = in_order(token_order, lax.ppermute(token_order, "seq_0", [(0, 1), (1, 0)]))
    order = order.reshape(-1, 1)
    j = order % (2 * per_patch_row)
    i = (order // (2 * per_patch_row)) % head_count
    f = order // (2 * per_patch_row * head_count)
    plane = (f // near_count) * head_count + i
    row = (plane * near_count + f % near_count) * per_patch_row + j % per_patch_row
    half = j // per_patch_row

    cot = in_order(*swapped(grad_out[0], 1)).reshape(-1, 2, HEAD_DIM)
    out, at, b = attention(
        every, m_high, m_low, gram, row, half, jnp.transpose(cot, (1, 0, 2))
    )
    out = jnp.transpose(out, (1, 0, 2)).reshape(2, -1, pair)
    mine = jnp.where(far == 0, out[0], out[1])
    other = lax.ppermute(jnp.where(far == 0, out[1], out[0]), "seq_0", [(0, 1), (1, 0)])
    attended = jnp.where(
        far == 0,
        jnp.concatenate([mine, other], axis=1),
        jnp.concatenate([other, mine], axis=1),
    )[None]

    at = lax.all_to_all(at.reshape(near_count, rows_each, 2 * FEAT), "seq_1", 0, 0, tiled=True)
    a_slice = jnp.sum(at, axis=0).reshape(rows_each * 2, FEAT)
    a_both = jnp.concatenate(two(a_slice), axis=1)
    t = mm(a_both, w_slice, TN)
    t = t[:FEAT] + t[FEAT:]
    t = t * norm_gain - mm(b, embed32, precision=HIGHEST)
    parts = lax.axis_size(("grp", "seq_0"))
    t = jnp.transpose(t.reshape(parts, FEAT // parts, head_count, -1), (2, 0, 1, 3))
    t = t.astype(BF16).reshape(parts * head_count, FEAT // parts, -1)
    t = lax.all_to_all(t, PLANE, 0, 0, tiled=True)
    t = jnp.sum(t.astype(F32), axis=0).astype(BF16)
    t = jnp.sum(from_everyone(t, "seq_1").astype(F32), axis=0)
    embed_grad = from_everyone(t, ("grp", "seq_0")).reshape(FEAT, -1)
    return (attended, embed_grad)


def solution(mesh):
    torus = Mesh(
        mesh.devices.reshape(mesh.shape["grp"], 2, 16, 4, 2),
        ("grp", "seq_0", "seq_1", "head_0", "head_1"),
    )
    return jax.shard_map(
        per_device,
        mesh=torus,
        in_specs=(
            P("grp", SEQ, HEAD, None, None),
            P(),
            P(),
            P(SEQ),
            P(),
            P(),
            P(SEQ, None, HEAD),
            P("grp", SEQ, HEAD),
        ),
        out_specs=(P("grp", SEQ, HEAD), P(None, HEAD)),
        check_vma=False,
    )
```

```python
import jax
import jax.numpy as jnp
from jax import lax
from jax.experimental import pallas as pl
from jax.experimental.pallas import tpu as pltpu
from jax.sharding import Mesh
from jax.sharding import PartitionSpec as P

D = 3072
HEAD_DIM = 64
FEAT = 64
SEQ = ("seq_0", "seq_1")
HEAD = ("head_0", "head_1")
F32 = jnp.float32
BF16 = jnp.bfloat16
CHUNK = 512
HIGHEST = lax.Precision.HIGHEST


def shifted(value, axis, steps):
    count = lax.axis_size(axis)
    leading, last = (max(0, -steps), min(count, count - steps))
    return lax.ppermute(value, axis, [(source, source + steps) for source in range(leading, last)])


def from_everyone(array, axis):
    copies = jnp.broadcast_to(array, (lax.axis_size(axis), *array.shape))
    return lax.all_to_all(copies, axis, split_axis=0, concat_axis=0, tiled=True)


def two(x):
    high = x.astype(BF16)
    return high, (x - high.astype(F32)).astype(BF16)


def three(x):
    high, rest = x.astype(BF16), None
    rest = x - high.astype(F32)
    mid = rest.astype(BF16)
    return high, mid, (rest - mid.astype(F32)).astype(BF16)


def mm(a, b, dims=((1,), (0,)), precision=None):
    return lax.dot_general(a, b, (dims, ((), ())), preferred_element_type=F32, precision=precision)


NT = ((1,), (1,))
TN = ((0,), (0,))


def conv_kernel(f_ref, w_ref, out_ref):
    tile = f_ref[...]
    spots, channels = tile.shape
    half = spots // 2
    cols = half // 2
    lat = w_ref.shape[0] // 27
    to = lax.broadcasted_iota(jnp.int32, (spots, spots), 0)
    source = (to // cols % 2) * half + (to % cols) * 2 + to // half
    pick = lax.broadcasted_iota(jnp.int32, (spots, spots), 1) == source
    tile = mm(pick.astype(F32).astype(BF16), tile).astype(BF16)
    zero = jnp.zeros((lat, channels), BF16)

    def block(a, taps):
        rows = []
        for b in (2, 1, 0):
            for e in taps:
                at = ((a * 3 + b) * 3 + e) * lat if e is not None else 0
                rows.append(zero if e is None else w_ref[at : at + lat, :])
        return rows + [zero, zero]

    row = lax.broadcasted_iota(jnp.int32, (cols, 128), 0)
    sums = [0.0] * 3
    for parity, here, there, shift in ((0, (1, 0), (None, 2), cols - 1), (1, (2, 1), (0, None), 1)):
        weights = jnp.concatenate(
            [w for taps in (here, there) for a in range(3) for w in block(a, taps)], axis=0
        )
        got = mm(tile[parity * half : (parity + 1) * half], weights, NT)
        edge = cols - 1 if parity == 0 else 0
        for a in range(3):
            near = got[:, a * 128 : (a + 1) * 128]
            far = got[:, (a + 3) * 128 : (a + 4) * 128]
            for r in range(2):
                moved = pltpu.roll(far[r * cols : (r + 1) * cols], shift, 0)
                both = near[r * cols : (r + 1) * cols] + jnp.where(row == edge, 0.0, moved)
                sums[a] = sums[a] + (both if r == 0 else pltpu.roll(both, 32, 1))
    for a in range(3):
        out_ref[a] = sums[a]


def encode_tile(tile, conv_weight, conv_bias):
    rows, columns, channels = tile.shape
    lat = conv_weight.shape[-1]
    weight = jnp.moveaxis(conv_weight, 4, 3).reshape(27 * lat, channels)
    parts = pl.pallas_call(
        conv_kernel,
        out_shape=jax.ShapeDtypeStruct((3, columns // 2, 8 * lat), F32),
        name="taps",
    )(tile.reshape(rows * columns, channels), weight)
    total = (parts[2] + shifted(parts[1], SEQ, 1)) + shifted(parts[0], SEQ, 2)
    above, below = shifted(total, HEAD, 1), shifted(total, HEAD, -1)
    own = total[:, 2 * lat : 6 * lat]
    own = own + jnp.concatenate([above[:, 6 * lat :], below[:, : 2 * lat]], axis=1)
    patch = (own + jnp.tile(conv_bias, 4)).astype(BF16)
    first, second = jnp.split(patch, 2, axis=0)
    return jnp.concatenate([first, second], axis=1)


def attention_kernel(
    x_ref, high_ref, low_ref, gram_ref, row_ref, half_ref, cot_ref,
    out_ref, at_ref, b_ref,
    both, keys, scores, probs, csum, query, qsum,
):
    head = pl.program_id(0)
    heads = pl.num_programs(0)
    pairs = both.shape[0]
    factor = HEAD_DIM**-0.5
    zero = jnp.zeros((FEAT, FEAT), BF16)

    @pl.when(head == 0)
    def _():
        x = x_ref[:, : pairs // x_ref.shape[0], :].reshape(pairs, 2 * FEAT)
        pieces = [
            jnp.concatenate(
                [jnp.concatenate([g, zero], axis=1), jnp.concatenate([zero, g], axis=1)], axis=0
            )
            for g in three(gram_ref[...])
        ]
        y = (mm(x, pieces[2]) + mm(x, pieces[1])) + mm(x, pieces[0])
        lane_i = lax.broadcasted_iota(jnp.int32, (2 * FEAT, 2 * FEAT), 0) // FEAT
        lane_j = lax.broadcasted_iota(jnp.int32, (2 * FEAT, 2 * FEAT), 1) // FEAT
        ones = (lane_i == lane_j).astype(F32).astype(BF16)
        z = three(y * x.astype(F32))
        square = (mm(z[2], ones) + mm(z[1], ones)) + mm(z[0], ones)
        normed = x.astype(F32) * lax.rsqrt(jnp.maximum(square, 0.0) + 1e-06)
        high, low = two(normed)
        both[:, : 2 * FEAT] = high
        both[:, 2 * FEAT :] = low
        csum[...] = jnp.zeros_like(csum)
        qsum[...] = jnp.zeros_like(qsum)
        hot = lax.broadcasted_iota(jnp.int32, (row_ref.shape[0], pairs), 1) == row_ref[...]
        got = mm(hot.astype(F32).astype(BF16), both[...])
        second = half_ref[...] == 1
        for k in range(2):
            piece = got[:, 2 * FEAT * k : 2 * FEAT * (k + 1)]
            query[:, FEAT * k : FEAT * (k + 1)] = jnp.where(
                second, piece[:, FEAT:], piece[:, :FEAT]
            ).astype(BF16)

    odd = head % 2

    def weight(t, ref):
        block = ref[t * FEAT : (t + 1) * FEAT, :]
        block = block.astype(F32)
        return jnp.where(odd == 1, block[:, FEAT:], block[:, :FEAT])

    w_high = [weight(t, high_ref) for t in range(3)]
    w_low = [weight(t, low_ref) for t in range(3)]
    w_k, w_v = w_high[1] + w_low[1], w_high[2] + w_low[2]

    def stacked(parts):
        rows = []
        for m in parts:
            rows.append(jnp.concatenate([m, zero], axis=1))
            rows.append(jnp.concatenate([zero, m], axis=1))
        return jnp.concatenate(rows, axis=0)

    main = stacked([w.astype(BF16) for w in w_high[1:]])
    rest = stacked([w.astype(BF16) for w in w_low[1:]])
    keys[...] = (
        mm(jnp.concatenate([main, main], axis=1), both[...], NT)
        + mm(rest, both[:, : 2 * FEAT], NT)
    ).astype(BF16)

    q_high, q_low = query[:, :FEAT], query[:, FEAT:]
    wq_high, wq_low = w_high[0].astype(BF16), w_low[0].astype(BF16)
    q = (mm(q_high, wq_high, NT) + (mm(q_high, wq_low, NT) + mm(q_low, wq_high, NT))).astype(BF16)
    q_scaled = (q.astype(F32) * factor).astype(BF16)
    cot = cot_ref[0]
    count = q.shape[0]

    top = jnp.full((count, 128), -jnp.inf, F32)
    for part in range(2):
        for c in range(0, pairs, CHUNK):
            s = mm(q_scaled, keys[part * FEAT : (part + 1) * FEAT, c : c + CHUNK])
            scores[:, part * pairs + c : part * pairs + c + CHUNK] = s
            for k in range(0, CHUNK, 128):
                top = jnp.maximum(top, s[:, k : k + 128])
    top = jnp.max(top, axis=1, keepdims=True)

    total = jnp.zeros((count, 128), F32)
    mixed = [jnp.zeros((count, 4 * FEAT), F32) for _ in range(2)]
    for part in range(2):
        for c in range(0, pairs, CHUNK):
            at = part * pairs + c
            p = jnp.exp(scores[:, at : at + CHUNK] - top)
            probs[:, at : at + CHUNK] = p
            for k in range(0, CHUNK, 128):
                total = total + p[:, k : k + 128]
            mixed[part] = mixed[part] + mm(p.astype(BF16), both[c : c + CHUNK, :])

    def folded(m):
        return (m[0][:, :FEAT] + m[0][:, 2 * FEAT : 3 * FEAT]) + (
            m[1][:, FEAT : 2 * FEAT] + m[1][:, 3 * FEAT :]
        )

    inverse = 1.0 / jnp.sum(total, axis=1, keepdims=True)
    value = folded(mixed) * inverse
    out = mm(value, w_v, NT, HIGHEST).astype(BF16)
    out_ref[0] = out
    delta = jnp.sum(cot.astype(F32) * out.astype(F32), axis=1, keepdims=True)

    mixed = [jnp.zeros((count, 4 * FEAT), F32) for _ in range(2)]
    for part in range(2):
        for c in range(0, pairs, CHUNK):
            at = part * pairs + c
            dp = mm(cot, keys[(2 + part) * FEAT : (3 + part) * FEAT, c : c + CHUNK])
            p = probs[:, at : at + CHUNK] * inverse
            ds = p * (dp - delta)
            mixed[part] = mixed[part] + mm(ds.astype(BF16), both[c : c + CHUNK, :])
            both_sides = ds * scores[:, at : at + CHUNK] + p * dp
            csum[:, at : at + CHUNK] += jnp.sum(both_sides.reshape(count // 8, 8, CHUNK), axis=0)
    grad = folded(mixed)
    dq = mm(grad, w_k, NT, HIGHEST) * factor
    q32 = q.astype(F32)
    qsum[...] += jnp.broadcast_to(jnp.sum(dq * q32, axis=1, keepdims=True), qsum.shape)
    own = q_high.astype(F32) + q_low.astype(F32)
    a_q = mm(dq, own, TN, HIGHEST)
    a_k = mm(q_scaled.astype(F32), grad, TN, HIGHEST)
    a_v = mm(cot.astype(F32), value, TN, HIGHEST)
    for t, a in enumerate((a_q, a_k, a_v)):
        for side in range(2):

            @pl.when(odd == side)
            def _():
                at_ref[t * FEAT : (t + 1) * FEAT, side * FEAT : (side + 1) * FEAT] = a

    @pl.when(head == heads - 1)
    def _():
        eye_i = lax.broadcasted_iota(jnp.int32, (2 * FEAT, 2 * FEAT), 0)
        eye_j = lax.broadcasted_iota(jnp.int32, (2 * FEAT, 2 * FEAT), 1)
        eye = (eye_i == eye_j).astype(F32).astype(BF16)
        high = both[:, : 2 * FEAT]
        turned = mm(eye, high, NT)
        c_all = jnp.sum(csum[...], axis=0, keepdims=True)
        weighted = jnp.concatenate(
            [turned[:FEAT] * c_all[:, :pairs], turned[FEAT:] * c_all[:, pairs:]], axis=0
        )
        full = mm(weighted.astype(BF16), high)
        own_part = mm(own * qsum[:, :FEAT], own, TN, HIGHEST)
        b_ref[...] = ((full[:FEAT, :FEAT] + full[FEAT:, FEAT:]) + own_part) * (1.0 / D)


def attention(x, pairs, high, low, gram, row, half, cot):
    heads, count, _ = cot.shape
    whole = lambda *shape: pl.BlockSpec(shape, lambda i: (0,) * len(shape))
    per_head = pl.BlockSpec((1, count, HEAD_DIM), lambda i: (i, 0, 0))
    return pl.pallas_call(
        attention_kernel,
        grid=(heads,),
        in_specs=[
            whole(*x.shape), whole(*high.shape), whole(*low.shape), whole(*gram.shape),
            whole(*row.shape), whole(*half.shape), per_head,
        ],
        out_specs=[per_head, whole(*high.shape), whole(*gram.shape)],
        out_shape=[
            jax.ShapeDtypeStruct(cot.shape, BF16),
            jax.ShapeDtypeStruct(high.shape, F32),
            jax.ShapeDtypeStruct(gram.shape, F32),
        ],
        scratch_shapes=[
            pltpu.VMEM((pairs, 4 * FEAT), BF16),
            pltpu.VMEM((4 * FEAT, pairs), BF16),
            pltpu.VMEM((count, 2 * pairs), F32),
            pltpu.VMEM((count, 2 * pairs), F32),
            pltpu.VMEM((8, 2 * pairs), F32),
            pltpu.VMEM((count, 2 * FEAT), BF16),
            pltpu.VMEM((count, 128), F32),
        ],
        compiler_params=pltpu.CompilerParams(
            dimension_semantics=("arbitrary",), vmem_limit_bytes=48 * 1024 * 1024
        ),
        name="attention",
    )(x, high, low, gram, row, half, cot)


def per_device(
    features, conv_weight, conv_bias, token_order, embed_weight, norm_gain, qkv_weight, grad_out
):
    far = lax.axis_index("seq_0")
    near_count = lax.axis_size("seq_1")
    depth, _, width = qkv_weight.shape
    pair = 2 * HEAD_DIM
    rows = 3 * HEAD_DIM
    rows_each = rows // near_count

    def swapped(array, axis):
        first, second = jnp.split(array, 2, axis=axis)
        mine = jnp.where(far == 0, first, second)
        given = jnp.where(far == 0, second, first)
        return mine, lax.ppermute(given, "seq_0", [(0, 1), (1, 0)])

    def in_order(mine, other):
        return jnp.where(far == 0, jnp.stack([mine, other]), jnp.stack([other, mine]))

    w = qkv_weight.reshape(depth, 3, 2, 2, HEAD_DIM)
    w = jnp.transpose(w, (2, 1, 4, 3, 0)).reshape(2 * near_count, rows_each * 2, depth)
    w_slice = lax.all_to_all(w, SEQ, 0, 0, tiled=True)
    w_blocks = w_slice
    w_slice = jnp.transpose(w_slice, (1, 0, 2)).reshape(rows_each * 2, D)
    embed32 = embed_weight.astype(F32)
    gained = jnp.concatenate(two(embed32 * norm_gain), axis=0)
    m_slice = mm(w_slice, gained, NT)
    m_slice = (m_slice[:, :FEAT] + m_slice[:, FEAT:]).reshape(rows_each, 2 * FEAT)
    columns = lax.axis_index(HEAD) * lax.axis_size(("grp", "seq_0"))
    columns = (columns + lax.axis_index(("grp", "seq_0"))) * depth
    gain_own = lax.dynamic_slice_in_dim(norm_gain, columns, depth, 0)
    embed_own = lax.dynamic_slice_in_dim(embed32, columns, depth, 1)
    b_each = FEAT // 2 // near_count
    b_at = lax.axis_index("seq_1") * b_each
    embed_own = jnp.concatenate(
        [lax.dynamic_slice_in_dim(embed_own, b_at + k, b_each, 0) for k in (0, FEAT // 2)], axis=0
    )
    gram = lax.dot_general(
        embed_weight, embed_weight, (((1,), (1,)), ((), ())), preferred_element_type=F32
    ) * (1.0 / D)

    patch = encode_tile(features[0, 0], conv_weight, conv_bias)
    token_order, grad_out, patch = lax.optimization_barrier((token_order, grad_out, patch))
    own_rows = patch.shape[0]
    arrived = from_everyone(jnp.concatenate([patch, *two(m_slice)], axis=0), "seq_1")
    far_count, head_count = lax.axis_size("seq_0"), lax.axis_size(HEAD)
    plane = far_count * head_count
    mine = w_blocks.reshape(head_count, -1, far_count, rows_each * 2, depth)
    mine = jnp.swapaxes(lax.dynamic_index_in_dim(mine, lax.axis_index("grp"), 1, False), 0, 1)
    mine = mine.reshape(plane, rows_each * 2, depth)
    mine = jnp.pad(mine, ((0, 0), (0, 0), (0, 2 * FEAT - depth)))
    latents = arrived[:, :own_rows].reshape(1, -1, 2 * FEAT)
    pairs_each = latents.shape[1]
    latents = jnp.broadcast_to(latents, (plane, pairs_each, 2 * FEAT))
    every = lax.all_to_all(
        jnp.concatenate([latents, mine], axis=1), ("seq_0", *HEAD), 0, 0, tiled=True
    )
    w_own = every[:, pairs_each:, :depth].reshape(-1, depth)
    m_high = arrived[:, own_rows : own_rows + rows_each].reshape(rows, 2 * FEAT)
    m_low = arrived[:, own_rows + rows_each :].reshape(rows, 2 * FEAT)

    per_patch_row = own_rows
    order = in_order(token_order, lax.ppermute(token_order, "seq_0", [(0, 1), (1, 0)]))
    order = order.reshape(-1, 1)
    j = order % (2 * per_patch_row)
    i = (order // (2 * per_patch_row)) % head_count
    f = order // (2 * per_patch_row * head_count)
    at_plane = (f // near_count) * head_count + i
    row = (at_plane * near_count + f % near_count) * per_patch_row + j % per_patch_row
    half = j // per_patch_row

    cot = in_order(*swapped(grad_out[0], 1)).reshape(-1, 2, HEAD_DIM)
    out, at, b = attention(
        every, plane * pairs_each, m_high, m_low, gram, row, half, jnp.transpose(cot, (1, 0, 2))
    )
    out = jnp.transpose(out, (1, 0, 2)).reshape(2, -1, pair)
    mine = jnp.where(far == 0, out[0], out[1])
    other = lax.ppermute(jnp.where(far == 0, out[1], out[0]), "seq_0", [(0, 1), (1, 0)])
    attended = jnp.where(
        far == 0,
        jnp.concatenate([mine, other], axis=1),
        jnp.concatenate([other, mine], axis=1),
    )[None]

    first, second = jnp.split(b, 2, axis=0)
    b = jnp.concatenate([first, second], axis=1)
    at = jnp.concatenate(
        [
            at.reshape(near_count, rows_each, 2 * FEAT),
            b.reshape(near_count, b_each, 2 * FEAT),
        ],
        axis=1,
    )
    at = jnp.sum(lax.all_to_all(at, "seq_1", 0, 0, tiled=True), axis=0)
    at = from_everyone(at, ("grp", "seq_0", *HEAD))
    at = jnp.sum(at.reshape(-1, plane, *at.shape[1:]), axis=0)
    a_both = jnp.concatenate(two(at[:, :rows_each].reshape(-1, FEAT)), axis=1)
    t = mm(a_both, w_own, TN)
    t = (t[:FEAT] + t[FEAT:]) * gain_own
    b_rows = jnp.sum(at[:, rows_each:], axis=0).reshape(b_each, 2, FEAT)
    t = t - mm(jnp.swapaxes(b_rows, 0, 1).reshape(-1, FEAT), embed_own, TN, HIGHEST)
    parts = FEAT * depth // (D // head_count)
    t = jnp.swapaxes(t.reshape(FEAT // parts, parts, depth), 0, 1).reshape(parts, -1)
    t = jnp.sum(from_everyone(t.astype(BF16), "seq_1").astype(F32), axis=0)
    t = from_everyone(t, ("grp", "seq_0")).reshape(-1, parts, FEAT // parts, depth)
    embed_grad = jnp.transpose(t, (2, 1, 0, 3)).reshape(FEAT, -1)
    return (attended, embed_grad)


def solution(mesh):
    torus = Mesh(
        mesh.devices.reshape(mesh.shape["grp"], 2, 16, 4, 2),
        ("grp", "seq_0", "seq_1", "head_0", "head_1"),
    )
    return jax.shard_map(
        per_device,
        mesh=torus,
        in_specs=(
            P("grp", SEQ, HEAD, None, None),
            P(),
            P(),
            P(SEQ),
            P(),
            P(),
            P(SEQ, None, HEAD),
            P("grp", SEQ, HEAD),
        ),
        out_specs=(P("grp", SEQ, HEAD), P(None, HEAD)),
        check_vma=False,
    )
```

```python
import jax
import jax.numpy as jnp
from jax import lax
from jax.experimental import pallas as pl
from jax.experimental.pallas import tpu as pltpu
from jax.sharding import Mesh
from jax.sharding import PartitionSpec as P

D = 3072
HEAD_DIM = 64
FEAT = 64
SEQ = ("seq_0", "seq_1")
HEAD = ("head_0", "head_1")
F32 = jnp.float32
BF16 = jnp.bfloat16
CHUNK = 512
HIGHEST = lax.Precision.HIGHEST


def shifted(value, axis, steps):
    count = lax.axis_size(axis)
    leading, last = (max(0, -steps), min(count, count - steps))
    return lax.ppermute(value, axis, [(source, source + steps) for source in range(leading, last)])


def from_everyone(array, axis):
    copies = jnp.broadcast_to(array, (lax.axis_size(axis), *array.shape))
    return lax.all_to_all(copies, axis, split_axis=0, concat_axis=0, tiled=True)


def two(x):
    high = x.astype(BF16)
    return high, (x - high.astype(F32)).astype(BF16)


def three(x):
    high, rest = x.astype(BF16), None
    rest = x - high.astype(F32)
    mid = rest.astype(BF16)
    return high, mid, (rest - mid.astype(F32)).astype(BF16)


def mm(a, b, dims=((1,), (0,)), precision=None):
    return lax.dot_general(a, b, (dims, ((), ())), preferred_element_type=F32, precision=precision)


NT = ((1,), (1,))
TN = ((0,), (0,))


def conv_kernel(f_ref, w_ref, out_ref):
    tile = f_ref[...]
    spots, channels = tile.shape
    half = spots // 2
    cols = half // 2
    lat = w_ref.shape[0] // 27
    to = lax.broadcasted_iota(jnp.int32, (spots, spots), 0)
    source = (to // cols % 2) * half + (to % cols) * 2 + to // half
    pick = lax.broadcasted_iota(jnp.int32, (spots, spots), 1) == source
    tile = mm(pick.astype(F32).astype(BF16), tile).astype(BF16)
    zero = jnp.zeros((lat, channels), BF16)

    def block(a, taps):
        rows = []
        for b in (2, 1, 0):
            for e in taps:
                at = ((a * 3 + b) * 3 + e) * lat if e is not None else 0
                rows.append(zero if e is None else w_ref[at : at + lat, :])
        return rows + [zero, zero]

    row = lax.broadcasted_iota(jnp.int32, (cols, 128), 0)
    sums = [0.0] * 3
    for parity, here, there, shift in ((0, (1, 0), (None, 2), cols - 1), (1, (2, 1), (0, None), 1)):
        weights = jnp.concatenate(
            [w for taps in (here, there) for a in range(3) for w in block(a, taps)], axis=0
        )
        got = mm(tile[parity * half : (parity + 1) * half], weights, NT)
        edge = cols - 1 if parity == 0 else 0
        for a in range(3):
            near = got[:, a * 128 : (a + 1) * 128]
            far = got[:, (a + 3) * 128 : (a + 4) * 128]
            for r in range(2):
                moved = pltpu.roll(far[r * cols : (r + 1) * cols], shift, 0)
                both = near[r * cols : (r + 1) * cols] + jnp.where(row == edge, 0.0, moved)
                sums[a] = sums[a] + (both if r == 0 else pltpu.roll(both, 32, 1))
    for a in range(3):
        out_ref[a] = sums[a]


def encode_tile(tile, conv_weight, conv_bias):
    rows, columns, channels = tile.shape
    lat = conv_weight.shape[-1]
    weight = jnp.moveaxis(conv_weight, 4, 3).reshape(27 * lat, channels)
    parts = pl.pallas_call(
        conv_kernel,
        out_shape=jax.ShapeDtypeStruct((3, columns // 2, 8 * lat), F32),
        name="taps",
    )(tile.reshape(rows * columns, channels), weight)
    total = (parts[2] + shifted(parts[1], SEQ, 1)) + shifted(parts[0], SEQ, 2)
    above, below = shifted(total, HEAD, 1), shifted(total, HEAD, -1)
    own = total[:, 2 * lat : 6 * lat]
    own = own + jnp.concatenate([above[:, 6 * lat :], below[:, : 2 * lat]], axis=1)
    patch = (own + jnp.tile(conv_bias, 4)).astype(BF16)
    first, second = jnp.split(patch, 2, axis=0)
    return jnp.concatenate([first, second], axis=1)


def attention_kernel(
    x_ref, high_ref, low_ref, gram_ref, row_ref, half_ref, cot_ref,
    out_ref, at_ref, b_ref,
    both, keys, scores, probs, csum, query, qsum,
):
    head = pl.program_id(0)
    heads = pl.num_programs(0)
    pairs = both.shape[0]
    factor = HEAD_DIM**-0.5
    zero = jnp.zeros((FEAT, FEAT), BF16)

    @pl.when(head == 0)
    def _():
        x = x_ref[:, : pairs // x_ref.shape[0], :].reshape(pairs, 2 * FEAT)
        pieces = [
            jnp.concatenate(
                [jnp.concatenate([g, zero], axis=1), jnp.concatenate([zero, g], axis=1)], axis=0
            )
            for g in three(gram_ref[...])
        ]
        y = (mm(x, pieces[2]) + mm(x, pieces[1])) + mm(x, pieces[0])
        lane_i = lax.broadcasted_iota(jnp.int32, (2 * FEAT, 2 * FEAT), 0) // FEAT
        lane_j = lax.broadcasted_iota(jnp.int32, (2 * FEAT, 2 * FEAT), 1) // FEAT
        ones = (lane_i == lane_j).astype(F32).astype(BF16)
        z = three(y * x.astype(F32))
        square = (mm(z[2], ones) + mm(z[1], ones)) + mm(z[0], ones)
        normed = x.astype(F32) * lax.rsqrt(jnp.maximum(square, 0.0) + 1e-06)
        high, low = two(normed)
        both[:, : 2 * FEAT] = high
        both[:, 2 * FEAT :] = low
        csum[...] = jnp.zeros_like(csum)
        qsum[...] = jnp.zeros_like(qsum)
        hot = lax.broadcasted_iota(jnp.int32, (row_ref.shape[0], pairs), 1) == row_ref[...]
        got = mm(hot.astype(F32).astype(BF16), both[...])
        second = half_ref[...] == 1
        for k in range(2):
            piece = got[:, 2 * FEAT * k : 2 * FEAT * (k + 1)]
            query[:, FEAT * k : FEAT * (k + 1)] = jnp.where(
                second, piece[:, FEAT:], piece[:, :FEAT]
            ).astype(BF16)

    odd = head % 2

    def weight(t, ref):
        block = ref[t * FEAT : (t + 1) * FEAT, :]
        block = block.astype(F32)
        return jnp.where(odd == 1, block[:, FEAT:], block[:, :FEAT])

    w_high = [weight(t, high_ref) for t in range(3)]
    w_low = [weight(t, low_ref) for t in range(3)]
    w_k, w_v = w_high[1] + w_low[1], w_high[2] + w_low[2]

    def stacked(parts):
        rows = []
        for m in parts:
            rows.append(jnp.concatenate([m, zero], axis=1))
            rows.append(jnp.concatenate([zero, m], axis=1))
        return jnp.concatenate(rows, axis=0)

    main = stacked([w.astype(BF16) for w in w_high[1:]])
    rest = stacked([w.astype(BF16) for w in w_low[1:]])
    keys[...] = (
        mm(jnp.concatenate([main, main], axis=1), both[...], NT)
        + mm(rest, both[:, : 2 * FEAT], NT)
    ).astype(BF16)

    q_high, q_low = query[:, :FEAT], query[:, FEAT:]
    wq_high, wq_low = w_high[0].astype(BF16), w_low[0].astype(BF16)
    q = (mm(q_high, wq_high, NT) + (mm(q_high, wq_low, NT) + mm(q_low, wq_high, NT))).astype(BF16)
    q_scaled = (q.astype(F32) * factor).astype(BF16)
    cot = cot_ref[0]
    count = q.shape[0]

    top = jnp.full((count, 128), -jnp.inf, F32)
    for part in range(2):
        for c in range(0, pairs, CHUNK):
            s = mm(q_scaled, keys[part * FEAT : (part + 1) * FEAT, c : c + CHUNK])
            scores[:, part * pairs + c : part * pairs + c + CHUNK] = s
            for k in range(0, CHUNK, 128):
                top = jnp.maximum(top, s[:, k : k + 128])
    top = jnp.max(top, axis=1, keepdims=True)

    total = jnp.zeros((count, 128), F32)
    mixed = [jnp.zeros((count, 4 * FEAT), F32) for _ in range(2)]
    for part in range(2):
        for c in range(0, pairs, CHUNK):
            at = part * pairs + c
            p = jnp.exp(scores[:, at : at + CHUNK] - top)
            probs[:, at : at + CHUNK] = p
            for k in range(0, CHUNK, 128):
                total = total + p[:, k : k + 128]
            mixed[part] = mixed[part] + mm(p.astype(BF16), both[c : c + CHUNK, :])

    def folded(m):
        return (m[0][:, :FEAT] + m[0][:, 2 * FEAT : 3 * FEAT]) + (
            m[1][:, FEAT : 2 * FEAT] + m[1][:, 3 * FEAT :]
        )

    inverse = 1.0 / jnp.sum(total, axis=1, keepdims=True)
    value = folded(mixed) * inverse
    out = mm(value, w_v, NT, HIGHEST).astype(BF16)
    out_ref[0] = out
    delta = jnp.sum(cot.astype(F32) * out.astype(F32), axis=1, keepdims=True)

    mixed = [jnp.zeros((count, 4 * FEAT), F32) for _ in range(2)]
    for part in range(2):
        for c in range(0, pairs, CHUNK):
            at = part * pairs + c
            dp = mm(cot, keys[(2 + part) * FEAT : (3 + part) * FEAT, c : c + CHUNK])
            p = probs[:, at : at + CHUNK] * inverse
            ds = p * (dp - delta)
            mixed[part] = mixed[part] + mm(ds.astype(BF16), both[c : c + CHUNK, :])
            both_sides = ds * scores[:, at : at + CHUNK] + p * dp
            csum[:, at : at + CHUNK] += jnp.sum(both_sides.reshape(count // 8, 8, CHUNK), axis=0)
    grad = folded(mixed)
    dq = mm(grad, w_k, NT, HIGHEST) * factor
    q32 = q.astype(F32)
    qsum[...] += jnp.broadcast_to(jnp.sum(dq * q32, axis=1, keepdims=True), qsum.shape)
    own = q_high.astype(F32) + q_low.astype(F32)
    a_q = mm(dq, own, TN, HIGHEST)
    a_k = mm(q_scaled.astype(F32), grad, TN, HIGHEST)
    a_v = mm(cot.astype(F32), value, TN, HIGHEST)
    for t, a in enumerate((a_q, a_k, a_v)):
        for side in range(2):

            @pl.when(odd == side)
            def _():
                at_ref[t * FEAT : (t + 1) * FEAT, side * FEAT : (side + 1) * FEAT] = a

    @pl.when(head == heads - 1)
    def _():
        eye_i = lax.broadcasted_iota(jnp.int32, (2 * FEAT, 2 * FEAT), 0)
        eye_j = lax.broadcasted_iota(jnp.int32, (2 * FEAT, 2 * FEAT), 1)
        eye = (eye_i == eye_j).astype(F32).astype(BF16)
        high = both[:, : 2 * FEAT]
        turned = mm(eye, high, NT)
        c_all = jnp.sum(csum[...], axis=0, keepdims=True)
        weighted = jnp.concatenate(
            [turned[:FEAT] * c_all[:, :pairs], turned[FEAT:] * c_all[:, pairs:]], axis=0
        )
        full = mm(weighted.astype(BF16), high)
        own_part = mm(own * qsum[:, :FEAT], own, TN, HIGHEST)
        b_ref[...] = ((full[:FEAT, :FEAT] + full[FEAT:, FEAT:]) + own_part) * (1.0 / D)


def attention(x, pairs, high, low, gram, row, half, cot):
    heads, count, _ = cot.shape
    whole = lambda *shape: pl.BlockSpec(shape, lambda i: (0,) * len(shape))
    per_head = pl.BlockSpec((1, count, HEAD_DIM), lambda i: (i, 0, 0))
    return pl.pallas_call(
        attention_kernel,
        grid=(heads,),
        in_specs=[
            whole(*x.shape), whole(*high.shape), whole(*low.shape), whole(*gram.shape),
            whole(*row.shape), whole(*half.shape), per_head,
        ],
        out_specs=[per_head, whole(*high.shape), whole(*gram.shape)],
        out_shape=[
            jax.ShapeDtypeStruct(cot.shape, BF16),
            jax.ShapeDtypeStruct(high.shape, F32),
            jax.ShapeDtypeStruct(gram.shape, F32),
        ],
        scratch_shapes=[
            pltpu.VMEM((pairs, 4 * FEAT), BF16),
            pltpu.VMEM((4 * FEAT, pairs), BF16),
            pltpu.VMEM((count, 2 * pairs), F32),
            pltpu.VMEM((count, 2 * pairs), F32),
            pltpu.VMEM((8, 2 * pairs), F32),
            pltpu.VMEM((count, 2 * FEAT), BF16),
            pltpu.VMEM((count, 128), F32),
        ],
        compiler_params=pltpu.CompilerParams(
            dimension_semantics=("arbitrary",), vmem_limit_bytes=48 * 1024 * 1024
        ),
        name="attention",
    )(x, high, low, gram, row, half, cot)


def per_device(
    features, conv_weight, conv_bias, token_order, embed_weight, norm_gain, qkv_weight, grad_out
):
    far = lax.axis_index("seq_0")
    near_count = lax.axis_size("seq_1")
    depth, _, width = qkv_weight.shape
    pair = 2 * HEAD_DIM
    rows = 3 * HEAD_DIM
    rows_each = rows // near_count

    def swapped(array, axis):
        first, second = jnp.split(array, 2, axis=axis)
        mine = jnp.where(far == 0, first, second)
        given = jnp.where(far == 0, second, first)
        return mine, lax.ppermute(given, "seq_0", [(0, 1), (1, 0)])

    def in_order(mine, other):
        return jnp.where(far == 0, jnp.stack([mine, other]), jnp.stack([other, mine]))

    clip = lax.axis_index("grp")
    half_rows = rows_each // 2

    def both_halves(mine, given, axis):
        other = lax.ppermute(given, "grp", [(0, 1), (1, 0)])
        return jnp.where(
            clip == 0, jnp.stack([mine, other], axis), jnp.stack([other, mine], axis)
        )

    w = qkv_weight.reshape(depth, 3, 2, 2, HEAD_DIM)
    w = jnp.transpose(w, (2, 1, 4, 3, 0)).reshape(2 * near_count, 2, rows_each, depth)
    w = jnp.where(clip == 0, w[:, 0], w[:, 1])
    w_blocks = lax.all_to_all(w, SEQ, 0, 0, tiled=True)
    w_slice = jnp.transpose(w_blocks, (1, 0, 2)).reshape(rows_each, D)
    embed32 = embed_weight.astype(F32)
    gained = jnp.concatenate(two(embed32 * norm_gain), axis=0)
    m_slice = mm(w_slice, gained, NT)
    m_slice = (m_slice[:, :FEAT] + m_slice[:, FEAT:]).reshape(half_rows, 2 * FEAT)
    columns = lax.axis_index(HEAD) * lax.axis_size(("grp", "seq_0"))
    columns = (columns + lax.axis_index(("grp", "seq_0"))) * depth
    gain_own = lax.dynamic_slice_in_dim(norm_gain, columns, depth, 0)
    embed_own = lax.dynamic_slice_in_dim(embed32, columns, depth, 1)
    b_each = FEAT // 2 // near_count
    b_at = lax.axis_index("seq_1") * b_each
    embed_own = jnp.concatenate(
        [lax.dynamic_slice_in_dim(embed_own, b_at + k, b_each, 0) for k in (0, FEAT // 2)], axis=0
    )
    gram = lax.dot_general(
        embed_weight, embed_weight, (((1,), (1,)), ((), ())), preferred_element_type=F32
    ) * (1.0 / D)

    patch = encode_tile(features[0, 0], conv_weight, conv_bias)
    token_order, grad_out, patch = lax.optimization_barrier((token_order, grad_out, patch))
    own_rows = patch.shape[0]
    arrived = from_everyone(jnp.concatenate([patch, *two(m_slice)], axis=0), "seq_1")
    far_count, head_count = lax.axis_size("seq_0"), lax.axis_size(HEAD)
    plane = far_count * head_count
    mine = w_blocks.reshape(head_count, -1, far_count, rows_each, depth)
    mine = both_halves(
        lax.dynamic_index_in_dim(mine, clip, 1, False),
        lax.dynamic_index_in_dim(mine, 1 - clip, 1, False),
        2,
    )
    mine = jnp.swapaxes(mine, 0, 1)
    mine = mine.reshape(plane, rows_each * 2, depth)
    mine = jnp.pad(mine, ((0, 0), (0, 0), (0, 2 * FEAT - depth)))
    latents = arrived[:, :own_rows].reshape(1, -1, 2 * FEAT)
    pairs_each = latents.shape[1]
    latents = jnp.broadcast_to(latents, (plane, pairs_each, 2 * FEAT))
    every = lax.all_to_all(
        jnp.concatenate([latents, mine], axis=1), ("seq_0", *HEAD), 0, 0, tiled=True
    )
    w_own = every[:, pairs_each:, :depth].reshape(-1, depth)
    m_half = arrived[:, own_rows:]
    m_both = both_halves(m_half, m_half, 1).reshape(near_count, 2, 2, half_rows, 2 * FEAT)
    m_high = m_both[:, :, 0].reshape(rows, 2 * FEAT)
    m_low = m_both[:, :, 1].reshape(rows, 2 * FEAT)

    per_patch_row = own_rows
    order = in_order(token_order, lax.ppermute(token_order, "seq_0", [(0, 1), (1, 0)]))
    order = order.reshape(-1, 1)
    j = order % (2 * per_patch_row)
    i = (order // (2 * per_patch_row)) % head_count
    f = order // (2 * per_patch_row * head_count)
    at_plane = (f // near_count) * head_count + i
    row = (at_plane * near_count + f % near_count) * per_patch_row + j % per_patch_row
    half = j // per_patch_row

    cot = in_order(*swapped(grad_out[0], 1)).reshape(-1, 2, HEAD_DIM)
    out, at, b = attention(
        every, plane * pairs_each, m_high, m_low, gram, row, half, jnp.transpose(cot, (1, 0, 2))
    )
    out = jnp.transpose(out, (1, 0, 2)).reshape(2, -1, pair)
    mine = jnp.where(far == 0, out[0], out[1])
    other = lax.ppermute(jnp.where(far == 0, out[1], out[0]), "seq_0", [(0, 1), (1, 0)])
    attended = jnp.where(
        far == 0,
        jnp.concatenate([mine, other], axis=1),
        jnp.concatenate([other, mine], axis=1),
    )[None]

    first, second = jnp.split(b, 2, axis=0)
    b = jnp.concatenate([first, second], axis=1)
    at = jnp.concatenate(
        [
            at.reshape(near_count, rows_each, 2 * FEAT),
            b.reshape(near_count, b_each, 2 * FEAT),
        ],
        axis=1,
    )
    at = jnp.sum(lax.all_to_all(at, "seq_1", 0, 0, tiled=True), axis=0)
    at = from_everyone(at, ("grp", "seq_0", *HEAD))
    at = jnp.sum(at.reshape(-1, plane, *at.shape[1:]), axis=0)
    a_both = jnp.concatenate(two(at[:, :rows_each].reshape(-1, FEAT)), axis=1)
    t = mm(a_both, w_own, TN)
    t = (t[:FEAT] + t[FEAT:]) * gain_own
    b_rows = jnp.sum(at[:, rows_each:], axis=0).reshape(b_each, 2, FEAT)
    t = t - mm(jnp.swapaxes(b_rows, 0, 1).reshape(-1, FEAT), embed_own, TN, HIGHEST)
    parts = FEAT * depth // (D // head_count)
    t = jnp.swapaxes(t.reshape(FEAT // parts, parts, depth), 0, 1).reshape(parts, -1)
    t = jnp.sum(from_everyone(t.astype(BF16), "seq_1").astype(F32), axis=0)
    t = from_everyone(t, ("grp", "seq_0")).reshape(-1, parts, FEAT // parts, depth)
    embed_grad = jnp.transpose(t, (2, 1, 0, 3)).reshape(FEAT, -1)
    return (attended, embed_grad)


def solution(mesh):
    torus = Mesh(
        mesh.devices.reshape(mesh.shape["grp"], 2, 16, 4, 2),
        ("grp", "seq_0", "seq_1", "head_0", "head_1"),
    )
    return jax.shard_map(
        per_device,
        mesh=torus,
        in_specs=(
            P("grp", SEQ, HEAD, None, None),
            P(),
            P(),
            P(SEQ),
            P(),
            P(),
            P(SEQ, None, HEAD),
            P("grp", SEQ, HEAD),
        ),
        out_specs=(P("grp", SEQ, HEAD), P(None, HEAD)),
        check_vma=False,
    )
```

```python
import jax
import jax.numpy as jnp
from jax import lax
from jax.experimental import pallas as pl
from jax.experimental.pallas import tpu as pltpu
from jax.sharding import Mesh
from jax.sharding import PartitionSpec as P

D = 3072
HEAD_DIM = 64
FEAT = 64
SEQ = ("seq_0", "seq_1")
HEAD = ("head_0", "head_1")
F32 = jnp.float32
BF16 = jnp.bfloat16
CHUNK = 512
HIGHEST = lax.Precision.HIGHEST


def shifted(value, axis, steps):
    count = lax.axis_size(axis)
    leading, last = (max(0, -steps), min(count, count - steps))
    return lax.ppermute(value, axis, [(source, source + steps) for source in range(leading, last)])


def from_everyone(array, axis):
    copies = jnp.broadcast_to(array, (lax.axis_size(axis), *array.shape))
    return lax.all_to_all(copies, axis, split_axis=0, concat_axis=0, tiled=True)


def two(x):
    high = x.astype(BF16)
    return high, (x - high.astype(F32)).astype(BF16)


def three(x):
    high, rest = x.astype(BF16), None
    rest = x - high.astype(F32)
    mid = rest.astype(BF16)
    return high, mid, (rest - mid.astype(F32)).astype(BF16)


def mm(a, b, dims=((1,), (0,)), precision=None):
    return lax.dot_general(a, b, (dims, ((), ())), preferred_element_type=F32, precision=precision)


NT = ((1,), (1,))
TN = ((0,), (0,))


def conv_kernel(f_ref, w_ref, out_ref):
    tile = f_ref[...]
    spots, channels = tile.shape
    half = spots // 2
    cols = half // 2
    lat = w_ref.shape[0] // 27
    to = lax.broadcasted_iota(jnp.int32, (spots, spots), 0)
    source = (to // cols % 2) * half + (to % cols) * 2 + to // half
    pick = lax.broadcasted_iota(jnp.int32, (spots, spots), 1) == source
    tile = mm(pick.astype(F32).astype(BF16), tile).astype(BF16)
    zero = jnp.zeros((lat, channels), BF16)

    def block(a, taps):
        rows = []
        for b in (2, 1, 0):
            for e in taps:
                at = ((a * 3 + b) * 3 + e) * lat if e is not None else 0
                rows.append(zero if e is None else w_ref[at : at + lat, :])
        return rows + [zero, zero]

    row = lax.broadcasted_iota(jnp.int32, (cols, 128), 0)
    sums = [0.0] * 3
    for parity, here, there, shift in ((0, (1, 0), (None, 2), cols - 1), (1, (2, 1), (0, None), 1)):
        weights = jnp.concatenate(
            [w for taps in (here, there) for a in range(3) for w in block(a, taps)], axis=0
        )
        got = mm(tile[parity * half : (parity + 1) * half], weights, NT)
        edge = cols - 1 if parity == 0 else 0
        for a in range(3):
            near = got[:, a * 128 : (a + 1) * 128]
            far = got[:, (a + 3) * 128 : (a + 4) * 128]
            for r in range(2):
                moved = pltpu.roll(far[r * cols : (r + 1) * cols], shift, 0)
                both = near[r * cols : (r + 1) * cols] + jnp.where(row == edge, 0.0, moved)
                sums[a] = sums[a] + (both if r == 0 else pltpu.roll(both, 32, 1))
    for a in range(3):
        out_ref[a] = sums[a]


def taps(tile, conv_weight):
    rows, columns, channels = tile.shape
    lat = conv_weight.shape[-1]
    weight = jnp.moveaxis(conv_weight, 4, 3).reshape(27 * lat, channels)
    parts = pl.pallas_call(
        conv_kernel,
        out_shape=jax.ShapeDtypeStruct((3, columns // 2, 8 * lat), F32),
        name="taps",
    )(tile.reshape(rows * columns, channels), weight)
    return parts


def latent_patches(parts, conv_bias):
    lat = conv_bias.shape[0]
    total = (parts[2] + shifted(parts[1], SEQ, 1)) + shifted(parts[0], SEQ, 2)
    above, below = shifted(total, HEAD, 1), shifted(total, HEAD, -1)
    own = total[:, 2 * lat : 6 * lat]
    own = own + jnp.concatenate([above[:, 6 * lat :], below[:, : 2 * lat]], axis=1)
    patch = (own + jnp.tile(conv_bias, 4)).astype(BF16)
    first, second = jnp.split(patch, 2, axis=0)
    return jnp.concatenate([first, second], axis=1)


def attention_kernel(
    x_ref, high_ref, low_ref, gram_ref, row_ref, half_ref, cot_ref,
    out_ref, at_ref, b_ref,
    both, keys, scores, probs, csum, query, qsum,
):
    head = pl.program_id(0)
    heads = pl.num_programs(0)
    pairs = both.shape[0]
    factor = HEAD_DIM**-0.5
    zero = jnp.zeros((FEAT, FEAT), BF16)

    @pl.when(head == 0)
    def _():
        x = x_ref[:, : pairs // x_ref.shape[0], :].reshape(pairs, 2 * FEAT)
        pieces = [
            jnp.concatenate(
                [jnp.concatenate([g, zero], axis=1), jnp.concatenate([zero, g], axis=1)], axis=0
            )
            for g in three(gram_ref[...])
        ]
        y = (mm(x, pieces[2]) + mm(x, pieces[1])) + mm(x, pieces[0])
        lane_i = lax.broadcasted_iota(jnp.int32, (2 * FEAT, 2 * FEAT), 0) // FEAT
        lane_j = lax.broadcasted_iota(jnp.int32, (2 * FEAT, 2 * FEAT), 1) // FEAT
        ones = (lane_i == lane_j).astype(F32).astype(BF16)
        z = three(y * x.astype(F32))
        square = (mm(z[2], ones) + mm(z[1], ones)) + mm(z[0], ones)
        normed = x.astype(F32) * lax.rsqrt(jnp.maximum(square, 0.0) + 1e-06)
        high, low = two(normed)
        both[:, : 2 * FEAT] = high
        both[:, 2 * FEAT :] = low
        csum[...] = jnp.zeros_like(csum)
        qsum[...] = jnp.zeros_like(qsum)
        hot = lax.broadcasted_iota(jnp.int32, (row_ref.shape[0], pairs), 1) == row_ref[...]
        got = mm(hot.astype(F32).astype(BF16), both[...])
        second = half_ref[...] == 1
        for k in range(2):
            piece = got[:, 2 * FEAT * k : 2 * FEAT * (k + 1)]
            query[:, FEAT * k : FEAT * (k + 1)] = jnp.where(
                second, piece[:, FEAT:], piece[:, :FEAT]
            ).astype(BF16)

    odd = head % 2

    def weight(t, ref):
        block = ref[t * FEAT : (t + 1) * FEAT, :]
        block = block.astype(F32)
        return jnp.where(odd == 1, block[:, FEAT:], block[:, :FEAT])

    w_high = [weight(t, high_ref) for t in range(3)]
    w_low = [weight(t, low_ref) for t in range(3)]
    w_k, w_v = w_high[1] + w_low[1], w_high[2] + w_low[2]

    def stacked(parts):
        rows = []
        for m in parts:
            rows.append(jnp.concatenate([m, zero], axis=1))
            rows.append(jnp.concatenate([zero, m], axis=1))
        return jnp.concatenate(rows, axis=0)

    main = stacked([w.astype(BF16) for w in w_high[1:]])
    rest = stacked([w.astype(BF16) for w in w_low[1:]])
    keys[...] = (
        mm(jnp.concatenate([main, main], axis=1), both[...], NT)
        + mm(rest, both[:, : 2 * FEAT], NT)
    ).astype(BF16)

    q_high, q_low = query[:, :FEAT], query[:, FEAT:]
    wq_high, wq_low = w_high[0].astype(BF16), w_low[0].astype(BF16)
    q = (mm(q_high, wq_high, NT) + (mm(q_high, wq_low, NT) + mm(q_low, wq_high, NT))).astype(BF16)
    q_scaled = (q.astype(F32) * factor).astype(BF16)
    cot = cot_ref[0]
    count = q.shape[0]

    top = jnp.full((count, 128), -jnp.inf, F32)
    for part in range(2):
        for c in range(0, pairs, CHUNK):
            s = mm(q_scaled, keys[part * FEAT : (part + 1) * FEAT, c : c + CHUNK])
            scores[:, part * pairs + c : part * pairs + c + CHUNK] = s
            for k in range(0, CHUNK, 128):
                top = jnp.maximum(top, s[:, k : k + 128])
    top = jnp.max(top, axis=1, keepdims=True)

    total = jnp.zeros((count, 128), F32)
    mixed = [jnp.zeros((count, 4 * FEAT), F32) for _ in range(2)]
    for part in range(2):
        for c in range(0, pairs, CHUNK):
            at = part * pairs + c
            p = jnp.exp(scores[:, at : at + CHUNK] - top)
            probs[:, at : at + CHUNK] = p
            for k in range(0, CHUNK, 128):
                total = total + p[:, k : k + 128]
            mixed[part] = mixed[part] + mm(p.astype(BF16), both[c : c + CHUNK, :])

    def folded(m):
        return (m[0][:, :FEAT] + m[0][:, 2 * FEAT : 3 * FEAT]) + (
            m[1][:, FEAT : 2 * FEAT] + m[1][:, 3 * FEAT :]
        )

    inverse = 1.0 / jnp.sum(total, axis=1, keepdims=True)
    value = folded(mixed) * inverse
    out = mm(value, w_v, NT, HIGHEST).astype(BF16)
    out_ref[0] = out
    delta = jnp.sum(cot.astype(F32) * out.astype(F32), axis=1, keepdims=True)

    mixed = [jnp.zeros((count, 4 * FEAT), F32) for _ in range(2)]
    for part in range(2):
        for c in range(0, pairs, CHUNK):
            at = part * pairs + c
            dp = mm(cot, keys[(2 + part) * FEAT : (3 + part) * FEAT, c : c + CHUNK])
            p = probs[:, at : at + CHUNK] * inverse
            ds = p * (dp - delta)
            mixed[part] = mixed[part] + mm(ds.astype(BF16), both[c : c + CHUNK, :])
            both_sides = ds * scores[:, at : at + CHUNK] + p * dp
            csum[:, at : at + CHUNK] += jnp.sum(both_sides.reshape(count // 8, 8, CHUNK), axis=0)
    grad = folded(mixed)
    dq = mm(grad, w_k, NT, HIGHEST) * factor
    q32 = q.astype(F32)
    qsum[...] += jnp.broadcast_to(jnp.sum(dq * q32, axis=1, keepdims=True), qsum.shape)
    own = q_high.astype(F32) + q_low.astype(F32)
    a_q = mm(dq, own, TN, HIGHEST)
    a_k = mm(q_scaled.astype(F32), grad, TN, HIGHEST)
    a_v = mm(cot.astype(F32), value, TN, HIGHEST)
    for t, a in enumerate((a_q, a_k, a_v)):
        for side in range(2):

            @pl.when(odd == side)
            def _():
                at_ref[t * FEAT : (t + 1) * FEAT, side * FEAT : (side + 1) * FEAT] = a

    @pl.when(head == heads - 1)
    def _():
        eye_i = lax.broadcasted_iota(jnp.int32, (2 * FEAT, 2 * FEAT), 0)
        eye_j = lax.broadcasted_iota(jnp.int32, (2 * FEAT, 2 * FEAT), 1)
        eye = (eye_i == eye_j).astype(F32).astype(BF16)
        high = both[:, : 2 * FEAT]
        turned = mm(eye, high, NT)
        c_all = jnp.sum(csum[...], axis=0, keepdims=True)
        weighted = jnp.concatenate(
            [turned[:FEAT] * c_all[:, :pairs], turned[FEAT:] * c_all[:, pairs:]], axis=0
        )
        full = mm(weighted.astype(BF16), high)
        own_part = mm(own * qsum[:, :FEAT], own, TN, HIGHEST)
        b_ref[...] = ((full[:FEAT, :FEAT] + full[FEAT:, FEAT:]) + own_part) * (1.0 / D)


def attention(x, pairs, high, low, gram, row, half, cot):
    heads, count, _ = cot.shape
    whole = lambda *shape: pl.BlockSpec(shape, lambda i: (0,) * len(shape))
    per_head = pl.BlockSpec((1, count, HEAD_DIM), lambda i: (i, 0, 0))
    return pl.pallas_call(
        attention_kernel,
        grid=(heads,),
        in_specs=[
            whole(*x.shape), whole(*high.shape), whole(*low.shape), whole(*gram.shape),
            whole(*row.shape), whole(*half.shape), per_head,
        ],
        out_specs=[per_head, whole(*high.shape), whole(*gram.shape)],
        out_shape=[
            jax.ShapeDtypeStruct(cot.shape, BF16),
            jax.ShapeDtypeStruct(high.shape, F32),
            jax.ShapeDtypeStruct(gram.shape, F32),
        ],
        scratch_shapes=[
            pltpu.VMEM((pairs, 4 * FEAT), BF16),
            pltpu.VMEM((4 * FEAT, pairs), BF16),
            pltpu.VMEM((count, 2 * pairs), F32),
            pltpu.VMEM((count, 2 * pairs), F32),
            pltpu.VMEM((8, 2 * pairs), F32),
            pltpu.VMEM((count, 2 * FEAT), BF16),
            pltpu.VMEM((count, 128), F32),
        ],
        compiler_params=pltpu.CompilerParams(
            dimension_semantics=("arbitrary",), vmem_limit_bytes=48 * 1024 * 1024
        ),
        name="attention",
    )(x, high, low, gram, row, half, cot)


def per_device(
    features, conv_weight, conv_bias, token_order, embed_weight, norm_gain, qkv_weight, grad_out
):
    far = lax.axis_index("seq_0")
    near_count = lax.axis_size("seq_1")
    depth, _, width = qkv_weight.shape
    pair = 2 * HEAD_DIM
    rows = 3 * HEAD_DIM
    rows_each = rows // near_count

    def swapped(array, axis):
        first, second = jnp.split(array, 2, axis=axis)
        mine = jnp.where(far == 0, first, second)
        given = jnp.where(far == 0, second, first)
        return mine, lax.ppermute(given, "seq_0", [(0, 1), (1, 0)])

    def in_order(mine, other):
        return jnp.where(far == 0, jnp.stack([mine, other]), jnp.stack([other, mine]))

    clip = lax.axis_index("grp")
    half_rows = rows_each // 2

    def both_halves(mine, given, axis):
        other = lax.ppermute(given, "grp", [(0, 1), (1, 0)])
        return jnp.where(
            clip == 0, jnp.stack([mine, other], axis), jnp.stack([other, mine], axis)
        )

    w = qkv_weight.reshape(depth, 3, 2, 2, HEAD_DIM)
    w = jnp.transpose(w, (2, 1, 4, 3, 0)).reshape(2 * near_count, 2, rows_each, depth)
    w = jnp.where(clip == 0, w[:, 0], w[:, 1])
    parts = taps(features[0, 0], conv_weight)
    parts, w = lax.optimization_barrier((parts, w))
    w_blocks = lax.all_to_all(w, SEQ, 0, 0, tiled=True)
    w_slice = jnp.transpose(w_blocks, (1, 0, 2)).reshape(rows_each, D)
    embed32 = embed_weight.astype(F32)
    gained = jnp.concatenate(two(embed32 * norm_gain), axis=0)
    m_slice = mm(w_slice, gained, NT)
    m_slice = (m_slice[:, :FEAT] + m_slice[:, FEAT:]).reshape(half_rows, 2 * FEAT)
    columns = lax.axis_index(HEAD) * lax.axis_size(("grp", "seq_0"))
    columns = (columns + lax.axis_index(("grp", "seq_0"))) * depth
    gain_own = lax.dynamic_slice_in_dim(norm_gain, columns, depth, 0)
    embed_own = lax.dynamic_slice_in_dim(embed32, columns, depth, 1)
    b_each = FEAT // 2 // near_count
    b_at = lax.axis_index("seq_1") * b_each
    embed_own = jnp.concatenate(
        [lax.dynamic_slice_in_dim(embed_own, b_at + k, b_each, 0) for k in (0, FEAT // 2)], axis=0
    )

    patch = latent_patches(parts, conv_bias)
    token_order, m_slice, patch, embed_late = lax.optimization_barrier(
        (token_order, m_slice, patch, embed_weight)
    )
    gram = lax.dot_general(
        embed_late, embed_late, (((1,), (1,)), ((), ())), preferred_element_type=F32
    ) * (1.0 / D)
    own_rows = patch.shape[0]
    arrived = from_everyone(jnp.concatenate([patch, *two(m_slice)], axis=0), "seq_1")
    far_count, head_count = lax.axis_size("seq_0"), lax.axis_size(HEAD)
    plane = far_count * head_count
    mine = w_blocks.reshape(head_count, -1, far_count, rows_each, depth)
    mine = jnp.transpose(mine, (2, 0, 1, 3, 4)).reshape(plane, rows_each * 2, depth)
    mine = jnp.pad(mine, ((0, 0), (0, 0), (0, 2 * FEAT - depth)))
    latents = arrived[:, :own_rows].reshape(1, -1, 2 * FEAT)
    pairs_each = latents.shape[1]
    latents = jnp.broadcast_to(latents, (plane, pairs_each, 2 * FEAT))
    every = lax.all_to_all(
        jnp.concatenate([latents, mine], axis=1), ("seq_0", *HEAD), 0, 0, tiled=True
    )
    m_half = arrived[:, own_rows:]
    grad_out, m_half = lax.optimization_barrier((grad_out, m_half))
    m_both = both_halves(m_half, m_half, 1).reshape(near_count, 2, 2, half_rows, 2 * FEAT)
    m_high = m_both[:, :, 0].reshape(rows, 2 * FEAT)
    m_low = m_both[:, :, 1].reshape(rows, 2 * FEAT)

    per_patch_row = own_rows
    order = in_order(token_order, lax.ppermute(token_order, "seq_0", [(0, 1), (1, 0)]))
    order = order.reshape(-1, 1)
    j = order % (2 * per_patch_row)
    i = (order // (2 * per_patch_row)) % head_count
    f = order // (2 * per_patch_row * head_count)
    at_plane = (f // near_count) * head_count + i
    row = (at_plane * near_count + f % near_count) * per_patch_row + j % per_patch_row
    half = j // per_patch_row

    cot = in_order(*swapped(grad_out[0], 1)).reshape(-1, 2, HEAD_DIM)
    out, at, b = attention(
        every, plane * pairs_each, m_high, m_low, gram, row, half, jnp.transpose(cot, (1, 0, 2))
    )
    out = jnp.transpose(out, (1, 0, 2)).reshape(2, -1, pair)
    mine = jnp.where(far == 0, out[0], out[1])
    other = lax.ppermute(jnp.where(far == 0, out[1], out[0]), "seq_0", [(0, 1), (1, 0)])
    attended = jnp.where(
        far == 0,
        jnp.concatenate([mine, other], axis=1),
        jnp.concatenate([other, mine], axis=1),
    )[None]

    w_own, at = lax.optimization_barrier((every, at))
    w_own = w_own[:, pairs_each:].reshape(plane, 2, rows_each, 2 * FEAT)
    w_own = both_halves(
        lax.dynamic_index_in_dim(w_own, clip, 1, False),
        lax.dynamic_index_in_dim(w_own, 1 - clip, 1, False),
        1,
    )
    w_own = w_own.reshape(-1, 2 * FEAT)[:, :depth]
    first, second = jnp.split(b, 2, axis=0)
    b = jnp.concatenate([first, second], axis=1)
    at = jnp.concatenate(
        [
            at.reshape(near_count, rows_each, 2 * FEAT),
            b.reshape(near_count, b_each, 2 * FEAT),
        ],
        axis=1,
    )
    at = jnp.sum(lax.all_to_all(at, "seq_1", 0, 0, tiled=True), axis=0)
    at = from_everyone(at, ("grp", "seq_0", *HEAD))
    at = jnp.sum(at.reshape(-1, plane, *at.shape[1:]), axis=0)
    a_both = jnp.concatenate(two(at[:, :rows_each].reshape(-1, FEAT)), axis=1)
    t = mm(a_both, w_own, TN)
    t = (t[:FEAT] + t[FEAT:]) * gain_own
    b_rows = jnp.sum(at[:, rows_each:], axis=0).reshape(b_each, 2, FEAT)
    t = t - mm(jnp.swapaxes(b_rows, 0, 1).reshape(-1, FEAT), embed_own, TN, HIGHEST)
    parts = FEAT * depth // (D // head_count)
    t = jnp.swapaxes(t.reshape(FEAT // parts, parts, depth), 0, 1).reshape(parts, -1)
    t = jnp.sum(from_everyone(t.astype(BF16), "seq_1").astype(F32), axis=0)
    t = from_everyone(t, ("grp", "seq_0")).reshape(-1, parts, FEAT // parts, depth)
    embed_grad = jnp.transpose(t, (2, 1, 0, 3)).reshape(FEAT, -1)
    return (attended, embed_grad)


def solution(mesh):
    torus = Mesh(
        mesh.devices.reshape(mesh.shape["grp"], 2, 16, 4, 2),
        ("grp", "seq_0", "seq_1", "head_0", "head_1"),
    )
    return jax.shard_map(
        per_device,
        mesh=torus,
        in_specs=(
            P("grp", SEQ, HEAD, None, None),
            P(),
            P(),
            P(SEQ),
            P(),
            P(),
            P(SEQ, None, HEAD),
            P("grp", SEQ, HEAD),
        ),
        out_specs=(P("grp", SEQ, HEAD), P(None, HEAD)),
        check_vma=False,
    )
```

```python
import jax
import jax.numpy as jnp
from jax import lax
from jax.experimental import pallas as pl
from jax.experimental.pallas import tpu as pltpu
from jax.sharding import Mesh
from jax.sharding import PartitionSpec as P

D = 3072
HEAD_DIM = 64
FEAT = 64
SEQ = ("seq_0", "seq_1")
HEAD = ("head_0", "head_1")
F32 = jnp.float32
BF16 = jnp.bfloat16
CHUNK = 512
HIGHEST = lax.Precision.HIGHEST


def shifted(value, axis, steps):
    count = lax.axis_size(axis)
    leading, last = (max(0, -steps), min(count, count - steps))
    return lax.ppermute(value, axis, [(source, source + steps) for source in range(leading, last)])


def from_everyone(array, axis):
    copies = jnp.broadcast_to(array, (lax.axis_size(axis), *array.shape))
    return lax.all_to_all(copies, axis, split_axis=0, concat_axis=0, tiled=True)


def two(x):
    high = x.astype(BF16)
    return high, (x - high.astype(F32)).astype(BF16)


def three(x):
    high, rest = x.astype(BF16), None
    rest = x - high.astype(F32)
    mid = rest.astype(BF16)
    return high, mid, (rest - mid.astype(F32)).astype(BF16)


def mm(a, b, dims=((1,), (0,)), precision=None):
    return lax.dot_general(a, b, (dims, ((), ())), preferred_element_type=F32, precision=precision)


NT = ((1,), (1,))
TN = ((0,), (0,))


def conv_kernel(f_ref, w_ref, out_ref):
    tile = f_ref[...]
    spots, channels = tile.shape
    half = spots // 2
    cols = half // 2
    lat = w_ref.shape[0] // 27
    to = lax.broadcasted_iota(jnp.int32, (spots, spots), 0)
    source = (to // cols % 2) * half + (to % cols) * 2 + to // half
    pick = lax.broadcasted_iota(jnp.int32, (spots, spots), 1) == source
    tile = mm(pick.astype(F32).astype(BF16), tile).astype(BF16)
    zero = jnp.zeros((lat, channels), BF16)

    def block(a, taps):
        rows = []
        for b in (2, 1, 0):
            for e in taps:
                at = ((a * 3 + b) * 3 + e) * lat if e is not None else 0
                rows.append(zero if e is None else w_ref[at : at + lat, :])
        return rows + [zero, zero]

    row = lax.broadcasted_iota(jnp.int32, (cols, 128), 0)
    sums = [0.0] * 3
    for parity, here, there, shift in ((0, (1, 0), (None, 2), cols - 1), (1, (2, 1), (0, None), 1)):
        weights = jnp.concatenate(
            [w for taps in (here, there) for a in range(3) for w in block(a, taps)], axis=0
        )
        got = mm(tile[parity * half : (parity + 1) * half], weights, NT)
        edge = cols - 1 if parity == 0 else 0
        for a in range(3):
            near = got[:, a * 128 : (a + 1) * 128]
            far = got[:, (a + 3) * 128 : (a + 4) * 128]
            for r in range(2):
                moved = pltpu.roll(far[r * cols : (r + 1) * cols], shift, 0)
                both = near[r * cols : (r + 1) * cols] + jnp.where(row == edge, 0.0, moved)
                sums[a] = sums[a] + (both if r == 0 else pltpu.roll(both, 32, 1))
    for a in range(3):
        out_ref[a] = sums[a]


def taps(tile, conv_weight):
    rows, columns, channels = tile.shape
    lat = conv_weight.shape[-1]
    weight = jnp.moveaxis(conv_weight, 4, 3).reshape(27 * lat, channels)
    return pl.pallas_call(
        conv_kernel,
        out_shape=jax.ShapeDtypeStruct((3, columns // 2, 8 * lat), F32),
        name="taps",
    )(tile.reshape(rows * columns, channels), weight)


def latent_patches(parts, conv_bias):
    lat = conv_bias.shape[0]
    total = (parts[2] + shifted(parts[1], SEQ, 1)) + shifted(parts[0], SEQ, 2)
    above, below = shifted(total, HEAD, 1), shifted(total, HEAD, -1)
    own = total[:, 2 * lat : 6 * lat]
    own = own + jnp.concatenate([above[:, 6 * lat :], below[:, : 2 * lat]], axis=1)
    patch = (own + jnp.tile(conv_bias, 4)).astype(BF16)
    first, second = jnp.split(patch, 2, axis=0)
    return jnp.concatenate([first, second], axis=1)


def attention_kernel(
    x_ref, high_ref, low_ref, gram_ref, row_ref, half_ref, cot_ref,
    out_ref, at_ref, b_ref,
    both, keys_all, scores_all, probs_all, csum, query, qsum,
):
    heads = cot_ref.shape[0]
    pairs = both.shape[0]
    factor = HEAD_DIM**-0.5
    zero = jnp.zeros((FEAT, FEAT), BF16)

    x = x_ref[:, : pairs // x_ref.shape[0], :].reshape(pairs, 2 * FEAT)
    pieces = [
        jnp.concatenate(
            [jnp.concatenate([g, zero], axis=1), jnp.concatenate([zero, g], axis=1)], axis=0
        )
        for g in three(gram_ref[...])
    ]
    y = (mm(x, pieces[2]) + mm(x, pieces[1])) + mm(x, pieces[0])
    lane_i = lax.broadcasted_iota(jnp.int32, (2 * FEAT, 2 * FEAT), 0) // FEAT
    lane_j = lax.broadcasted_iota(jnp.int32, (2 * FEAT, 2 * FEAT), 1) // FEAT
    ones = (lane_i == lane_j).astype(F32).astype(BF16)
    z = three(y * x.astype(F32))
    square = (mm(z[2], ones) + mm(z[1], ones)) + mm(z[0], ones)
    normed = x.astype(F32) * lax.rsqrt(jnp.maximum(square, 0.0) + 1e-06)
    high, low = two(normed)
    both[:, : 2 * FEAT] = high
    both[:, 2 * FEAT :] = low
    csum[...] = jnp.zeros_like(csum)
    qsum[...] = jnp.zeros_like(qsum)
    hot = lax.broadcasted_iota(jnp.int32, (row_ref.shape[0], pairs), 1) == row_ref[...]
    got = mm(hot.astype(F32).astype(BF16), both[...])
    second = half_ref[...] == 1
    for k in range(2):
        piece = got[:, 2 * FEAT * k : 2 * FEAT * (k + 1)]
        query[:, FEAT * k : FEAT * (k + 1)] = jnp.where(
            second, piece[:, FEAT:], piece[:, :FEAT]
        ).astype(BF16)

    for head in range(heads):
        keys, scores, probs = keys_all.at[head], scores_all.at[head], probs_all.at[head]

        def weight(t, ref):
            block = ref[t * FEAT : (t + 1) * FEAT, :]
            block = block.astype(F32)
            return block[:, head * FEAT : (head + 1) * FEAT]

        w_high = [weight(t, high_ref) for t in range(3)]
        w_low = [weight(t, low_ref) for t in range(3)]
        w_k, w_v = w_high[1] + w_low[1], w_high[2] + w_low[2]

        def stacked(parts):
            rows = []
            for m in parts:
                rows.append(jnp.concatenate([m, zero], axis=1))
                rows.append(jnp.concatenate([zero, m], axis=1))
            return jnp.concatenate(rows, axis=0)

        main = stacked([w.astype(BF16) for w in w_high[1:]])
        rest = stacked([w.astype(BF16) for w in w_low[1:]])
        keys[...] = (
            mm(jnp.concatenate([main, main], axis=1), both[...], NT)
            + mm(rest, both[:, : 2 * FEAT], NT)
        ).astype(BF16)

        q_high, q_low = query[:, :FEAT], query[:, FEAT:]
        wq_high, wq_low = w_high[0].astype(BF16), w_low[0].astype(BF16)
        q = (mm(q_high, wq_high, NT) + (mm(q_high, wq_low, NT) + mm(q_low, wq_high, NT))).astype(BF16)
        q_scaled = (q.astype(F32) * factor).astype(BF16)
        cot = cot_ref[head]
        count = q.shape[0]

        top = jnp.full((count, 128), -jnp.inf, F32)
        for part in range(2):
            for c in range(0, pairs, CHUNK):
                s = mm(q_scaled, keys[part * FEAT : (part + 1) * FEAT, c : c + CHUNK])
                scores[:, part * pairs + c : part * pairs + c + CHUNK] = s
                for k in range(0, CHUNK, 128):
                    top = jnp.maximum(top, s[:, k : k + 128])
        top = jnp.max(top, axis=1, keepdims=True)

        total = jnp.zeros((count, 128), F32)
        mixed = [jnp.zeros((count, 4 * FEAT), F32) for _ in range(2)]
        for part in range(2):
            for c in range(0, pairs, CHUNK):
                at = part * pairs + c
                p = jnp.exp(scores[:, at : at + CHUNK] - top)
                probs[:, at : at + CHUNK] = p
                for k in range(0, CHUNK, 128):
                    total = total + p[:, k : k + 128]
                mixed[part] = mixed[part] + mm(p.astype(BF16), both[c : c + CHUNK, :])

        def folded(m):
            return (m[0][:, :FEAT] + m[0][:, 2 * FEAT : 3 * FEAT]) + (
                m[1][:, FEAT : 2 * FEAT] + m[1][:, 3 * FEAT :]
            )

        inverse = 1.0 / jnp.sum(total, axis=1, keepdims=True)
        value = folded(mixed) * inverse
        out = mm(value, w_v, NT, HIGHEST).astype(BF16)
        out_ref[head] = out
        delta = jnp.sum(cot.astype(F32) * out.astype(F32), axis=1, keepdims=True)

        mixed = [jnp.zeros((count, 4 * FEAT), F32) for _ in range(2)]
        for part in range(2):
            for c in range(0, pairs, CHUNK):
                at = part * pairs + c
                dp = mm(cot, keys[(2 + part) * FEAT : (3 + part) * FEAT, c : c + CHUNK])
                p = probs[:, at : at + CHUNK] * inverse
                ds = p * (dp - delta)
                mixed[part] = mixed[part] + mm(ds.astype(BF16), both[c : c + CHUNK, :])
                both_sides = ds * scores[:, at : at + CHUNK] + p * dp
                csum[:, at : at + CHUNK] += jnp.sum(both_sides.reshape(count // 8, 8, CHUNK), axis=0)
        grad = folded(mixed)
        dq = mm(grad, w_k, NT, HIGHEST) * factor
        q32 = q.astype(F32)
        qsum[...] += jnp.broadcast_to(jnp.sum(dq * q32, axis=1, keepdims=True), qsum.shape)
        own = q_high.astype(F32) + q_low.astype(F32)
        a_q = mm(dq, own, TN, HIGHEST)
        a_k = mm(q_scaled.astype(F32), grad, TN, HIGHEST)
        a_v = mm(cot.astype(F32), value, TN, HIGHEST)
        for t, a in enumerate((a_q, a_k, a_v)):
            at_ref[t * FEAT : (t + 1) * FEAT, head * FEAT : (head + 1) * FEAT] = a

    eye_i = lax.broadcasted_iota(jnp.int32, (2 * FEAT, 2 * FEAT), 0)
    eye_j = lax.broadcasted_iota(jnp.int32, (2 * FEAT, 2 * FEAT), 1)
    eye = (eye_i == eye_j).astype(F32).astype(BF16)
    high = both[:, : 2 * FEAT]
    turned = mm(eye, high, NT)
    c_all = jnp.sum(csum[...], axis=0, keepdims=True)
    weighted = jnp.concatenate(
        [turned[:FEAT] * c_all[:, :pairs], turned[FEAT:] * c_all[:, pairs:]], axis=0
    )
    full = mm(weighted.astype(BF16), high)
    own_part = mm(own * qsum[:, :FEAT], own, TN, HIGHEST)
    b_ref[...] = ((full[:FEAT, :FEAT] + full[FEAT:, FEAT:]) + own_part) * (1.0 / D)


def attention(x, pairs, high, low, gram, row, half, cot):
    heads, count, _ = cot.shape
    return pl.pallas_call(
        attention_kernel,
        out_shape=[
            jax.ShapeDtypeStruct(cot.shape, BF16),
            jax.ShapeDtypeStruct(high.shape, F32),
            jax.ShapeDtypeStruct(gram.shape, F32),
        ],
        scratch_shapes=[
            pltpu.VMEM((pairs, 4 * FEAT), BF16),
            pltpu.VMEM((heads, 4 * FEAT, pairs), BF16),
            pltpu.VMEM((heads, count, 2 * pairs), F32),
            pltpu.VMEM((heads, count, 2 * pairs), F32),
            pltpu.VMEM((8, 2 * pairs), F32),
            pltpu.VMEM((count, 2 * FEAT), BF16),
            pltpu.VMEM((count, 128), F32),
        ],
        compiler_params=pltpu.CompilerParams(
            vmem_limit_bytes=48 * 1024 * 1024
        ),
        name="attention",
    )(x, high, low, gram, row, half, cot)


def per_device(
    features, conv_weight, conv_bias, token_order, embed_weight, norm_gain, qkv_weight, grad_out
):
    far = lax.axis_index("seq_0")
    near_count = lax.axis_size("seq_1")
    depth, _, width = qkv_weight.shape
    pair = 2 * HEAD_DIM
    rows = 3 * HEAD_DIM
    rows_each = rows // near_count

    def swapped(array, axis):
        first, second = jnp.split(array, 2, axis=axis)
        mine = jnp.where(far == 0, first, second)
        given = jnp.where(far == 0, second, first)
        return mine, lax.ppermute(given, "seq_0", [(0, 1), (1, 0)])

    def in_order(mine, other):
        return jnp.where(far == 0, jnp.stack([mine, other]), jnp.stack([other, mine]))

    w = qkv_weight.reshape(depth, 3, 2, 2, HEAD_DIM)
    w = jnp.transpose(w, (2, 1, 4, 3, 0)).reshape(2 * near_count, rows_each * 2, depth)
    parts = taps(features[0, 0], conv_weight)
    parts, w = lax.optimization_barrier((parts, w))
    w_slice = lax.all_to_all(w, SEQ, 0, 0, tiled=True)
    w_blocks = w_slice
    w_slice = jnp.transpose(w_slice, (1, 0, 2)).reshape(rows_each * 2, D)
    embed32 = embed_weight.astype(F32)
    gained = jnp.concatenate(two(embed32 * norm_gain), axis=0)
    m_slice = mm(w_slice, gained, NT)
    m_slice = (m_slice[:, :FEAT] + m_slice[:, FEAT:]).reshape(rows_each, 2 * FEAT)
    columns = lax.axis_index(HEAD) * lax.axis_size(("grp", "seq_0"))
    columns = (columns + lax.axis_index(("grp", "seq_0"))) * depth
    gain_own = lax.dynamic_slice_in_dim(norm_gain, columns, depth, 0)
    embed_own = lax.dynamic_slice_in_dim(embed32, columns, depth, 1)
    b_each = FEAT // 2 // near_count
    b_at = lax.axis_index("seq_1") * b_each
    embed_own = jnp.concatenate(
        [lax.dynamic_slice_in_dim(embed_own, b_at + k, b_each, 0) for k in (0, FEAT // 2)], axis=0
    )
    gram = lax.dot_general(
        embed_weight, embed_weight, (((1,), (1,)), ((), ())), preferred_element_type=F32
    ) * (1.0 / D)

    patch = latent_patches(parts, conv_bias)
    token_order, m_slice, patch, gram = lax.optimization_barrier(
        (token_order, m_slice, patch, gram)
    )
    own_rows = patch.shape[0]
    arrived = from_everyone(jnp.concatenate([patch, *two(m_slice)], axis=0), "seq_1")
    grad_out, arrived = lax.optimization_barrier((grad_out, arrived))
    far_count, head_count = lax.axis_size("seq_0"), lax.axis_size(HEAD)
    plane = far_count * head_count
    mine = w_blocks.reshape(head_count, -1, far_count, rows_each * 2, depth)
    mine = jnp.swapaxes(lax.dynamic_index_in_dim(mine, lax.axis_index("grp"), 1, False), 0, 1)
    mine = mine.reshape(plane, rows_each * 2, depth)
    mine = jnp.pad(mine, ((0, 0), (0, 0), (0, 2 * FEAT - depth)))
    latents = arrived[:, :own_rows].reshape(1, -1, 2 * FEAT)
    pairs_each = latents.shape[1]
    latents = jnp.broadcast_to(latents, (plane, pairs_each, 2 * FEAT))
    every = lax.all_to_all(
        jnp.concatenate([latents, mine], axis=1), ("seq_0", *HEAD), 0, 0, tiled=True
    )
    w_own = every[:, pairs_each:, :depth].reshape(-1, depth)
    m_high = arrived[:, own_rows : own_rows + rows_each].reshape(rows, 2 * FEAT)
    m_low = arrived[:, own_rows + rows_each :].reshape(rows, 2 * FEAT)

    per_patch_row = own_rows
    order = in_order(token_order, lax.ppermute(token_order, "seq_0", [(0, 1), (1, 0)]))
    order = order.reshape(-1, 1)
    j = order % (2 * per_patch_row)
    i = (order // (2 * per_patch_row)) % head_count
    f = order // (2 * per_patch_row * head_count)
    at_plane = (f // near_count) * head_count + i
    row = (at_plane * near_count + f % near_count) * per_patch_row + j % per_patch_row
    half = j // per_patch_row

    cot = in_order(*swapped(grad_out[0], 1)).reshape(-1, 2, HEAD_DIM)
    out, at, b = attention(
        every, plane * pairs_each, m_high, m_low, gram, row, half, jnp.transpose(cot, (1, 0, 2))
    )
    out = jnp.transpose(out, (1, 0, 2)).reshape(2, -1, pair)
    mine = jnp.where(far == 0, out[0], out[1])
    other = lax.ppermute(jnp.where(far == 0, out[1], out[0]), "seq_0", [(0, 1), (1, 0)])
    attended = jnp.where(
        far == 0,
        jnp.concatenate([mine, other], axis=1),
        jnp.concatenate([other, mine], axis=1),
    )[None]

    first, second = jnp.split(b, 2, axis=0)
    b = jnp.concatenate([first, second], axis=1)
    at = jnp.concatenate(
        [
            at.reshape(near_count, rows_each, 2 * FEAT),
            b.reshape(near_count, b_each, 2 * FEAT),
        ],
        axis=1,
    )
    at = jnp.sum(lax.all_to_all(at, "seq_1", 0, 0, tiled=True), axis=0)
    at = from_everyone(at, ("grp", "seq_0", *HEAD))
    at = jnp.sum(at.reshape(-1, plane, *at.shape[1:]), axis=0)
    a_both = jnp.concatenate(two(at[:, :rows_each].reshape(-1, FEAT)), axis=1)
    t = mm(a_both, w_own, TN)
    t = (t[:FEAT] + t[FEAT:]) * gain_own
    b_rows = jnp.sum(at[:, rows_each:], axis=0).reshape(b_each, 2, FEAT)
    t = t - mm(jnp.swapaxes(b_rows, 0, 1).reshape(-1, FEAT), embed_own, TN, HIGHEST)
    parts = FEAT * depth // (D // head_count)
    t = jnp.swapaxes(t.reshape(FEAT // parts, parts, depth), 0, 1).reshape(parts, -1)
    t = jnp.sum(from_everyone(t.astype(BF16), "seq_1").astype(F32), axis=0)
    t = from_everyone(t, ("grp", "seq_0")).reshape(-1, parts, FEAT // parts, depth)
    embed_grad = jnp.transpose(t, (2, 1, 0, 3)).reshape(FEAT, -1)
    return (attended, embed_grad)


def solution(mesh):
    torus = Mesh(
        mesh.devices.reshape(mesh.shape["grp"], 2, 16, 4, 2),
        ("grp", "seq_0", "seq_1", "head_0", "head_1"),
    )
    return jax.shard_map(
        per_device,
        mesh=torus,
        in_specs=(
            P("grp", SEQ, HEAD, None, None),
            P(),
            P(),
            P(SEQ),
            P(),
            P(),
            P(SEQ, None, HEAD),
            P("grp", SEQ, HEAD),
        ),
        out_specs=(P("grp", SEQ, HEAD), P(None, HEAD)),
        check_vma=False,
    )
```

```python
import jax
import jax.numpy as jnp
from jax import lax
from jax.experimental import pallas as pl
from jax.experimental.pallas import tpu as pltpu
from jax.sharding import Mesh
from jax.sharding import PartitionSpec as P

D = 3072
HEAD_DIM = 64
FEAT = 64
SEQ = ("seq_0", "seq_1")
HEAD = ("head_0", "head_1")
F32 = jnp.float32
BF16 = jnp.bfloat16
CHUNK = 512
HIGHEST = lax.Precision.HIGHEST


def shifted(value, axis, steps):
    count = lax.axis_size(axis)
    leading, last = (max(0, -steps), min(count, count - steps))
    return lax.ppermute(value, axis, [(source, source + steps) for source in range(leading, last)])


def from_everyone(array, axis):
    copies = jnp.broadcast_to(array, (lax.axis_size(axis), *array.shape))
    return lax.all_to_all(copies, axis, split_axis=0, concat_axis=0, tiled=True)


def two(x):
    high = x.astype(BF16)
    return high, (x - high.astype(F32)).astype(BF16)


def three(x):
    high, rest = x.astype(BF16), None
    rest = x - high.astype(F32)
    mid = rest.astype(BF16)
    return high, mid, (rest - mid.astype(F32)).astype(BF16)


def mm(a, b, dims=((1,), (0,)), precision=None):
    return lax.dot_general(a, b, (dims, ((), ())), preferred_element_type=F32, precision=precision)


NT = ((1,), (1,))
TN = ((0,), (0,))


def conv_kernel(f_ref, w_ref, out_ref):
    tile = f_ref[...]
    spots, channels = tile.shape
    half = spots // 2
    cols = half // 2
    lat = w_ref.shape[0] // 27
    to = lax.broadcasted_iota(jnp.int32, (spots, spots), 0)
    source = (to // cols % 2) * half + (to % cols) * 2 + to // half
    pick = lax.broadcasted_iota(jnp.int32, (spots, spots), 1) == source
    tile = mm(pick.astype(F32).astype(BF16), tile).astype(BF16)
    zero = jnp.zeros((lat, channels), BF16)

    def block(a, taps):
        rows = []
        for b in (2, 1, 0):
            for e in taps:
                at = ((a * 3 + b) * 3 + e) * lat if e is not None else 0
                rows.append(zero if e is None else w_ref[at : at + lat, :])
        return rows + [zero, zero]

    row = lax.broadcasted_iota(jnp.int32, (cols, 128), 0)
    sums = [0.0] * 3
    for parity, here, there, shift in ((0, (1, 0), (None, 2), cols - 1), (1, (2, 1), (0, None), 1)):
        weights = jnp.concatenate(
            [w for taps in (here, there) for a in range(3) for w in block(a, taps)], axis=0
        )
        got = mm(tile[parity * half : (parity + 1) * half], weights, NT)
        edge = cols - 1 if parity == 0 else 0
        for a in range(3):
            near = got[:, a * 128 : (a + 1) * 128]
            far = got[:, (a + 3) * 128 : (a + 4) * 128]
            for r in range(2):
                moved = pltpu.roll(far[r * cols : (r + 1) * cols], shift, 0)
                both = near[r * cols : (r + 1) * cols] + jnp.where(row == edge, 0.0, moved)
                sums[a] = sums[a] + (both if r == 0 else pltpu.roll(both, 32, 1))
    for a in range(3):
        out_ref[a] = sums[a]


def encode_tile(tile, conv_weight, conv_bias):
    rows, columns, channels = tile.shape
    lat = conv_weight.shape[-1]
    weight = jnp.moveaxis(conv_weight, 4, 3).reshape(27 * lat, channels)
    parts = pl.pallas_call(
        conv_kernel,
        out_shape=jax.ShapeDtypeStruct((3, columns // 2, 8 * lat), F32),
        name="taps",
    )(tile.reshape(rows * columns, channels), weight)
    total = (parts[2] + shifted(parts[1], SEQ, 1)) + shifted(parts[0], SEQ, 2)
    above, below = shifted(total, HEAD, 1), shifted(total, HEAD, -1)
    own = total[:, 2 * lat : 6 * lat]
    own = own + jnp.concatenate([above[:, 6 * lat :], below[:, : 2 * lat]], axis=1)
    patch = (own + jnp.tile(conv_bias, 4)).astype(BF16)
    first, second = jnp.split(patch, 2, axis=0)
    return jnp.concatenate([first, second], axis=1)


def attention_kernel(
    x_ref, high_ref, low_ref, gram_ref, row_ref, half_ref, cot_ref,
    out_ref, at_ref, b_ref,
    both, keys, scores, probs, csum, query,
):
    heads = cot_ref.shape[0]
    pairs = both.shape[0]
    factor = HEAD_DIM**-0.5
    zero = jnp.zeros((FEAT, FEAT), BF16)

    x = x_ref[:, : pairs // x_ref.shape[0], :].reshape(pairs, 2 * FEAT)
    pieces = [
        jnp.concatenate(
            [jnp.concatenate([g, zero], axis=1), jnp.concatenate([zero, g], axis=1)], axis=0
        )
        for g in three(gram_ref[...])
    ]
    y = (mm(x, pieces[2]) + mm(x, pieces[1])) + mm(x, pieces[0])
    lane_i = lax.broadcasted_iota(jnp.int32, (2 * FEAT, 2 * FEAT), 0) // FEAT
    lane_j = lax.broadcasted_iota(jnp.int32, (2 * FEAT, 2 * FEAT), 1) // FEAT
    ones = (lane_i == lane_j).astype(F32).astype(BF16)
    z = three(y * x.astype(F32))
    square = (mm(z[2], ones) + mm(z[1], ones)) + mm(z[0], ones)
    normed = x.astype(F32) * lax.rsqrt(jnp.maximum(square, 0.0) + 1e-06)
    high, low = two(normed)
    both[:, : 2 * FEAT] = high
    both[:, 2 * FEAT :] = low
    hot = lax.broadcasted_iota(jnp.int32, (row_ref.shape[0], pairs), 1) == row_ref[...]
    got = mm(hot.astype(F32).astype(BF16), both[...])
    second = half_ref[...] == 1
    for k in range(2):
        piece = got[:, 2 * FEAT * k : 2 * FEAT * (k + 1)]
        query[:, FEAT * k : FEAT * (k + 1)] = jnp.where(
            second, piece[:, FEAT:], piece[:, :FEAT]
        ).astype(BF16)

    sides = [slice(head * FEAT, (head + 1) * FEAT) for head in range(heads)]
    q_high, q_low = query[:, :FEAT], query[:, FEAT:]
    own = q_high.astype(F32) + q_low.astype(F32)
    count = q_high.shape[0]
    queries, w_keys, w_values = [], [], []
    for head, side in enumerate(sides):
        w_high = [high_ref[t * FEAT : (t + 1) * FEAT, side] for t in range(3)]
        w_low = [low_ref[t * FEAT : (t + 1) * FEAT, side] for t in range(3)]
        w_keys.append(w_high[1].astype(F32) + w_low[1].astype(F32))
        w_values.append(w_high[2].astype(F32) + w_low[2].astype(F32))

        def stacked(parts):
            rows = []
            for m in parts:
                rows.append(jnp.concatenate([m, zero], axis=1))
                rows.append(jnp.concatenate([zero, m], axis=1))
            return jnp.concatenate(rows, axis=0)

        main, rest = stacked(w_high[1:]), stacked(w_low[1:])
        keys[head] = (
            mm(jnp.concatenate([main, main], axis=1), both[...], NT)
            + mm(rest, both[:, : 2 * FEAT], NT)
        ).astype(BF16)
        q = mm(q_high, w_high[0], NT) + (mm(q_high, w_low[0], NT) + mm(q_low, w_high[0], NT))
        queries.append(q.astype(BF16))
    scaled = [(q.astype(F32) * factor).astype(BF16) for q in queries]
    cots = [cot_ref[head] for head in range(heads)]

    def products(rows, part, c):
        return jnp.concatenate(
            [
                mm(r, keys[head, part * FEAT : (part + 1) * FEAT, c : c + CHUNK])
                for head, r in enumerate(rows)
            ],
            axis=0,
        )

    top = jnp.full((heads * count, 128), -jnp.inf, F32)
    for part in range(2):
        for c in range(0, pairs, CHUNK):
            s = products(scaled, part, c)
            scores[:, part * pairs + c : part * pairs + c + CHUNK] = s
            for k in range(0, CHUNK, 128):
                top = jnp.maximum(top, s[:, k : k + 128])
    top = jnp.max(top, axis=1, keepdims=True)

    total = jnp.zeros((heads * count, 128), F32)
    mixed = [jnp.zeros((heads * count, 4 * FEAT), F32) for _ in range(2)]
    for part in range(2):
        for c in range(0, pairs, CHUNK):
            at = part * pairs + c
            p = jnp.exp(scores[:, at : at + CHUNK] - top)
            probs[:, at : at + CHUNK] = p
            for k in range(0, CHUNK, 128):
                total = total + p[:, k : k + 128]
            mixed[part] = mixed[part] + mm(p.astype(BF16), both[c : c + CHUNK, :])

    def folded(m):
        return (m[0][:, :FEAT] + m[0][:, 2 * FEAT : 3 * FEAT]) + (
            m[1][:, FEAT : 2 * FEAT] + m[1][:, 3 * FEAT :]
        )

    inverse = 1.0 / jnp.sum(total, axis=1, keepdims=True)
    value = folded(mixed) * inverse
    deltas = []
    for head in range(heads):
        out = mm(value[head * count : (head + 1) * count], w_values[head], NT, HIGHEST)
        out = out.astype(BF16)
        out_ref[head] = out
        deltas.append(
            jnp.sum(cots[head].astype(F32) * out.astype(F32), axis=1, keepdims=True)
        )
    delta = jnp.concatenate(deltas, axis=0)

    mixed = [jnp.zeros((heads * count, 4 * FEAT), F32) for _ in range(2)]
    for part in range(2):
        for c in range(0, pairs, CHUNK):
            at = part * pairs + c
            dp = products(cots, 2 + part, c)
            p = probs[:, at : at + CHUNK] * inverse
            ds = p * (dp - delta)
            mixed[part] = mixed[part] + mm(ds.astype(BF16), both[c : c + CHUNK, :])
            both_sides = ds * scores[:, at : at + CHUNK] + p * dp
            csum[:, at : at + CHUNK] = jnp.sum(
                both_sides.reshape(heads * count // 8, 8, CHUNK), axis=0
            )
    grad = folded(mixed)
    inner = 0.0
    for head, side in enumerate(sides):
        mine = slice(head * count, (head + 1) * count)
        dq = mm(grad[mine], w_keys[head], NT, HIGHEST) * factor
        inner = inner + jnp.sum(dq * queries[head].astype(F32), axis=1, keepdims=True)
        at_ref[:FEAT, side] = mm(dq, own, TN, HIGHEST)
        at_ref[FEAT : 2 * FEAT, side] = mm(scaled[head].astype(F32), grad[mine], TN, HIGHEST)
        at_ref[2 * FEAT :, side] = mm(cots[head].astype(F32), value[mine], TN, HIGHEST)

    eye_i = lax.broadcasted_iota(jnp.int32, (2 * FEAT, 2 * FEAT), 0)
    eye_j = lax.broadcasted_iota(jnp.int32, (2 * FEAT, 2 * FEAT), 1)
    eye = (eye_i == eye_j).astype(F32).astype(BF16)
    high = both[:, : 2 * FEAT]
    turned = mm(eye, high, NT)
    c_all = jnp.sum(csum[...], axis=0, keepdims=True)
    weighted = jnp.concatenate(
        [turned[:FEAT] * c_all[:, :pairs], turned[FEAT:] * c_all[:, pairs:]], axis=0
    )
    full = mm(weighted.astype(BF16), high)
    own_part = mm(own * inner, own, TN, HIGHEST)
    b_ref[...] = ((full[:FEAT, :FEAT] + full[FEAT:, FEAT:]) + own_part) * (1.0 / D)


def attention(x, pairs, high, low, gram, row, half, cot):
    heads, count, _ = cot.shape
    return pl.pallas_call(
        attention_kernel,
        out_shape=[
            jax.ShapeDtypeStruct(cot.shape, BF16),
            jax.ShapeDtypeStruct(high.shape, F32),
            jax.ShapeDtypeStruct(gram.shape, F32),
        ],
        scratch_shapes=[
            pltpu.VMEM((pairs, 4 * FEAT), BF16),
            pltpu.VMEM((heads, 4 * FEAT, pairs), BF16),
            pltpu.VMEM((heads * count, 2 * pairs), F32),
            pltpu.VMEM((heads * count, 2 * pairs), F32),
            pltpu.VMEM((8, 2 * pairs), F32),
            pltpu.VMEM((count, 2 * FEAT), BF16),
        ],
        compiler_params=pltpu.CompilerParams(
            vmem_limit_bytes=48 * 1024 * 1024
        ),
        name="attention",
    )(x, high, low, gram, row, half, cot)


def per_device(
    features, conv_weight, conv_bias, token_order, embed_weight, norm_gain, qkv_weight, grad_out
):
    far = lax.axis_index("seq_0")
    near_count = lax.axis_size("seq_1")
    depth, _, width = qkv_weight.shape
    pair = 2 * HEAD_DIM
    rows = 3 * HEAD_DIM
    rows_each = rows // near_count

    def swapped(array, axis):
        first, second = jnp.split(array, 2, axis=axis)
        mine = jnp.where(far == 0, first, second)
        given = jnp.where(far == 0, second, first)
        return mine, lax.ppermute(given, "seq_0", [(0, 1), (1, 0)])

    def in_order(mine, other):
        return jnp.where(far == 0, jnp.stack([mine, other]), jnp.stack([other, mine]))

    w = qkv_weight.reshape(depth, 3, 2, 2, HEAD_DIM)
    w = jnp.transpose(w, (2, 1, 4, 3, 0)).reshape(2 * near_count, rows_each * 2, depth)
    w_slice = lax.all_to_all(w, SEQ, 0, 0, tiled=True)
    w_blocks = w_slice
    w_slice = jnp.transpose(w_slice, (1, 0, 2)).reshape(rows_each * 2, D)
    embed32 = embed_weight.astype(F32)
    gained = jnp.concatenate(two(embed32 * norm_gain), axis=0)
    m_slice = mm(w_slice, gained, NT)
    m_slice = (m_slice[:, :FEAT] + m_slice[:, FEAT:]).reshape(rows_each, 2 * FEAT)
    columns = lax.axis_index(HEAD) * lax.axis_size(("grp", "seq_0"))
    columns = (columns + lax.axis_index(("grp", "seq_0"))) * depth
    gain_own = lax.dynamic_slice_in_dim(norm_gain, columns, depth, 0)
    embed_own = lax.dynamic_slice_in_dim(embed32, columns, depth, 1)
    b_each = FEAT // 2 // near_count
    b_at = lax.axis_index("seq_1") * b_each
    embed_own = jnp.concatenate(
        [lax.dynamic_slice_in_dim(embed_own, b_at + k, b_each, 0) for k in (0, FEAT // 2)], axis=0
    )
    gram = lax.dot_general(
        embed_weight, embed_weight, (((1,), (1,)), ((), ())), preferred_element_type=F32
    ) * (1.0 / D)

    patch = encode_tile(features[0, 0], conv_weight, conv_bias)
    token_order, grad_out, patch = lax.optimization_barrier((token_order, grad_out, patch))
    own_rows = patch.shape[0]
    arrived = from_everyone(jnp.concatenate([patch, *two(m_slice)], axis=0), "seq_1")
    far_count, head_count = lax.axis_size("seq_0"), lax.axis_size(HEAD)
    plane = far_count * head_count
    mine = w_blocks.reshape(head_count, -1, far_count, rows_each * 2, depth)
    mine = jnp.swapaxes(lax.dynamic_index_in_dim(mine, lax.axis_index("grp"), 1, False), 0, 1)
    mine = mine.reshape(plane, rows_each * 2, depth)
    mine = jnp.pad(mine, ((0, 0), (0, 0), (0, 2 * FEAT - depth)))
    latents = arrived[:, :own_rows].reshape(1, -1, 2 * FEAT)
    pairs_each = latents.shape[1]
    latents = jnp.broadcast_to(latents, (plane, pairs_each, 2 * FEAT))
    every = lax.all_to_all(
        jnp.concatenate([latents, mine], axis=1), ("seq_0", *HEAD), 0, 0, tiled=True
    )
    w_own = every[:, pairs_each:, :depth].reshape(-1, depth)
    m_high = arrived[:, own_rows : own_rows + rows_each].reshape(rows, 2 * FEAT)
    m_low = arrived[:, own_rows + rows_each :].reshape(rows, 2 * FEAT)

    per_patch_row = own_rows
    order = in_order(token_order, lax.ppermute(token_order, "seq_0", [(0, 1), (1, 0)]))
    order = order.reshape(-1, 1)
    j = order % (2 * per_patch_row)
    i = (order // (2 * per_patch_row)) % head_count
    f = order // (2 * per_patch_row * head_count)
    at_plane = (f // near_count) * head_count + i
    row = (at_plane * near_count + f % near_count) * per_patch_row + j % per_patch_row
    half = j // per_patch_row

    cot = in_order(*swapped(grad_out[0], 1)).reshape(-1, 2, HEAD_DIM)
    out, at, b = attention(
        every, plane * pairs_each, m_high, m_low, gram, row, half, jnp.transpose(cot, (1, 0, 2))
    )
    out = jnp.transpose(out, (1, 0, 2)).reshape(2, -1, pair)
    mine = jnp.where(far == 0, out[0], out[1])
    other = lax.ppermute(jnp.where(far == 0, out[1], out[0]), "seq_0", [(0, 1), (1, 0)])
    attended = jnp.where(
        far == 0,
        jnp.concatenate([mine, other], axis=1),
        jnp.concatenate([other, mine], axis=1),
    )[None]

    first, second = jnp.split(b, 2, axis=0)
    b = jnp.concatenate([first, second], axis=1)
    at = jnp.concatenate(
        [
            at.reshape(near_count, rows_each, 2 * FEAT),
            b.reshape(near_count, b_each, 2 * FEAT),
        ],
        axis=1,
    )
    at = jnp.sum(lax.all_to_all(at, "seq_1", 0, 0, tiled=True), axis=0)
    at = from_everyone(at, ("grp", "seq_0", *HEAD))
    at = jnp.sum(at.reshape(-1, plane, *at.shape[1:]), axis=0)
    a_both = jnp.concatenate(two(at[:, :rows_each].reshape(-1, FEAT)), axis=1)
    t = mm(a_both, w_own, TN)
    t = (t[:FEAT] + t[FEAT:]) * gain_own
    b_rows = jnp.sum(at[:, rows_each:], axis=0).reshape(b_each, 2, FEAT)
    t = t - mm(jnp.swapaxes(b_rows, 0, 1).reshape(-1, FEAT), embed_own, TN, HIGHEST)
    parts = FEAT * depth // (D // head_count)
    t = jnp.swapaxes(t.reshape(FEAT // parts, parts, depth), 0, 1).reshape(parts, -1)
    t = jnp.sum(from_everyone(t.astype(BF16), "seq_1").astype(F32), axis=0)
    t = from_everyone(t, ("grp", "seq_0")).reshape(-1, parts, FEAT // parts, depth)
    embed_grad = jnp.transpose(t, (2, 1, 0, 3)).reshape(FEAT, -1)
    return (attended, embed_grad)


def solution(mesh):
    torus = Mesh(
        mesh.devices.reshape(mesh.shape["grp"], 2, 16, 4, 2),
        ("grp", "seq_0", "seq_1", "head_0", "head_1"),
    )
    return jax.shard_map(
        per_device,
        mesh=torus,
        in_specs=(
            P("grp", SEQ, HEAD, None, None),
            P(),
            P(),
            P(SEQ),
            P(),
            P(),
            P(SEQ, None, HEAD),
            P("grp", SEQ, HEAD),
        ),
        out_specs=(P("grp", SEQ, HEAD), P(None, HEAD)),
        check_vma=False,
    )
```

```python
import jax
import jax.numpy as jnp
from jax import lax
from jax.experimental import pallas as pl
from jax.experimental.pallas import tpu as pltpu
from jax.sharding import Mesh
from jax.sharding import PartitionSpec as P

D = 3072
HEAD_DIM = 64
FEAT = 64
SEQ = ("seq_0", "seq_1")
HEAD = ("head_0", "head_1")
F32 = jnp.float32
BF16 = jnp.bfloat16
CHUNK = 512
HIGHEST = lax.Precision.HIGHEST


def shifted(value, axis, steps):
    count = lax.axis_size(axis)
    leading, last = (max(0, -steps), min(count, count - steps))
    return lax.ppermute(value, axis, [(source, source + steps) for source in range(leading, last)])


def from_everyone(array, axis):
    copies = jnp.broadcast_to(array, (lax.axis_size(axis), *array.shape))
    return lax.all_to_all(copies, axis, split_axis=0, concat_axis=0, tiled=True)


def two(x):
    high = x.astype(BF16)
    return high, (x - high.astype(F32)).astype(BF16)


def three(x):
    high, rest = x.astype(BF16), None
    rest = x - high.astype(F32)
    mid = rest.astype(BF16)
    return high, mid, (rest - mid.astype(F32)).astype(BF16)


def mm(a, b, dims=((1,), (0,)), precision=None):
    return lax.dot_general(a, b, (dims, ((), ())), preferred_element_type=F32, precision=precision)


NT = ((1,), (1,))
TN = ((0,), (0,))


def conv_kernel(f_ref, w_ref, out_ref):
    tile = f_ref[...]
    spots, channels = tile.shape
    half = spots // 2
    cols = half // 2
    lat = w_ref.shape[0] // 27
    to = lax.broadcasted_iota(jnp.int32, (spots, spots), 0)
    source = (to // cols % 2) * half + (to % cols) * 2 + to // half
    pick = lax.broadcasted_iota(jnp.int32, (spots, spots), 1) == source
    tile = mm(pick.astype(F32).astype(BF16), tile).astype(BF16)
    zero = jnp.zeros((lat, channels), BF16)

    def block(a, taps):
        rows = []
        for b in (2, 1, 0):
            for e in taps:
                at = ((a * 3 + b) * 3 + e) * lat if e is not None else 0
                rows.append(zero if e is None else w_ref[at : at + lat, :])
        return rows + [zero, zero]

    row = lax.broadcasted_iota(jnp.int32, (cols, 128), 0)
    sums = [0.0] * 3
    for parity, here, there, shift in ((0, (1, 0), (None, 2), cols - 1), (1, (2, 1), (0, None), 1)):
        weights = jnp.concatenate(
            [w for taps in (here, there) for a in range(3) for w in block(a, taps)], axis=0
        )
        got = mm(tile[parity * half : (parity + 1) * half], weights, NT)
        edge = cols - 1 if parity == 0 else 0
        for a in range(3):
            near = got[:, a * 128 : (a + 1) * 128]
            far = got[:, (a + 3) * 128 : (a + 4) * 128]
            for r in range(2):
                moved = pltpu.roll(far[r * cols : (r + 1) * cols], shift, 0)
                both = near[r * cols : (r + 1) * cols] + jnp.where(row == edge, 0.0, moved)
                sums[a] = sums[a] + (both if r == 0 else pltpu.roll(both, 32, 1))
    for a in range(3):
        out_ref[a] = sums[a]


def taps(tile, conv_weight):
    rows, columns, channels = tile.shape
    lat = conv_weight.shape[-1]
    weight = jnp.moveaxis(conv_weight, 4, 3).reshape(27 * lat, channels)
    parts = pl.pallas_call(
        conv_kernel,
        out_shape=jax.ShapeDtypeStruct((3, columns // 2, 8 * lat), F32),
        name="taps",
    )(tile.reshape(rows * columns, channels), weight)
    return parts


def latent_patches(parts, conv_bias):
    lat = conv_bias.shape[0]
    total = (parts[2] + shifted(parts[1], SEQ, 1)) + shifted(parts[0], SEQ, 2)
    above, below = shifted(total, HEAD, 1), shifted(total, HEAD, -1)
    own = total[:, 2 * lat : 6 * lat]
    own = own + jnp.concatenate([above[:, 6 * lat :], below[:, : 2 * lat]], axis=1)
    patch = (own + jnp.tile(conv_bias, 4)).astype(BF16)
    first, second = jnp.split(patch, 2, axis=0)
    return jnp.concatenate([first, second], axis=1)


def attention_kernel(
    x_ref, high_ref, low_ref, gram_ref, row_ref, half_ref, cot_ref,
    out_ref, at_ref, b_ref,
    both, keys, scores, probs, csum, query,
):
    heads = cot_ref.shape[0]
    pairs = both.shape[0]
    factor = HEAD_DIM**-0.5
    zero = jnp.zeros((FEAT, FEAT), BF16)

    x = x_ref[:, : pairs // x_ref.shape[0], :].reshape(pairs, 2 * FEAT)
    pieces = [
        jnp.concatenate(
            [jnp.concatenate([g, zero], axis=1), jnp.concatenate([zero, g], axis=1)], axis=0
        )
        for g in three(gram_ref[...])
    ]
    y = (mm(x, pieces[2]) + mm(x, pieces[1])) + mm(x, pieces[0])
    lane_i = lax.broadcasted_iota(jnp.int32, (2 * FEAT, 2 * FEAT), 0) // FEAT
    lane_j = lax.broadcasted_iota(jnp.int32, (2 * FEAT, 2 * FEAT), 1) // FEAT
    ones = (lane_i == lane_j).astype(F32).astype(BF16)
    z = three(y * x.astype(F32))
    square = (mm(z[2], ones) + mm(z[1], ones)) + mm(z[0], ones)
    normed = x.astype(F32) * lax.rsqrt(jnp.maximum(square, 0.0) + 1e-06)
    high, low = two(normed)
    both[:, : 2 * FEAT] = high
    both[:, 2 * FEAT :] = low
    hot = lax.broadcasted_iota(jnp.int32, (row_ref.shape[0], pairs), 1) == row_ref[...]
    got = mm(hot.astype(F32).astype(BF16), both[...])
    second = half_ref[...] == 1
    for k in range(2):
        piece = got[:, 2 * FEAT * k : 2 * FEAT * (k + 1)]
        query[:, FEAT * k : FEAT * (k + 1)] = jnp.where(
            second, piece[:, FEAT:], piece[:, :FEAT]
        ).astype(BF16)

    sides = [slice(head * FEAT, (head + 1) * FEAT) for head in range(heads)]
    q_high, q_low = query[:, :FEAT], query[:, FEAT:]
    own = q_high.astype(F32) + q_low.astype(F32)
    count = q_high.shape[0]
    queries, w_keys, w_values = [], [], []
    for head, side in enumerate(sides):
        w_high = [high_ref[t * FEAT : (t + 1) * FEAT, side] for t in range(3)]
        w_low = [low_ref[t * FEAT : (t + 1) * FEAT, side] for t in range(3)]
        w_keys.append(w_high[1].astype(F32) + w_low[1].astype(F32))
        w_values.append(w_high[2].astype(F32) + w_low[2].astype(F32))

        def stacked(parts):
            rows = []
            for m in parts:
                rows.append(jnp.concatenate([m, zero], axis=1))
                rows.append(jnp.concatenate([zero, m], axis=1))
            return jnp.concatenate(rows, axis=0)

        main, rest = stacked(w_high[1:]), stacked(w_low[1:])
        keys[head] = (
            mm(jnp.concatenate([main, main], axis=1), both[...], NT)
            + mm(rest, both[:, : 2 * FEAT], NT)
        ).astype(BF16)
        q = mm(q_high, w_high[0], NT) + (mm(q_high, w_low[0], NT) + mm(q_low, w_high[0], NT))
        queries.append(q.astype(BF16))
    scaled = [(q.astype(F32) * factor).astype(BF16) for q in queries]
    cots = [cot_ref[head] for head in range(heads)]

    def products(rows, part, c):
        return jnp.concatenate(
            [
                mm(r, keys[head, part * FEAT : (part + 1) * FEAT, c : c + CHUNK])
                for head, r in enumerate(rows)
            ],
            axis=0,
        )

    top = jnp.full((heads * count, 128), -jnp.inf, F32)
    for part in range(2):
        for c in range(0, pairs, CHUNK):
            s = products(scaled, part, c)
            scores[:, part * pairs + c : part * pairs + c + CHUNK] = s
            for k in range(0, CHUNK, 128):
                top = jnp.maximum(top, s[:, k : k + 128])
    top = jnp.max(top, axis=1, keepdims=True)

    total = jnp.zeros((heads * count, 128), F32)
    mixed = [jnp.zeros((heads * count, 4 * FEAT), F32) for _ in range(2)]
    for part in range(2):
        for c in range(0, pairs, CHUNK):
            at = part * pairs + c
            p = jnp.exp(scores[:, at : at + CHUNK] - top)
            probs[:, at : at + CHUNK] = p
            for k in range(0, CHUNK, 128):
                total = total + p[:, k : k + 128]
            mixed[part] = mixed[part] + mm(p.astype(BF16), both[c : c + CHUNK, :])

    def folded(m):
        return (m[0][:, :FEAT] + m[0][:, 2 * FEAT : 3 * FEAT]) + (
            m[1][:, FEAT : 2 * FEAT] + m[1][:, 3 * FEAT :]
        )

    inverse = 1.0 / jnp.sum(total, axis=1, keepdims=True)
    value = folded(mixed) * inverse
    deltas = []
    for head in range(heads):
        out = mm(value[head * count : (head + 1) * count], w_values[head], NT, HIGHEST)
        out = out.astype(BF16)
        out_ref[head] = out
        deltas.append(
            jnp.sum(cots[head].astype(F32) * out.astype(F32), axis=1, keepdims=True)
        )
    delta = jnp.concatenate(deltas, axis=0)

    mixed = [jnp.zeros((heads * count, 4 * FEAT), F32) for _ in range(2)]
    for part in range(2):
        for c in range(0, pairs, CHUNK):
            at = part * pairs + c
            dp = products(cots, 2 + part, c)
            p = probs[:, at : at + CHUNK] * inverse
            ds = p * (dp - delta)
            mixed[part] = mixed[part] + mm(ds.astype(BF16), both[c : c + CHUNK, :])
            both_sides = ds * scores[:, at : at + CHUNK] + p * dp
            csum[:, at : at + CHUNK] = jnp.sum(
                both_sides.reshape(heads * count // 8, 8, CHUNK), axis=0
            )
    grad = folded(mixed)
    inner = 0.0
    for head, side in enumerate(sides):
        mine = slice(head * count, (head + 1) * count)
        dq = mm(grad[mine], w_keys[head], NT, HIGHEST) * factor
        inner = inner + jnp.sum(dq * queries[head].astype(F32), axis=1, keepdims=True)
        at_ref[:FEAT, side] = mm(dq, own, TN, HIGHEST)
        at_ref[FEAT : 2 * FEAT, side] = mm(scaled[head].astype(F32), grad[mine], TN, HIGHEST)
        at_ref[2 * FEAT :, side] = mm(cots[head].astype(F32), value[mine], TN, HIGHEST)

    eye_i = lax.broadcasted_iota(jnp.int32, (2 * FEAT, 2 * FEAT), 0)
    eye_j = lax.broadcasted_iota(jnp.int32, (2 * FEAT, 2 * FEAT), 1)
    eye = (eye_i == eye_j).astype(F32).astype(BF16)
    high = both[:, : 2 * FEAT]
    turned = mm(eye, high, NT)
    c_all = jnp.sum(csum[...], axis=0, keepdims=True)
    weighted = jnp.concatenate(
        [turned[:FEAT] * c_all[:, :pairs], turned[FEAT:] * c_all[:, pairs:]], axis=0
    )
    full = mm(weighted.astype(BF16), high)
    own_part = mm(own * inner, own, TN, HIGHEST)
    b_ref[...] = ((full[:FEAT, :FEAT] + full[FEAT:, FEAT:]) + own_part) * (1.0 / D)


def attention(x, pairs, high, low, gram, row, half, cot):
    heads, count, _ = cot.shape
    return pl.pallas_call(
        attention_kernel,
        out_shape=[
            jax.ShapeDtypeStruct(cot.shape, BF16),
            jax.ShapeDtypeStruct(high.shape, F32),
            jax.ShapeDtypeStruct(gram.shape, F32),
        ],
        scratch_shapes=[
            pltpu.VMEM((pairs, 4 * FEAT), BF16),
            pltpu.VMEM((heads, 4 * FEAT, pairs), BF16),
            pltpu.VMEM((heads * count, 2 * pairs), F32),
            pltpu.VMEM((heads * count, 2 * pairs), F32),
            pltpu.VMEM((8, 2 * pairs), F32),
            pltpu.VMEM((count, 2 * FEAT), BF16),
        ],
        compiler_params=pltpu.CompilerParams(
            vmem_limit_bytes=48 * 1024 * 1024
        ),
        name="attention",
    )(x, high, low, gram, row, half, cot)


def per_device(
    features, conv_weight, conv_bias, token_order, embed_weight, norm_gain, qkv_weight, grad_out
):
    far = lax.axis_index("seq_0")
    near_count = lax.axis_size("seq_1")
    depth, _, width = qkv_weight.shape
    pair = 2 * HEAD_DIM
    rows = 3 * HEAD_DIM
    rows_each = rows // near_count

    def swapped(array, axis):
        first, second = jnp.split(array, 2, axis=axis)
        mine = jnp.where(far == 0, first, second)
        given = jnp.where(far == 0, second, first)
        return mine, lax.ppermute(given, "seq_0", [(0, 1), (1, 0)])

    def in_order(mine, other):
        return jnp.where(far == 0, jnp.stack([mine, other]), jnp.stack([other, mine]))

    clip = lax.axis_index("grp")
    half_rows = rows_each // 2

    def both_halves(mine, given, axis):
        other = lax.ppermute(given, "grp", [(0, 1), (1, 0)])
        return jnp.where(
            clip == 0, jnp.stack([mine, other], axis), jnp.stack([other, mine], axis)
        )

    w = qkv_weight.reshape(depth, 3, 2, 2, HEAD_DIM)
    w = jnp.transpose(w, (2, 1, 4, 3, 0)).reshape(2, near_count, 2, rows_each, depth)
    w = jnp.where(clip == 0, w[:, :, 0], w[:, :, 1])
    w = jnp.swapaxes(in_order(*swapped(w, 0))[:, 0], 0, 1).reshape(near_count, 2 * rows_each, depth)
    parts = taps(features[0, 0], conv_weight)
    parts, w = lax.optimization_barrier((parts, w))
    w_blocks = lax.all_to_all(w, "seq_1", 0, 0, tiled=True)
    w_blocks = w_blocks.reshape(near_count, 2, rows_each, depth)
    w_blocks = jnp.swapaxes(w_blocks, 0, 1).reshape(2 * near_count, rows_each, depth)
    w_slice = jnp.transpose(w_blocks, (1, 0, 2)).reshape(rows_each, D)
    embed32 = embed_weight.astype(F32)
    gained = jnp.concatenate(two(embed32 * norm_gain), axis=0)
    m_slice = mm(w_slice, gained, NT)
    m_slice = (m_slice[:, :FEAT] + m_slice[:, FEAT:]).reshape(half_rows, 2 * FEAT)
    columns = lax.axis_index(HEAD) * lax.axis_size(("grp", "seq_0"))
    columns = (columns + lax.axis_index(("grp", "seq_0"))) * depth
    gain_own = lax.dynamic_slice_in_dim(norm_gain, columns, depth, 0)
    embed_own = lax.dynamic_slice_in_dim(embed32, columns, depth, 1)
    b_each = FEAT // 2 // near_count
    b_at = lax.axis_index("seq_1") * b_each
    embed_own = jnp.concatenate(
        [lax.dynamic_slice_in_dim(embed_own, b_at + k, b_each, 0) for k in (0, FEAT // 2)], axis=0
    )

    patch = latent_patches(parts, conv_bias)
    token_order, m_slice, patch, embed_late = lax.optimization_barrier(
        (token_order, m_slice, patch, embed_weight)
    )
    gram = lax.dot_general(
        embed_late, embed_late, (((1,), (1,)), ((), ())), preferred_element_type=F32
    ) * (1.0 / D)
    own_rows = patch.shape[0]
    arrived = from_everyone(jnp.concatenate([patch, *two(m_slice)], axis=0), "seq_1")
    far_count, head_count = lax.axis_size("seq_0"), lax.axis_size(HEAD)
    plane = far_count * head_count
    mine = w_blocks.reshape(head_count, -1, far_count, rows_each, depth)
    mine = jnp.transpose(mine, (2, 0, 1, 3, 4)).reshape(plane, rows_each * 2, depth)
    mine = jnp.pad(mine, ((0, 0), (0, 0), (0, 2 * FEAT - depth)))
    latents = arrived[:, :own_rows].reshape(1, -1, 2 * FEAT)
    pairs_each = latents.shape[1]
    latents = jnp.broadcast_to(latents, (plane, pairs_each, 2 * FEAT))
    every = lax.all_to_all(
        jnp.concatenate([latents, mine], axis=1), ("seq_0", *HEAD), 0, 0, tiled=True
    )
    m_half = arrived[:, own_rows:]
    grad_out, m_half = lax.optimization_barrier((grad_out, m_half))
    m_both = both_halves(m_half, m_half, 1).reshape(near_count, 2, 2, half_rows, 2 * FEAT)
    m_high = m_both[:, :, 0].reshape(rows, 2 * FEAT)
    m_low = m_both[:, :, 1].reshape(rows, 2 * FEAT)

    per_patch_row = own_rows
    order = in_order(token_order, lax.ppermute(token_order, "seq_0", [(0, 1), (1, 0)]))
    order = order.reshape(-1, 1)
    j = order % (2 * per_patch_row)
    i = (order // (2 * per_patch_row)) % head_count
    f = order // (2 * per_patch_row * head_count)
    at_plane = (f // near_count) * head_count + i
    row = (at_plane * near_count + f % near_count) * per_patch_row + j % per_patch_row
    half = j // per_patch_row

    cot = in_order(*swapped(grad_out[0], 1)).reshape(-1, 2, HEAD_DIM)
    out, at, b = attention(
        every, plane * pairs_each, m_high, m_low, gram, row, half, jnp.transpose(cot, (1, 0, 2))
    )
    out = jnp.transpose(out, (1, 0, 2)).reshape(2, -1, pair)
    mine = jnp.where(far == 0, out[0], out[1])
    other = lax.ppermute(jnp.where(far == 0, out[1], out[0]), "seq_0", [(0, 1), (1, 0)])
    attended = jnp.where(
        far == 0,
        jnp.concatenate([mine, other], axis=1),
        jnp.concatenate([other, mine], axis=1),
    )[None]

    w_own, at = lax.optimization_barrier((every, at))
    w_own = w_own[:, pairs_each:].reshape(plane, 2, rows_each, 2 * FEAT)
    w_own = both_halves(
        lax.dynamic_index_in_dim(w_own, clip, 1, False),
        lax.dynamic_index_in_dim(w_own, 1 - clip, 1, False),
        1,
    )
    w_own = w_own.reshape(-1, 2 * FEAT)[:, :depth]
    first, second = jnp.split(b, 2, axis=0)
    b = jnp.concatenate([first, second], axis=1)
    at = jnp.concatenate(
        [
            at.reshape(near_count, rows_each, 2 * FEAT),
            b.reshape(near_count, b_each, 2 * FEAT),
        ],
        axis=1,
    )
    at = jnp.sum(lax.all_to_all(at, "seq_1", 0, 0, tiled=True), axis=0)
    at = from_everyone(at, ("grp", "seq_0", *HEAD))
    at = jnp.sum(at.reshape(-1, plane, *at.shape[1:]), axis=0)
    a_both = jnp.concatenate(two(at[:, :rows_each].reshape(-1, FEAT)), axis=1)
    t = mm(a_both, w_own, TN)
    t = (t[:FEAT] + t[FEAT:]) * gain_own
    b_rows = jnp.sum(at[:, rows_each:], axis=0).reshape(b_each, 2, FEAT)
    t = t - mm(jnp.swapaxes(b_rows, 0, 1).reshape(-1, FEAT), embed_own, TN, HIGHEST)
    parts = FEAT * depth // (D // head_count)
    t = jnp.swapaxes(t.reshape(FEAT // parts, parts, depth), 0, 1).reshape(parts, -1)
    t = jnp.sum(from_everyone(t.astype(BF16), "seq_1").astype(F32), axis=0)
    t = from_everyone(t, ("grp", "seq_0")).reshape(-1, parts, FEAT // parts, depth)
    embed_grad = jnp.transpose(t, (2, 1, 0, 3)).reshape(FEAT, -1)
    return (attended, embed_grad)


def solution(mesh):
    torus = Mesh(
        mesh.devices.reshape(mesh.shape["grp"], 2, 16, 4, 2),
        ("grp", "seq_0", "seq_1", "head_0", "head_1"),
    )
    return jax.shard_map(
        per_device,
        mesh=torus,
        in_specs=(
            P("grp", SEQ, HEAD, None, None),
            P(),
            P(),
            P(SEQ),
            P(),
            P(),
            P(SEQ, None, HEAD),
            P("grp", SEQ, HEAD),
        ),
        out_specs=(P("grp", SEQ, HEAD), P(None, HEAD)),
        check_vma=False,
    )
```
